32 devices in a mesh: groups: 2 (over x), expert: 16 (over z, y, core).
Axes of the slice: x: 2, y: 2, z: 4, core: 2. Of those that a mesh axis runs over, the one named last changes fastest.
Arguments:
- tokens: bfloat16 [4096, 2048], P(('groups', 'expert')), parts along dimension 0, may hold values from -6 to 6
- cotangent: bfloat16 [4096, 2048], P(('groups', 'expert')), parts along dimension 0, may hold values from -4 to 4
- expert_ids: int32 [4096, 4], P(('groups', 'expert')), parts along dimension 0, may hold values from 0 to 15, all different within a row; in each aligned block of 128 rows (0 to 127, 128 to 255, ...) at most 48 rows name the same one
- gate_levels: int32 [4096, 4], P(('groups', 'expert')), parts along dimension 0, may hold values from 1 to 256
- w_gate: bfloat16 [16, 2048, 384], P('expert'), may hold values from -0.125 to 0.125
- w_up: bfloat16 [16, 2048, 384], P('expert'), may hold values from -0.125 to 0.125
- w_down: bfloat16 [16, 384, 2048], P('expert'), may hold values from -0.3125 to 0.3125
Outputs:
- input_grad: bfloat16 [4096, 2048], P(('groups', 'expert')), parts along dimension 0
- router_grad: bfloat16 [4096, 4], P(('groups', 'expert')), parts along dimension 0
- gate_delta: bfloat16 [32, 2048, 384], P(('groups', 'expert')), parts along dimension 0
- up_delta: bfloat16 [32, 2048, 384], P(('groups', 'expert')), parts along dimension 0
- down_delta: bfloat16 [32, 384, 2048], P(('groups', 'expert')), parts along dimension 0
The draws below stay inside these ranges and needn't reach their ends.
There are 2 independent parts, one for each index of `groups`. The reference program is written for one: setup_inputs(seed, part) draws one part's arguments, and reference() takes and returns one part's arrays. A program takes and returns all parts, laid end to end along the dimension named above; an argument that names none is the same for every part. Nothing has to cross between parts.
Inputs may be any that keep to these rules, and one draw needn't show every extreme that they name: `expert_ids`: each token names 4 different experts. Among the tokens of one device no expert is named more than 48 times, and in every draw some expert is named exactly 48 times by some device.
All inputs are finite; a program needn't handle non-finite values.
Results may differ from the reference program's by a relative error of at most 0.014.
Values may be sent and summed in bfloat16 or wider, within the bound.
No kernel may reach another device: no remote copies, remote signals or barrier semaphores. Data moves between devices by JAX's collectives and lax.ppermute only.
A program may use at most 128 MiB of HBM per device.

```python
import math
import jax
import jax.numpy as jnp
import numpy as np
from jax import lax

D = 2048
FF = 384
TOP = 4
TOK_DEV = 128
EXPERTS = 16
CAP = 48
TOKENS = 2048
N_EXPERT = 16


def touch_ends(entries, rng, least, top_value):
    shape = entries.shape
    index_at = [jax.random.randint(jax.random.fold_in(rng, axis), (), 0, shape[axis]) for axis in range(len(shape))]
    entries = entries.at[tuple(index_at)].set(least)
    longest = shape.index(max(shape))
    index_at[longest] = (index_at[longest] + 1) % shape[longest]
    return entries.at[tuple(index_at)].set(top_value)


def steps_of(rng, extent, pieces, low, top_value):
    def one(dim, shards_of):
        draws = jax.random.uniform(jax.random.fold_in(jax.random.fold_in(rng, 6), dim), (shards_of,), jnp.float32, low / len(pieces), top_value / len(pieces))
        return jnp.repeat(jnp.exp(draws), extent[dim] // shards_of).reshape((-1,) + (1,) * (len(extent) - dim - 1))

    level = one(*pieces[0])
    for cut in pieces[1:]:
        level = level * one(*cut)
    return level


def shared_out(rng, own, number, rows, number_of, top, most, skew):
    sequence = jax.random.permutation(rng, number_of)
    crowded, ordinary = portions_of(number_of, rows * top, most, skew, True), portions_of(number_of, rows * top, most, skew, False)
    places = jnp.arange(number_of)

    def named(tallies, rotation):
        used = int((tallies > 0).sum())
        fixed = max(1, used // 4)
        passed = fixed + (places - fixed + rotation * (used - fixed)) % max(1, number_of - fixed)
        return jnp.zeros((number_of,), jnp.int32).at[sequence[jnp.where(places < fixed, places, passed)]].set(jnp.asarray(tallies, jnp.int32))

    tallies = jnp.where(number % 4 == 0, named(crowded, number // 4), named(ordinary, number - number // 4 - 1))
    mixed = jax.random.permutation(jax.random.fold_in(own, 3), number_of)
    source_of, taker = mixed[0:number_of // 2 * 2:2], mixed[1:number_of // 2 * 2:2]
    room = jnp.minimum(tallies[source_of] - 1, most - tallies[taker]) // 2
    room = jnp.where((source_of == sequence[0]) | (taker == sequence[0]) | (tallies[taker] == 0), 0, jnp.maximum(room, 0))
    passed = jax.random.randint(jax.random.fold_in(own, 4), (number_of // 2,), 0, 1 << 20) % (room + 1)
    tallies = tallies.at[source_of].add(-passed).at[taker].add(passed)
    labels = jnp.searchsorted(jnp.cumsum(tallies), jnp.arange(rows * top), side="right").astype(jnp.int32)
    listing = labels.reshape(top, rows).T
    listing = listing[jax.random.permutation(jax.random.fold_in(own, 1), rows)]
    rotation = jax.random.randint(jax.random.fold_in(own, 2), (rows, 1), 0, top)
    return jnp.take_along_axis(listing, (jnp.arange(top)[None, :] + rotation) % top, axis=1)


def portions_of(amount, total, limit, skew, full):
    loads = [(1 << 20) // math.isqrt(grade ** skew) + 1 for grade in range(1, amount + 1)]
    largest = limit if full else min(limit, max(-(-total // amount), total * loads[0] // sum(loads)))
    least = 1 if total - largest >= amount - 1 else 0
    given, surplus = [largest] + [least] * (amount - 1), total - largest - least * (amount - 1)
    while surplus > 0:
        movable = [i for i in range(1, amount) if given[i] < largest] or [i for i in range(1, amount) if given[i] < limit]
        whole, left = sum([loads[i] for i in movable]), surplus
        for i in movable:
            more = min(limit - given[i], max(1, left * loads[i] // whole), surplus)
            given[i] = given[i] + more
            surplus = surplus - more
    return np.array(given)


def noise(own_key, shape, deviation, most, cuts=(), kind=jnp.bfloat16):
    values = jax.random.normal(own_key, shape, jnp.float32) * deviation
    if len(cuts) > 0:
        values = steps_of(own_key, shape, cuts, -0.22, 0.18) * values
    return jnp.clip(values, min=-most, max=most).astype(kind)


def setup_inputs(seed: int = 0, part: int = 0) -> dict:
    streams_of = jax.random.split(jax.random.key(seed), 8)
    part_splits = jax.random.split(jax.random.fold_in(streams_of[7], part), 8)
    tokens = noise(part_splits[0], (TOKENS, D), 1.0, 6.0, ((0, 16),))
    cotangent = noise(part_splits[1], (TOKENS, D), 0.5, 4.0, ((0, 16),))
    expert_ids_keys = jax.random.split(jax.random.fold_in(part_splits[2], 1), TOKENS // TOK_DEV)
    expert_ids_turns = jax.random.permutation(jax.random.fold_in(part_splits[2], 3), TOKENS // TOK_DEV)
    expert_ids = jax.vmap(lambda own, number: shared_out(jax.random.fold_in(part_splits[2], 2), own, number, TOK_DEV, EXPERTS, TOP, CAP, 2))(expert_ids_keys, expert_ids_turns).reshape((TOKENS, TOP))
    gate_levels = touch_ends(jax.random.randint(part_splits[3], (TOKENS, TOP), 1, 257), jax.random.fold_in(part_splits[3], 1), 1, 256).astype(jnp.int32)
    w_gate = noise(streams_of[4], (EXPERTS, D, FF), D ** -0.5, 0.125, ((0, 16),))
    w_up = noise(streams_of[5], (EXPERTS, D, FF), D ** -0.5, 0.125, ((0, 16),))
    w_down = noise(streams_of[6], (EXPERTS, FF, D), FF ** -0.5, 0.3125, ((0, 16),))
    return {"tokens": tokens, "cotangent": cotangent, "expert_ids": expert_ids, "gate_levels": gate_levels, "w_gate": w_gate, "w_up": w_up, "w_down": w_down}


def project(inputs, gate_mat, up_mat):
    gate_pre = jnp.dot(inputs, gate_mat, preferred_element_type=jnp.float32)
    up_pre = jnp.dot(inputs, up_mat, preferred_element_type=jnp.float32)
    return gate_pre, up_pre


def backward(inputs, prepared, cotangent, gating, gate_mat, up_mat, down_mat):
    gate_pre, up_pre = prepared
    sigmoid_gate = jax.nn.sigmoid(gate_pre)
    hidden = (gate_pre * sigmoid_gate * up_pre).astype(jnp.bfloat16)
    back_grad = lax.dot_general(cotangent, down_mat, (((1,), (1,)), ((), ())), preferred_element_type=jnp.float32)
    router_term = jnp.sum(hidden.astype(jnp.float32) * back_grad, axis=1).astype(jnp.bfloat16)
    hidden_grad = gating[:, None] * back_grad
    gate_grad = (hidden_grad * up_pre * sigmoid_gate * (1.0 + gate_pre * (1.0 - sigmoid_gate))).astype(jnp.bfloat16)
    up_grad = (hidden_grad * gate_pre * sigmoid_gate).astype(jnp.bfloat16)
    input_term = lax.dot_general(gate_grad, gate_mat, (((1,), (1,)), ((), ())), preferred_element_type=jnp.float32)
    input_term = input_term + lax.dot_general(up_grad, up_mat, (((1,), (1,)), ((), ())), preferred_element_type=jnp.float32)
    input_term = input_term.astype(jnp.bfloat16)
    scaled = (gating[:, None] * cotangent.astype(jnp.float32)).astype(jnp.bfloat16)
    down_delta = lax.dot_general(hidden, scaled, (((0,), (0,)), ((), ())), preferred_element_type=jnp.float32)
    gate_delta = lax.dot_general(inputs, gate_grad, (((0,), (0,)), ((), ())), preferred_element_type=jnp.float32)
    up_delta = lax.dot_general(inputs, up_grad, (((0,), (0,)), ((), ())), preferred_element_type=jnp.float32)
    return input_term, router_term, gate_delta, up_delta, down_delta


def reference(tokens, cotangent, expert_ids, gate_levels, w_gate, w_up, w_down):
    token_count = tokens.shape[0]
    per_device = TOK_DEV * TOP
    slot_rows = N_EXPERT * CAP
    chosen = expert_ids.reshape(N_EXPERT, per_device)
    indicator = (chosen[:, :, None] == jnp.arange(EXPERTS, dtype=jnp.int32)[None, None, :]).astype(jnp.int32)
    earlier = jnp.cumsum(indicator, axis=1) - indicator
    position = jnp.sum(earlier * indicator, axis=2).astype(jnp.int32)
    sources = jnp.arange(N_EXPERT, dtype=jnp.int32)[:, None]
    columns = (sources * CAP + position).astype(jnp.int32)
    table = jnp.full((EXPERTS, slot_rows), -1, jnp.int32)
    table = table.at[chosen.reshape(-1), columns.reshape(-1)].set(jnp.arange(token_count * TOP, dtype=jnp.int32))
    gating_all = gate_levels.reshape(-1).astype(jnp.float32) / 256.0

    def visit(carried, member):
        accumulated, router_grads = carried
        assigned, gate_mat, up_mat, down_mat = member
        present = assigned >= 0
        clipped = jnp.where(present, assigned, 0).astype(jnp.int32)
        token_row = (clipped // TOP).astype(jnp.int32)
        rows_x = jnp.where(present[:, None], tokens[token_row], jnp.zeros((), jnp.bfloat16))
        rows_dy = jnp.where(present[:, None], cotangent[token_row], jnp.zeros((), jnp.bfloat16))
        gating = jnp.where(present, gating_all[clipped], jnp.float32(0.0))
        prepared = project(rows_x, gate_mat, up_mat)
        input_term, router_term, gate_delta, up_delta, down_delta = backward(rows_x, prepared, rows_dy, gating, gate_mat, up_mat, down_mat)
        accumulated = accumulated.at[token_row].add(jnp.where(present[:, None], input_term.astype(jnp.float32), jnp.float32(0.0)))
        router_grads = router_grads.at[clipped].add(jnp.where(present, router_term.astype(jnp.float32), jnp.float32(0.0)))
        return (accumulated, router_grads), (gate_delta.astype(jnp.bfloat16), up_delta.astype(jnp.bfloat16), down_delta.astype(jnp.bfloat16))

    initial = (jnp.zeros((token_count, D), jnp.float32), jnp.zeros((token_count * TOP,), jnp.float32))
    (accumulated, router_grads), deltas = lax.scan(visit, initial, (table, w_gate, w_up, w_down))
    input_grad = accumulated.astype(jnp.bfloat16)
    router_grad = router_grads.reshape(token_count, TOP).astype(jnp.bfloat16)
    return input_grad, router_grad, deltas[0], deltas[1], deltas[2]
```

```python
import functools

import jax
import jax.numpy as jnp
from jax import lax
from jax.experimental import pallas as pl
from jax.experimental.pallas import tpu as pltpu
from jax.sharding import PartitionSpec as P

BF16 = jnp.bfloat16
F32 = jnp.float32
LANES = 128
PLANE = 4


def project(inputs, gate_mat, up_mat):
    gate_pre = jnp.dot(inputs, gate_mat, preferred_element_type=jnp.float32)
    up_pre = jnp.dot(inputs, up_mat, preferred_element_type=jnp.float32)
    return (gate_pre, up_pre)


def backward(inputs, prepared, cotangent, gating, gate_mat, up_mat, down_mat):
    gate_pre, up_pre = prepared
    sigmoid_gate = jax.nn.sigmoid(gate_pre)
    hidden = (gate_pre * sigmoid_gate * up_pre).astype(jnp.bfloat16)
    back_grad = lax.dot_general(
        cotangent, down_mat, (((1,), (1,)), ((), ())), preferred_element_type=jnp.float32
    )
    router_term = jnp.sum(hidden.astype(jnp.float32) * back_grad, axis=1).astype(jnp.bfloat16)
    hidden_grad = gating[:, None] * back_grad
    gate_grad = (
        hidden_grad * up_pre * sigmoid_gate * (1.0 + gate_pre * (1.0 - sigmoid_gate))
    ).astype(jnp.bfloat16)
    up_grad = (hidden_grad * gate_pre * sigmoid_gate).astype(jnp.bfloat16)
    input_term = lax.dot_general(
        gate_grad, gate_mat, (((1,), (1,)), ((), ())), preferred_element_type=jnp.float32
    )
    input_term = input_term + lax.dot_general(
        up_grad, up_mat, (((1,), (1,)), ((), ())), preferred_element_type=jnp.float32
    )
    input_term = input_term.astype(jnp.bfloat16)
    scaled = (gating[:, None] * cotangent.astype(jnp.float32)).astype(jnp.bfloat16)
    down_delta = lax.dot_general(
        hidden, scaled, (((0,), (0,)), ((), ())), preferred_element_type=jnp.float32
    )
    gate_delta = lax.dot_general(
        inputs, gate_grad, (((0,), (0,)), ((), ())), preferred_element_type=jnp.float32
    )
    up_delta = lax.dot_general(
        inputs, up_grad, (((0,), (0,)), ((), ())), preferred_element_type=jnp.float32
    )
    return (input_term, router_term, gate_delta, up_delta, down_delta)


def direct(tokens, cotangent, expert_ids, gate_levels, w_gate, w_up, w_down):
    devices = lax.axis_size("expert")
    tok_rows, fanout = expert_ids.shape
    features = tokens.shape[1]
    capacity = 3 * tok_rows * fanout // (2 * devices)
    slot_rows = devices * capacity
    gate_mat = w_gate[0]
    up_mat = w_up[0]
    down_mat = w_down[0]
    chosen = expert_ids.reshape(-1)
    indicator = (chosen[:, None] == jnp.arange(devices, dtype=jnp.int32)[None, :]).astype(jnp.int32)
    earlier = jnp.cumsum(indicator, axis=0) - indicator
    position = jnp.sum(earlier * indicator, axis=1)
    target = chosen * capacity + position
    gating_local = (gate_levels.reshape(-1).astype(jnp.float32) / 256.0).astype(jnp.bfloat16)
    outbox_x = (
        jnp.zeros((slot_rows, features), jnp.bfloat16)
        .at[target]
        .set(jnp.repeat(tokens, fanout, axis=0))
    )
    outbox_dy = (
        jnp.zeros((slot_rows, features), jnp.bfloat16)
        .at[target]
        .set(jnp.repeat(cotangent, fanout, axis=0))
    )
    outbox_g = jnp.zeros((slot_rows,), jnp.bfloat16).at[target].set(gating_local)
    outbox_x = outbox_x.reshape(devices, capacity, features)
    outbox_dy = outbox_dy.reshape(devices, capacity, features)
    outbox_g = outbox_g.reshape(devices, capacity)
    exchange = functools.partial(
        lax.all_to_all, axis_name="expert", split_axis=0, concat_axis=0, tiled=True
    )
    rows_x = exchange(outbox_x).reshape(slot_rows, features)
    rows_dy = exchange(outbox_dy).reshape(slot_rows, features)
    rows_g = exchange(outbox_g).reshape(-1).astype(jnp.float32)
    prepared = project(rows_x, gate_mat, up_mat)
    input_term, router_term, gate_delta, up_delta, down_delta = backward(
        rows_x, prepared, rows_dy, rows_g, gate_mat, up_mat, down_mat
    )
    back_term = exchange(input_term.reshape(devices, capacity, features))
    back_router = exchange(router_term.reshape(devices, capacity))
    gathered_term = back_term.reshape(slot_rows, features)[target].astype(jnp.float32)
    input_grad = jnp.sum(gathered_term.reshape(tok_rows, fanout, features), axis=1).astype(
        jnp.bfloat16
    )
    router_grad = back_router.reshape(-1)[target].reshape(tok_rows, fanout)
    return (
        input_grad,
        router_grad,
        gate_delta.astype(jnp.bfloat16)[None],
        up_delta.astype(jnp.bfloat16)[None],
        down_delta.astype(jnp.bfloat16)[None],
    )


def dot(a, b, contract=((1,), (0,))):
    return lax.dot_general(a, b, (contract, ((), ())), preferred_element_type=F32)


def call(kernel, outs, name, *operands, scratch=(), smem=0, limit=60):
    vmem = pl.BlockSpec(memory_space=pltpu.VMEM)
    scalar = pl.BlockSpec(memory_space=pltpu.SMEM)
    return pl.pallas_call(
        kernel,
        out_shape=[jax.ShapeDtypeStruct(shape, kind) for shape, kind in outs],
        in_specs=[scalar] * smem + [vmem] * (len(operands) - smem),
        out_specs=[vmem] * len(outs),
        scratch_shapes=list(scratch),
        name=name,
        compiler_params=pltpu.CompilerParams(vmem_limit_bytes=limit << 20),
        cost_estimate=pl.CostEstimate(flops=1000, bytes_accessed=1000, transcendentals=0),
    )(*operands)


def pack_kernel(ids_ref, levels_ref, x_ref, out_ref):
    fanout, rows = ids_ref.shape
    features = x_ref.shape[1]
    expert = lax.broadcasted_iota(jnp.int32, (LANES, rows), 0)
    gates = jnp.zeros((LANES, rows), F32)
    for k in range(fanout):
        value = levels_ref[k : k + 1, :].astype(F32) * (1.0 / 256.0)
        gates = gates + jnp.where(ids_ref[k : k + 1, :] == expert, value, 0.0)
    out_ref[:, :features] = x_ref[...]
    out_ref[:, features:] = gates.T.astype(BF16)


def slot_kernel(capacity, me_ref, x_ref, pick_ref, *slot_refs):
    rows = x_ref.shape[0]
    features = x_ref.shape[1] - LANES
    me = me_ref[0]
    expert = lax.broadcasted_iota(jnp.int32, (8, LANES), 1)
    wanted = jnp.bitwise_xor(lax.broadcasted_iota(jnp.int32, (8, LANES), 0), me)
    chooser = jnp.where(expert == wanted, 1.0, 0.0).astype(BF16)
    gates = dot(chooser, x_ref[:, features:], ((1,), (1,)))
    routed = jnp.where(gates > 0.0, 1.0, 0.0)
    before = lax.broadcasted_iota(jnp.int32, (rows, rows), 0)
    after = lax.broadcasted_iota(jnp.int32, (rows, rows), 1)
    earlier = jnp.where(before < after, 1.0, 0.0).astype(BF16)
    place = dot(routed.astype(BF16), earlier)
    place = jnp.where(routed > 0.0, place, -1.0)
    slot = lax.broadcasted_iota(jnp.int32, (capacity, rows), 0).astype(F32)
    pick = jnp.concatenate(
        [jnp.where(place[j : j + 1, :] == slot, 1.0, 0.0) for j in range(PLANE)], axis=0
    ).astype(BF16)
    pick_ref[...] = pick
    picked = dot(pick, x_ref[...]).astype(BF16)
    for j in range(PLANE):
        slot_refs[j][...] = picked[j * capacity : (j + 1) * capacity, :]


def gather_kernel(capacity, pick_ref, d_ref, *slot_refs):
    picked = dot(pick_ref[...], d_ref[...]).astype(BF16)
    for j in range(PLANE):
        slot_refs[j][...] = picked[j * capacity : (j + 1) * capacity, :]


def expert_kernel(capacity, me_ref, *refs):
    x_refs, d_refs = refs[:PLANE], refs[PLANE : 2 * PLANE]
    gate_ref, up_ref, down_ref = refs[2 * PLANE : 2 * PLANE + 3]
    term_refs = refs[2 * PLANE + 3 : 3 * PLANE + 3]
    grads_ref, hidden_ref = refs[3 * PLANE + 3 :]
    features = d_refs[0].shape[1]
    units = gate_ref.shape[1]
    rows = PLANE * capacity
    x = jnp.concatenate([ref[:, :features] for ref in x_refs], axis=0)
    gates = jnp.concatenate([ref[:, features:] for ref in x_refs], axis=0).astype(F32)
    mine = lax.broadcasted_iota(jnp.int32, (rows, LANES), 1) == me_ref[0]
    gating = jnp.sum(jnp.where(mine, gates, 0.0), axis=1, keepdims=True)
    d = jnp.concatenate([ref[...] for ref in d_refs], axis=0)
    gate_pre = dot(x, gate_ref[...])
    up_pre = dot(x, up_ref[...])
    back_grad = dot(d, down_ref[...], ((1,), (1,)))
    sigmoid_gate = jax.nn.sigmoid(gate_pre)
    silu = gate_pre * sigmoid_gate
    hidden = (silu * up_pre).astype(BF16).astype(F32)
    router = jnp.sum(hidden * back_grad, axis=1, keepdims=True)
    hidden_grad = gating * back_grad
    gate_grad = (hidden_grad * up_pre * sigmoid_gate * (1.0 + gate_pre * (1.0 - sigmoid_gate))).astype(BF16)
    up_grad = (hidden_grad * silu).astype(BF16)
    grads_ref[:, :units] = gate_grad
    grads_ref[:, units:] = up_grad
    hidden_ref[...] = (gating * hidden).astype(BF16)
    term = dot(gate_grad, gate_ref[...], ((1,), (1,))) + dot(up_grad, up_ref[...], ((1,), (1,)))
    term = term.astype(BF16)
    router = jnp.where(mine, router, 0.0).astype(BF16)
    for j in range(PLANE):
        part = slice(j * capacity, (j + 1) * capacity)
        term_refs[j][:, :features] = term[part, :]
        term_refs[j][:, features:] = router[part, :]


def combine_kernel(pick_ref, *refs):
    terms = jnp.concatenate([ref[...] for ref in refs[:PLANE]], axis=0)
    refs[PLANE][...] = dot(pick_ref[...], terms, ((0,), (0,))).astype(BF16)


def total_kernel(ids_ref, *refs):
    parts, (grad_ref, router_ref) = refs[:-2], refs[-2:]
    fanout, rows = ids_ref.shape
    features = grad_ref.shape[1]
    total = parts[0][...].astype(F32)
    for part in parts[1:]:
        total = total + part[...].astype(F32)
    grad_ref[...] = total[:, :features].astype(BF16)
    router = total[:, features:].T
    expert = lax.broadcasted_iota(jnp.int32, (LANES, rows), 0)
    for k in range(fanout):
        own = jnp.where(ids_ref[k : k + 1, :] == expert, router, 0.0)
        router_ref[k : k + 1, :] = jnp.sum(own, axis=0, keepdims=True).astype(BF16)


def delta_kernel(chunks, *refs):
    x_refs, d_refs = refs[: chunks * PLANE], refs[chunks * PLANE : 2 * chunks * PLANE]
    grads_refs = refs[2 * chunks * PLANE : 2 * chunks * PLANE + chunks]
    hidden_refs = refs[2 * chunks * PLANE + chunks : 2 * chunks * PLANE + 2 * chunks]
    gate_ref, up_ref, down_ref, x_all, d_all = refs[-5:]
    units = gate_ref.shape[1]
    features = gate_ref.shape[0]
    capacity = x_refs[0].shape[0]
    for i in range(chunks * PLANE):
        part = slice(i * capacity, (i + 1) * capacity)
        x_all[part, :] = x_refs[i][:, :features]
        d_all[part, :] = d_refs[i][...]
    grads = jnp.concatenate([ref[...] for ref in grads_refs], axis=0)
    hidden = jnp.concatenate([ref[...] for ref in hidden_refs], axis=0)
    step = 512

    @pl.loop(0, features // step)
    def _(i):
        cols = pl.ds(pl.multiple_of(i * step, step), step)
        both = dot(x_all[:, cols], grads, ((0,), (0,))).astype(BF16)
        gate_ref[cols, :] = both[:, :units]
        up_ref[cols, :] = both[:, units:]
        down_ref[:, cols] = dot(hidden, d_all[:, cols], ((0,), (0,))).astype(BF16)


def staged(tokens, cotangent, expert_ids, gate_levels, w_gate, w_up, w_down):
    devices = lax.axis_size("expert")
    planes = devices // PLANE
    tok_rows, fanout = expert_ids.shape
    features = tokens.shape[1]
    units = w_gate.shape[2]
    capacity = 3 * tok_rows * fanout // (2 * devices)
    wide = features + LANES
    me = lax.axis_index("expert").reshape(1)
    ids = expert_ids.T
    gate_mat, up_mat, down_mat = w_gate[0], w_up[0], w_down[0]

    def along(array, distance):
        pairs = [(i, (i + distance * PLANE) % devices) for i in range(devices)]
        return lax.ppermute(array, "expert", pairs)

    def within(arrays):
        moved = [
            lax.ppermute(arrays[j], "expert", [(i, i ^ j) for i in range(devices)])
            for j in range(1, PLANE)
        ]
        return [arrays[0]] + moved

    (packed,) = call(pack_kernel, [((tok_rows, wide), BF16)], "pack", ids, gate_levels.T, tokens)
    xs, ds = [packed], [cotangent]
    for _ in range(planes - 1):
        xs.append(along(xs[-1], 1))
        ds.append(along(ds[-1], 1))

    all_x, all_d, all_grads, all_hidden, parts = [], [], [], [], []
    rows = PLANE * capacity
    for s in range(planes):
        pick, *slots = call(
            functools.partial(slot_kernel, capacity),
            [((rows, tok_rows), BF16)] + [((capacity, wide), BF16)] * PLANE,
            "slots_x",
            me,
            xs[s],
            smem=1,
        )
        rows_x = within(slots)
        slots = call(
            functools.partial(gather_kernel, capacity),
            [((capacity, features), BF16)] * PLANE,
            "slots_d",
            pick,
            ds[s],
        )
        rows_d = within(slots)
        *terms, grads, hidden = call(
            functools.partial(expert_kernel, capacity),
            [((capacity, wide), BF16)] * PLANE + [((rows, 2 * units), BF16), ((rows, units), BF16)],
            "expert",
            me,
            *rows_x,
            *rows_d,
            gate_mat,
            up_mat,
            down_mat,
            smem=1,
        )
        (part,) = call(combine_kernel, [((tok_rows, wide), BF16)], "combine", pick, *within(terms))
        parts.append(along(part, -s) if s else part)
        all_x += rows_x
        all_d += rows_d
        all_grads.append(grads)
        all_hidden.append(hidden)

    gate_delta, up_delta, down_delta = call(
        functools.partial(delta_kernel, planes),
        [((features, units), BF16), ((features, units), BF16), ((units, features), BF16)],
        "deltas",
        *all_x,
        *all_d,
        *all_grads,
        *all_hidden,
        scratch=[pltpu.VMEM((planes * rows, features), BF16)] * 2,
    )
    input_grad, router_grad = call(
        total_kernel,
        [((tok_rows, features), BF16), ((fanout, tok_rows), BF16)],
        "total",
        ids,
        *parts,
    )
    return input_grad, router_grad.T, gate_delta[None], up_delta[None], down_delta[None]


def solution(mesh):
    devices = mesh.shape["expert"]
    tokens, experts = P(("groups", "expert"), None), P("expert", None, None)
    deltas = P(("groups", "expert"), None, None)

    def on_device(*arrays):
        tok_rows, fanout = arrays[2].shape
        capacity = 3 * tok_rows * fanout // (2 * devices)
        plan = staged if PLANE * capacity > tok_rows and devices % PLANE == 0 else direct
        return plan(*arrays)

    return jax.shard_map(
        on_device,
        mesh=mesh,
        in_specs=(tokens, tokens, tokens, tokens, experts, experts, experts),
        out_specs=(tokens, tokens, deltas, deltas, deltas),
        check_vma=False,
    )
```

```python
import functools

import jax
import jax.numpy as jnp
from jax import lax
from jax.experimental import pallas as pl
from jax.experimental.pallas import tpu as pltpu
from jax.sharding import PartitionSpec as P

BF16 = jnp.bfloat16
F32 = jnp.float32
LANES = 128
PLANE = 4


def project(inputs, gate_mat, up_mat):
    gate_pre = jnp.dot(inputs, gate_mat, preferred_element_type=jnp.float32)
    up_pre = jnp.dot(inputs, up_mat, preferred_element_type=jnp.float32)
    return (gate_pre, up_pre)


def backward(inputs, prepared, cotangent, gating, gate_mat, up_mat, down_mat):
    gate_pre, up_pre = prepared
    sigmoid_gate = jax.nn.sigmoid(gate_pre)
    hidden = (gate_pre * sigmoid_gate * up_pre).astype(jnp.bfloat16)
    back_grad = lax.dot_general(
        cotangent, down_mat, (((1,), (1,)), ((), ())), preferred_element_type=jnp.float32
    )
    router_term = jnp.sum(hidden.astype(jnp.float32) * back_grad, axis=1).astype(jnp.bfloat16)
    hidden_grad = gating[:, None] * back_grad
    gate_grad = (
        hidden_grad * up_pre * sigmoid_gate * (1.0 + gate_pre * (1.0 - sigmoid_gate))
    ).astype(jnp.bfloat16)
    up_grad = (hidden_grad * gate_pre * sigmoid_gate).astype(jnp.bfloat16)
    input_term = lax.dot_general(
        gate_grad, gate_mat, (((1,), (1,)), ((), ())), preferred_element_type=jnp.float32
    )
    input_term = input_term + lax.dot_general(
        up_grad, up_mat, (((1,), (1,)), ((), ())), preferred_element_type=jnp.float32
    )
    input_term = input_term.astype(jnp.bfloat16)
    scaled = (gating[:, None] * cotangent.astype(jnp.float32)).astype(jnp.bfloat16)
    down_delta = lax.dot_general(
        hidden, scaled, (((0,), (0,)), ((), ())), preferred_element_type=jnp.float32
    )
    gate_delta = lax.dot_general(
        inputs, gate_grad, (((0,), (0,)), ((), ())), preferred_element_type=jnp.float32
    )
    up_delta = lax.dot_general(
        inputs, up_grad, (((0,), (0,)), ((), ())), preferred_element_type=jnp.float32
    )
    return (input_term, router_term, gate_delta, up_delta, down_delta)


def direct(tokens, cotangent, expert_ids, gate_levels, w_gate, w_up, w_down):
    devices = lax.axis_size("expert")
    tok_rows, fanout = expert_ids.shape
    features = tokens.shape[1]
    capacity = 3 * tok_rows * fanout // (2 * devices)
    slot_rows = devices * capacity
    gate_mat = w_gate[0]
    up_mat = w_up[0]
    down_mat = w_down[0]
    chosen = expert_ids.reshape(-1)
    indicator = (chosen[:, None] == jnp.arange(devices, dtype=jnp.int32)[None, :]).astype(jnp.int32)
    earlier = jnp.cumsum(indicator, axis=0) - indicator
    position = jnp.sum(earlier * indicator, axis=1)
    target = chosen * capacity + position
    gating_local = (gate_levels.reshape(-1).astype(jnp.float32) / 256.0).astype(jnp.bfloat16)
    outbox_x = (
        jnp.zeros((slot_rows, features), jnp.bfloat16)
        .at[target]
        .set(jnp.repeat(tokens, fanout, axis=0))
    )
    outbox_dy = (
        jnp.zeros((slot_rows, features), jnp.bfloat16)
        .at[target]
        .set(jnp.repeat(cotangent, fanout, axis=0))
    )
    outbox_g = jnp.zeros((slot_rows,), jnp.bfloat16).at[target].set(gating_local)
    outbox_x = outbox_x.reshape(devices, capacity, features)
    outbox_dy = outbox_dy.reshape(devices, capacity, features)
    outbox_g = outbox_g.reshape(devices, capacity)
    exchange = functools.partial(
        lax.all_to_all, axis_name="expert", split_axis=0, concat_axis=0, tiled=True
    )
    rows_x = exchange(outbox_x).reshape(slot_rows, features)
    rows_dy = exchange(outbox_dy).reshape(slot_rows, features)
    rows_g = exchange(outbox_g).reshape(-1).astype(jnp.float32)
    prepared = project(rows_x, gate_mat, up_mat)
    input_term, router_term, gate_delta, up_delta, down_delta = backward(
        rows_x, prepared, rows_dy, rows_g, gate_mat, up_mat, down_mat
    )
    back_term = exchange(input_term.reshape(devices, capacity, features))
    back_router = exchange(router_term.reshape(devices, capacity))
    gathered_term = back_term.reshape(slot_rows, features)[target].astype(jnp.float32)
    input_grad = jnp.sum(gathered_term.reshape(tok_rows, fanout, features), axis=1).astype(
        jnp.bfloat16
    )
    router_grad = back_router.reshape(-1)[target].reshape(tok_rows, fanout)
    return (
        input_grad,
        router_grad,
        gate_delta.astype(jnp.bfloat16)[None],
        up_delta.astype(jnp.bfloat16)[None],
        down_delta.astype(jnp.bfloat16)[None],
    )


def dot(a, b, contract=((1,), (0,))):
    return lax.dot_general(a, b, (contract, ((), ())), preferred_element_type=F32)


class Chain:
    def __init__(self):
        self.last = []

    def __call__(self, kernel, outs, name, *operands, after=(), scratch=(), smem=0, limit=16):
        vmem = pl.BlockSpec(memory_space=pltpu.VMEM)
        scalar = pl.BlockSpec(memory_space=pltpu.SMEM)
        unused = [*self.last, *after]
        fixed = len(operands)

        def body(*refs):
            kernel(*refs[:fixed], *refs[fixed + len(unused) :])

        made = pl.pallas_call(
            body,
            out_shape=[jax.ShapeDtypeStruct(shape, kind) for shape, kind in outs],
            in_specs=[scalar] * smem
            + [vmem] * (fixed - smem)
            + [pl.BlockSpec(memory_space=pl.ANY)] * len(unused),
            out_specs=[vmem] * len(outs),
            scratch_shapes=list(scratch),
            name=name,
            compiler_params=pltpu.CompilerParams(vmem_limit_bytes=limit << 20),
            cost_estimate=pl.CostEstimate(flops=1000, bytes_accessed=1000, transcendentals=0),
        )(*operands, *unused)
        self.last = made[:1]
        return made

    def hold(self, array, after=()):
        unused = [*self.last, *after]
        rows, width = array.shape
        half = jax.ShapeDtypeStruct((rows // 2, width), array.dtype)

        def body(*refs):
            whole, halves, sems = refs[0], refs[-3:-1], refs[-1]
            copies = [
                pltpu.make_async_copy(whole.at[pl.ds(rows // 2 * i, rows // 2)], halves[i], sems.at[i])
                for i in range(2)
            ]
            for copy in copies:
                copy.start()
            for copy in copies:
                copy.wait()

        vmem, anywhere = pl.BlockSpec(memory_space=pltpu.VMEM), pl.BlockSpec(memory_space=pl.ANY)
        made = pl.pallas_call(
            body,
            out_shape=[jax.ShapeDtypeStruct(array.shape, array.dtype), half, half],
            in_specs=[anywhere] * (1 + len(unused)),
            out_specs=[anywhere, vmem, vmem],
            input_output_aliases={0: 0},
            scratch_shapes=[pltpu.SemaphoreType.DMA((2,))],
            name="hold",
            compiler_params=pltpu.CompilerParams(vmem_limit_bytes=4 << 20),
            cost_estimate=pl.CostEstimate(flops=1000, bytes_accessed=1000, transcendentals=0),
        )(array, *unused)
        self.last = made[1:2]
        return made[0], made[1:]


def pack_kernel(ids_ref, levels_ref, x_ref, d_ref, out_ref, *half_refs):
    fanout, rows = ids_ref.shape
    features = x_ref.shape[1]
    expert = lax.broadcasted_iota(jnp.int32, (LANES, rows), 0)
    gates = jnp.zeros((LANES, rows), F32)
    for k in range(fanout):
        value = levels_ref[k : k + 1, :].astype(F32) * (1.0 / 256.0)
        gates = gates + jnp.where(ids_ref[k : k + 1, :] == expert, value, 0.0)
    gates = gates.T.astype(BF16)
    out_ref[:, :features] = x_ref[...]
    out_ref[:, features:] = gates
    for i in range(2):
        part = slice(rows // 2 * i, rows // 2 * (i + 1))
        half_refs[i][:, :features] = x_ref[part, :]
        half_refs[i][:, features:] = gates[part, :]
        half_refs[2 + i][...] = d_ref[part, :]


def joined(upper_ref, lower_ref):
    return jnp.concatenate([upper_ref[...], lower_ref[...]], axis=0)


def slot_kernel(capacity, me_ref, mine_ref, upper_ref, lower_ref, pick_ref, own_ref, sent_ref):
    rows = mine_ref.shape[0]
    features = mine_ref.shape[1] - LANES
    me = me_ref[0]
    expert = lax.broadcasted_iota(jnp.int32, (8, LANES), 1)
    wanted = jnp.bitwise_xor(2 * lax.broadcasted_iota(jnp.int32, (8, LANES), 0), me)
    chooser = jnp.where(expert == wanted, 1.0, 0.0).astype(BF16)
    before = lax.broadcasted_iota(jnp.int32, (rows, rows), 0)
    after = lax.broadcasted_iota(jnp.int32, (rows, rows), 1)
    earlier = jnp.where(before < after, 1.0, 0.0).astype(BF16)
    slot = lax.broadcasted_iota(jnp.int32, (capacity, rows), 0).astype(F32)
    for j, x in enumerate((mine_ref[...], joined(upper_ref, lower_ref))):
        gates = dot(chooser, x[:, features:], ((1,), (1,)))
        routed = jnp.where(gates > 0.0, 1.0, 0.0)
        place = dot(routed.astype(BF16), earlier)
        place = jnp.where(routed > 0.0, place, -1.0)
        pick = jnp.concatenate(
            [jnp.where(place[i : i + 1, :] == slot, 1.0, 0.0) for i in range(2)], axis=0
        ).astype(BF16)
        pick_ref[2 * capacity * j : 2 * capacity * (j + 1), :] = pick
        picked = dot(pick, x).astype(BF16)
        own_ref[capacity * j : capacity * (j + 1), :] = picked[:capacity, :]
        sent_ref[capacity * j : capacity * (j + 1), :] = picked[capacity:, :]


def gather_kernel(capacity, pick_ref, mine_ref, upper_ref, lower_ref, own_ref, sent_ref):
    for j, d in enumerate((mine_ref[...], joined(upper_ref, lower_ref))):
        picked = dot(pick_ref[2 * capacity * j : 2 * capacity * (j + 1), :], d).astype(BF16)
        own_ref[capacity * j : capacity * (j + 1), :] = picked[:capacity, :]
        sent_ref[capacity * j : capacity * (j + 1), :] = picked[capacity:, :]


def expert_kernel(
    me_ref,
    x_own_ref,
    x_far_ref,
    d_own_ref,
    d_far_ref,
    gate_ref,
    up_ref,
    down_ref,
    far_ref,
    own_ref,
    grads_ref,
    hidden_ref,
):
    features = d_own_ref.shape[1]
    units = gate_ref.shape[1]
    half = d_own_ref.shape[0]
    rows = 2 * half
    x = jnp.concatenate([x_own_ref[:, :features], x_far_ref[:, :features]], axis=0)
    gates = jnp.concatenate([x_own_ref[:, features:], x_far_ref[:, features:]], axis=0).astype(F32)
    mine = lax.broadcasted_iota(jnp.int32, (rows, LANES), 1) == me_ref[0]
    gating = jnp.sum(jnp.where(mine, gates, 0.0), axis=1, keepdims=True)
    d = jnp.concatenate([d_own_ref[...], d_far_ref[...]], axis=0)
    gate_pre = dot(x, gate_ref[...])
    up_pre = dot(x, up_ref[...])
    back_grad = dot(d, down_ref[...], ((1,), (1,)))
    sigmoid_gate = jax.nn.sigmoid(gate_pre)
    silu = gate_pre * sigmoid_gate
    hidden = (silu * up_pre).astype(BF16).astype(F32)
    router = jnp.sum(hidden * back_grad, axis=1, keepdims=True)
    hidden_grad = gating * back_grad
    gate_grad = hidden_grad * up_pre * sigmoid_gate * (1.0 + gate_pre * (1.0 - sigmoid_gate))
    gate_grad = gate_grad.astype(BF16)
    up_grad = (hidden_grad * silu).astype(BF16)
    grads_ref[:, :units] = gate_grad
    grads_ref[:, units:] = up_grad
    hidden_ref[...] = (gating * hidden).astype(BF16)
    term = dot(gate_grad, gate_ref[...], ((1,), (1,))) + dot(up_grad, up_ref[...], ((1,), (1,)))
    term = term.astype(BF16)
    router = jnp.where(mine, router, 0.0).astype(BF16)
    own_ref[:, :features] = term[:half, :]
    own_ref[:, features:] = router[:half, :]
    far_ref[:, :features] = term[half:, :]
    far_ref[:, features:] = router[half:, :]


def combine_kernel(capacity, pick_ref, own_ref, back_ref, upper_ref, lower_ref, mine_ref):
    rows = mine_ref.shape[0]
    for j in range(2):
        part = slice(capacity * j, capacity * (j + 1))
        terms = jnp.concatenate([own_ref[part, :], back_ref[part, :]], axis=0)
        total = dot(pick_ref[2 * capacity * j : 2 * capacity * (j + 1), :], terms, ((0,), (0,)))
        if j == 0:
            mine_ref[...] = total
        else:
            upper_ref[...] = total[: rows // 2, :].astype(BF16)
            lower_ref[...] = total[rows // 2 :, :].astype(BF16)


def summed(mine_ref, upper_ref, lower_ref, *refs):
    total = mine_ref[...] + joined(upper_ref, lower_ref).astype(F32)
    for ref in refs:
        total = total + ref[...].astype(F32)
    return total


def add_kernel(*refs):
    refs[-1][...] = summed(*refs[:-1]).astype(BF16)


def total_kernel(ids_ref, *refs):
    parts, (grad_ref, router_ref) = refs[:-2], refs[-2:]
    fanout, rows = ids_ref.shape
    features = grad_ref.shape[1]
    total = summed(*parts)
    grad_ref[...] = total[:, :features].astype(BF16)
    router = total[:, features:].T
    expert = lax.broadcasted_iota(jnp.int32, (LANES, rows), 0)
    for k in range(fanout):
        own = jnp.where(ids_ref[k : k + 1, :] == expert, router, 0.0)
        router_ref[k : k + 1, :] = jnp.sum(own, axis=0, keepdims=True).astype(BF16)


def delta_kernel(blocks, *refs):
    x_refs, d_refs = refs[:blocks], refs[blocks : 2 * blocks]
    grads_refs = refs[2 * blocks : 5 * blocks // 2]
    hidden_refs = refs[5 * blocks // 2 : 3 * blocks]
    gate_ref, up_ref, down_ref, x_all, d_all = refs[-5:]
    features, units = gate_ref.shape
    rows = d_refs[0].shape[0]
    for i in range(blocks):
        part = slice(i * rows, (i + 1) * rows)
        x_all[part, :] = x_refs[i][:, :features]
        d_all[part, :] = d_refs[i][...]
    grads = jnp.concatenate([ref[...] for ref in grads_refs], axis=0)
    hidden = jnp.concatenate([ref[...] for ref in hidden_refs], axis=0)
    step = 512

    @pl.loop(0, features // step)
    def _(i):
        cols = pl.ds(pl.multiple_of(i * step, step), step)
        both = dot(x_all[:, cols], grads, ((0,), (0,))).astype(BF16)
        gate_ref[cols, :] = both[:, :units]
        up_ref[cols, :] = both[:, units:]
        down_ref[:, cols] = dot(hidden, d_all[:, cols], ((0,), (0,))).astype(BF16)


def staged(tokens, cotangent, expert_ids, gate_levels, w_gate, w_up, w_down):
    devices = lax.axis_size("expert")
    planes = devices // PLANE
    tok_rows, fanout = expert_ids.shape
    features = tokens.shape[1]
    units = w_gate.shape[2]
    capacity = 3 * tok_rows * fanout // (2 * devices)
    wide = features + LANES
    half = 2 * capacity
    me = lax.axis_index("expert").reshape(1)
    ids = expert_ids.T
    gate_mat, up_mat, down_mat = w_gate[0], w_up[0], w_down[0]
    run = Chain()

    def along(array):
        return lax.ppermute(array, "expert", [(i, (i + PLANE) % devices) for i in range(devices)])

    def across(array):
        return lax.ppermute(array, "expert", [(i, i ^ 2) for i in range(devices)])

    def cores(halves):
        pairs = [(i, i ^ 1) for i in range(devices)]
        return [lax.ppermute(half, "expert", pairs) for half in halves]

    pick, own_x, far_x, own_d, far_d = ({} for _ in range(5))
    own_t, far_t, grads, hidden = ({} for _ in range(4))

    def slots_x(s, x, halves):
        pick[s], own_x[s], sent = run(
            functools.partial(slot_kernel, capacity),
            [((2 * half, tok_rows), BF16), ((half, wide), BF16), ((half, wide), BF16)],
            "slots_x",
            me,
            x,
            *cores(halves),
            smem=1,
        )
        far_x[s] = across(sent)

    def slots_d(s, d, halves):
        own_d[s], sent = run(
            functools.partial(gather_kernel, capacity),
            [((half, features), BF16)] * 2,
            "slots_d",
            pick[s],
            d,
            *cores(halves),
        )
        far_d[s] = across(sent)

    def expert(s):
        far, own_t[s], grads[s], hidden[s] = run(
            expert_kernel,
            [((half, wide), BF16)] * 2
            + [((2 * half, 2 * units), BF16), ((2 * half, units), BF16)],
            "expert",
            me,
            own_x[s],
            far_x[s],
            own_d[s],
            far_d[s],
            gate_mat,
            up_mat,
            down_mat,
            smem=1,
            limit=30,
        )
        far_t[s] = across(far)

    def combine(s):
        *halves, mine = run(
            functools.partial(combine_kernel, capacity),
            [((tok_rows // 2, wide), BF16)] * 2 + [((tok_rows, wide), F32)],
            "combine",
            pick[s],
            own_t[s],
            far_t[s],
        )
        return [mine, *cores(halves)]

    def add(*parts):
        return along(run(add_kernel, [((tok_rows, wide), BF16)], "add", *parts)[0])

    packed, *halves = run(
        pack_kernel,
        [((tok_rows, wide), BF16)]
        + [((tok_rows // 2, wide), BF16)] * 2
        + [((tok_rows // 2, features), BF16)] * 2,
        "pack",
        ids,
        gate_levels.T,
        tokens,
        cotangent,
    )
    x, d = along(packed), along(cotangent)
    slots_x(0, packed, halves[:2])
    slots_d(0, cotangent, halves[2:])
    last = planes - 1
    for s in range(1, planes):
        here, halves = run.hold(x, after=[far_x[s - 1]])
        if s < last:
            x = along(here)
        slots_x(s, here, halves)
        here, halves = run.hold(d, after=[far_d[s - 1]])
        if s < last:
            d = along(here)
        slots_d(s, here, halves)
        if 1 < s:
            expert(s - 1)
    passed = add(*combine(1))
    expert(last)
    expert(0)
    passed = add(*combine(2), passed)
    passed = add(*combine(3), passed)
    order = range(planes)
    gate_delta, up_delta, down_delta = run(
        functools.partial(delta_kernel, 2 * planes),
        [((features, units), BF16), ((features, units), BF16), ((units, features), BF16)],
        "deltas",
        *[block for s in order for block in (own_x[s], far_x[s])],
        *[block for s in order for block in (own_d[s], far_d[s])],
        *[grads[s] for s in order],
        *[hidden[s] for s in order],
        scratch=[pltpu.VMEM((2 * planes * half, features), BF16)] * 2,
        limit=40,
    )
    input_grad, router_grad = run(
        total_kernel,
        [((tok_rows, features), BF16), ((fanout, tok_rows), BF16)],
        "total",
        ids,
        *combine(0),
        passed,
    )
    return input_grad, router_grad.T, gate_delta[None], up_delta[None], down_delta[None]


def solution(mesh):
    devices = mesh.shape["expert"]
    tokens, experts = P(("groups", "expert"), None), P("expert", None, None)
    deltas = P(("groups", "expert"), None, None)

    def on_device(*arrays):
        tok_rows, fanout = arrays[2].shape
        capacity = 3 * tok_rows * fanout // (2 * devices)
        plan = staged if PLANE * capacity > tok_rows and devices % PLANE == 0 else direct
        return plan(*arrays)

    return jax.shard_map(
        on_device,
        mesh=mesh,
        in_specs=(tokens, tokens, tokens, tokens, experts, experts, experts),
        out_specs=(tokens, tokens, deltas, deltas, deltas),
        check_vma=False,
    )
```

```python
import functools

import jax
import jax.numpy as jnp
from jax import lax
from jax.experimental import pallas as pl
from jax.experimental.pallas import tpu as pltpu
from jax.sharding import PartitionSpec as P

BF16 = jnp.bfloat16
F32 = jnp.float32
LANES = 128
PLANE = 4


def project(inputs, gate_mat, up_mat):
    gate_pre = jnp.dot(inputs, gate_mat, preferred_element_type=jnp.float32)
    up_pre = jnp.dot(inputs, up_mat, preferred_element_type=jnp.float32)
    return (gate_pre, up_pre)


def backward(inputs, prepared, cotangent, gating, gate_mat, up_mat, down_mat):
    gate_pre, up_pre = prepared
    sigmoid_gate = jax.nn.sigmoid(gate_pre)
    hidden = (gate_pre * sigmoid_gate * up_pre).astype(jnp.bfloat16)
    back_grad = lax.dot_general(
        cotangent, down_mat, (((1,), (1,)), ((), ())), preferred_element_type=jnp.float32
    )
    router_term = jnp.sum(hidden.astype(jnp.float32) * back_grad, axis=1).astype(jnp.bfloat16)
    hidden_grad = gating[:, None] * back_grad
    gate_grad = (
        hidden_grad * up_pre * sigmoid_gate * (1.0 + gate_pre * (1.0 - sigmoid_gate))
    ).astype(jnp.bfloat16)
    up_grad = (hidden_grad * gate_pre * sigmoid_gate).astype(jnp.bfloat16)
    input_term = lax.dot_general(
        gate_grad, gate_mat, (((1,), (1,)), ((), ())), preferred_element_type=jnp.float32
    )
    input_term = input_term + lax.dot_general(
        up_grad, up_mat, (((1,), (1,)), ((), ())), preferred_element_type=jnp.float32
    )
    input_term = input_term.astype(jnp.bfloat16)
    scaled = (gating[:, None] * cotangent.astype(jnp.float32)).astype(jnp.bfloat16)
    down_delta = lax.dot_general(
        hidden, scaled, (((0,), (0,)), ((), ())), preferred_element_type=jnp.float32
    )
    gate_delta = lax.dot_general(
        inputs, gate_grad, (((0,), (0,)), ((), ())), preferred_element_type=jnp.float32
    )
    up_delta = lax.dot_general(
        inputs, up_grad, (((0,), (0,)), ((), ())), preferred_element_type=jnp.float32
    )
    return (input_term, router_term, gate_delta, up_delta, down_delta)


def direct(tokens, cotangent, expert_ids, gate_levels, w_gate, w_up, w_down):
    devices = lax.axis_size("expert")
    tok_rows, fanout = expert_ids.shape
    features = tokens.shape[1]
    capacity = 3 * tok_rows * fanout // (2 * devices)
    slot_rows = devices * capacity
    gate_mat = w_gate[0]
    up_mat = w_up[0]
    down_mat = w_down[0]
    chosen = expert_ids.reshape(-1)
    indicator = (chosen[:, None] == jnp.arange(devices, dtype=jnp.int32)[None, :]).astype(jnp.int32)
    earlier = jnp.cumsum(indicator, axis=0) - indicator
    position = jnp.sum(earlier * indicator, axis=1)
    target = chosen * capacity + position
    gating_local = (gate_levels.reshape(-1).astype(jnp.float32) / 256.0).astype(jnp.bfloat16)
    outbox_x = (
        jnp.zeros((slot_rows, features), jnp.bfloat16)
        .at[target]
        .set(jnp.repeat(tokens, fanout, axis=0))
    )
    outbox_dy = (
        jnp.zeros((slot_rows, features), jnp.bfloat16)
        .at[target]
        .set(jnp.repeat(cotangent, fanout, axis=0))
    )
    outbox_g = jnp.zeros((slot_rows,), jnp.bfloat16).at[target].set(gating_local)
    outbox_x = outbox_x.reshape(devices, capacity, features)
    outbox_dy = outbox_dy.reshape(devices, capacity, features)
    outbox_g = outbox_g.reshape(devices, capacity)
    exchange = functools.partial(
        lax.all_to_all, axis_name="expert", split_axis=0, concat_axis=0, tiled=True
    )
    rows_x = exchange(outbox_x).reshape(slot_rows, features)
    rows_dy = exchange(outbox_dy).reshape(slot_rows, features)
    rows_g = exchange(outbox_g).reshape(-1).astype(jnp.float32)
    prepared = project(rows_x, gate_mat, up_mat)
    input_term, router_term, gate_delta, up_delta, down_delta = backward(
        rows_x, prepared, rows_dy, rows_g, gate_mat, up_mat, down_mat
    )
    back_term = exchange(input_term.reshape(devices, capacity, features))
    back_router = exchange(router_term.reshape(devices, capacity))
    gathered_term = back_term.reshape(slot_rows, features)[target].astype(jnp.float32)
    input_grad = jnp.sum(gathered_term.reshape(tok_rows, fanout, features), axis=1).astype(
        jnp.bfloat16
    )
    router_grad = back_router.reshape(-1)[target].reshape(tok_rows, fanout)
    return (
        input_grad,
        router_grad,
        gate_delta.astype(jnp.bfloat16)[None],
        up_delta.astype(jnp.bfloat16)[None],
        down_delta.astype(jnp.bfloat16)[None],
    )


def dot(a, b, contract=((1,), (0,))):
    return lax.dot_general(a, b, (contract, ((), ())), preferred_element_type=F32)


class Chain:
    def __init__(self):
        self.last = []
        self.pending = []

    def __call__(self, kernel, outs, name, *operands, after=(), scratch=(), smem=0, hbm=0, limit=16):
        vmem = pl.BlockSpec(memory_space=pltpu.VMEM)
        scalar = pl.BlockSpec(memory_space=pltpu.SMEM)
        anywhere = pl.BlockSpec(memory_space=pl.ANY)
        outside = pl.BlockSpec(memory_space=pltpu.HBM)
        unused = [*self.last, *after]
        fixed = len(operands)

        def body(*refs):
            kernel(*refs[:fixed], *refs[fixed + len(unused) :])

        made = pl.pallas_call(
            body,
            out_shape=[jax.ShapeDtypeStruct(shape, kind) for shape, kind in outs],
            in_specs=[scalar] * smem
            + [outside] * hbm
            + [vmem] * (fixed - smem - hbm)
            + [anywhere] * len(unused),
            out_specs=[vmem] * len(outs),
            scratch_shapes=list(scratch),
            name=name,
            compiler_params=pltpu.CompilerParams(vmem_limit_bytes=limit << 20),
            cost_estimate=pl.CostEstimate(flops=1000, bytes_accessed=1000, transcendentals=0),
        )(*operands, *unused)
        self.last = [min(made, key=lambda array: array.size)]
        return made

    def hold(self, *arrays, after=()):
        unused = [*self.last, *self.pending, *after]
        self.pending = []
        anywhere = pl.BlockSpec(memory_space=pl.ANY)
        held = pl.pallas_call(
            lambda *refs: None,
            out_shape=[jax.ShapeDtypeStruct(array.shape, array.dtype) for array in arrays],
            in_specs=[anywhere] * (len(arrays) + len(unused)),
            out_specs=[anywhere] * len(arrays),
            input_output_aliases={i: i for i in range(len(arrays))},
            name="hold",
            compiler_params=pltpu.CompilerParams(vmem_limit_bytes=1 << 20),
            cost_estimate=pl.CostEstimate(flops=1000, bytes_accessed=1000, transcendentals=0),
        )(*arrays, *unused)
        self.last = held[:1]
        return held


def pack_kernel(ids_ref, levels_ref, x_ref, out_ref, ids_here, levels_here, sems):
    fanout, rows = ids_ref.shape
    features = x_ref.shape[1]
    moves = [(ids_ref, ids_here), (levels_ref, levels_here), (x_ref, out_ref.at[:, :features])]
    copies = [
        pltpu.make_async_copy(source, target, sems.at[i])
        for i, (source, target) in enumerate(moves)
    ]
    for copy in copies:
        copy.start()
    for copy in copies[:2]:
        copy.wait()
    expert = lax.broadcasted_iota(jnp.int32, (LANES, rows), 0)
    gates = jnp.zeros((LANES, rows), F32)
    for k in range(fanout):
        value = levels_here[k : k + 1, :].astype(F32) * (1.0 / 256.0)
        gates = gates + jnp.where(ids_here[k : k + 1, :] == expert, value, 0.0)
    out_ref[:, features:] = gates.T.astype(BF16)
    copies[2].wait()


def joined(refs):
    return jnp.concatenate([ref[...] for ref in refs], axis=0)


def slot_kernel(capacity, me_ref, x_ref, pick_ref, scaled_ref, *block_refs):
    rows = x_ref.shape[0]
    features = x_ref.shape[1] - LANES
    expert = lax.broadcasted_iota(jnp.int32, (8, LANES), 1)
    wanted = jnp.bitwise_xor(lax.broadcasted_iota(jnp.int32, (8, LANES), 0), me_ref[0])
    chooser = jnp.where(expert == wanted, 1.0, 0.0).astype(BF16)
    gates = dot(chooser, x_ref[:, features:], ((1,), (1,)))
    routed = jnp.where(gates > 0.0, 1.0, 0.0)
    before = lax.broadcasted_iota(jnp.int32, (rows, rows), 0)
    after = lax.broadcasted_iota(jnp.int32, (rows, rows), 1)
    earlier = jnp.where(before < after, 1.0, 0.0).astype(BF16)
    place = dot(routed.astype(BF16), earlier)
    place = jnp.where(routed > 0.0, place, -1.0)
    slot = lax.broadcasted_iota(jnp.int32, (capacity, rows), 0).astype(F32)
    chosen = [place[i : i + 1, :] == slot for i in range(PLANE)]
    pick = jnp.concatenate([jnp.where(here, 1.0, 0.0) for here in chosen], axis=0).astype(BF16)
    pick_ref[...] = pick
    scaled_ref[...] = jnp.concatenate(
        [jnp.where(here, gates[i : i + 1, :], 0.0) for i, here in enumerate(chosen)], axis=0
    ).astype(BF16)
    picked = dot(pick, x_ref[:, :features]).astype(BF16)
    for i, block_ref in enumerate(block_refs):
        block_ref[...] = picked[capacity * i : capacity * (i + 1), :]


def gather_kernel(capacity, scaled_ref, d_ref, *block_refs):
    picked = dot(scaled_ref[...], d_ref[...]).astype(BF16)
    for i, block_ref in enumerate(block_refs):
        block_ref[...] = picked[capacity * i : capacity * (i + 1), :]


def join_kernel(*refs):
    refs[-1][...] = joined(refs[:-1])


def expert_kernel(me_ref, *refs):
    x_refs, d_refs, (gate_ref, up_ref, down_ref) = refs[:3], refs[3:6], refs[6:9]
    grads_ref, hidden_ref, *term_refs = refs[9:]
    features, units = gate_ref.shape
    x, d = joined(x_refs), joined(d_refs)
    rows = x.shape[0]
    gate_pre = dot(x, gate_ref[...])
    up_pre = dot(x, up_ref[...])
    hidden_grad = dot(d, down_ref[...], ((1,), (1,)))
    sigmoid_gate = jax.nn.sigmoid(gate_pre)
    silu = gate_pre * sigmoid_gate
    hidden = (silu * up_pre).astype(BF16)
    router = jnp.sum(hidden.astype(F32) * hidden_grad, axis=1, keepdims=True)
    gate_grad = hidden_grad * up_pre * sigmoid_gate * (1.0 + gate_pre * (1.0 - sigmoid_gate))
    gate_grad = gate_grad.astype(BF16)
    up_grad = (hidden_grad * silu).astype(BF16)
    grads_ref[:, :units] = gate_grad
    grads_ref[:, units:] = up_grad
    hidden_ref[...] = hidden
    term = dot(gate_grad, gate_ref[...], ((1,), (1,))) + dot(up_grad, up_ref[...], ((1,), (1,)))
    term = term.astype(BF16)
    mine = lax.broadcasted_iota(jnp.int32, (rows, LANES), 1) == me_ref[0]
    router = jnp.where(mine, router, 0.0).astype(BF16)
    count = rows // len(term_refs)
    for i, term_ref in enumerate(term_refs):
        part = slice(count * i, count * (i + 1))
        term_ref[:, :features] = term[part, :]
        term_ref[:, features:] = router[part, :]


def home_kernel(columns, pick_ref, *refs):
    terms = jnp.concatenate([ref[:, columns] for ref in refs[:3]], axis=0)
    total = dot(pick_ref[...], terms, ((0,), (0,)))
    for passed_ref in refs[3:-1]:
        passed = passed_ref[...]
        if passed.shape[1] > terms.shape[1]:
            passed = passed[:, columns]
        total = total + passed.astype(F32)
    refs[-1][...] = total.astype(BF16)


def total_kernel(ids_ref, levels_ref, pick_ref, *refs):
    term_refs, passed_refs, (grad_ref, router_ref) = refs[:3], refs[3:-2], refs[-2:]
    fanout, rows = ids_ref.shape
    features = grad_ref.shape[1]
    passed = jnp.concatenate([ref[...] for ref in passed_refs], axis=1)
    total = dot(pick_ref[...], joined(term_refs), ((0,), (0,))) + passed.astype(F32)
    grad_ref[...] = total[:, :features].astype(BF16)
    router = total[:, features:].T
    expert = lax.broadcasted_iota(jnp.int32, (LANES, rows), 0)
    for k in range(fanout):
        own = jnp.where(ids_ref[k : k + 1, :] == expert, router, 0.0)
        own = jnp.sum(own, axis=0, keepdims=True)
        own = own * (256.0 / levels_ref[k : k + 1, :].astype(F32))
        router_ref[k : k + 1, :] = own.astype(BF16)


def delta_kernel(chunks, *refs):
    x_refs, d_refs = refs[: 3 * chunks], refs[3 * chunks : 6 * chunks]
    grads_refs, hidden_refs = refs[6 * chunks : 7 * chunks], refs[7 * chunks : 8 * chunks]
    gate_ref, up_ref, down_ref, done_ref, x_all, d_all = refs[8 * chunks :]
    done_ref[...] = jnp.zeros_like(done_ref)
    features, units = gate_ref.shape
    start = 0
    for x_ref, d_ref in zip(x_refs, d_refs):
        rows = x_ref.shape[0]
        x_all[start : start + rows, :] = x_ref[...]
        d_all[start : start + rows, :] = d_ref[...]
        start += rows
    grads = jnp.concatenate([ref[...] for ref in grads_refs], axis=0)
    hidden = jnp.concatenate([ref[...] for ref in hidden_refs], axis=0)
    step = 512

    @pl.loop(0, features // step)
    def _(i):
        cols = pl.ds(pl.multiple_of(i * step, step), step)
        both = dot(x_all[:, cols], grads, ((0,), (0,))).astype(BF16)
        gate_ref[cols, :] = both[:, :units]
        up_ref[cols, :] = both[:, units:]
        down_ref[:, cols] = dot(hidden, d_all[:, cols], ((0,), (0,))).astype(BF16)


def staged(tokens, cotangent, expert_ids, gate_levels, w_gate, w_up, w_down):
    devices = lax.axis_size("expert")
    planes = devices // PLANE
    tok_rows, fanout = expert_ids.shape
    features = tokens.shape[1]
    units = w_gate.shape[2]
    capacity = 3 * tok_rows * fanout // (2 * devices)
    wide = features + LANES
    rows = PLANE * capacity
    me = lax.axis_index("expert").reshape(1)
    ids, levels = expert_ids.T, gate_levels.T
    gate_mat, up_mat, down_mat = w_gate[0], w_up[0], w_down[0]
    run = Chain()

    def along(array):
        return lax.ppermute(array, "expert", [(i, (i + PLANE) % devices) for i in range(devices)])

    def across(array):
        return lax.ppermute(array, "expert", [(i, i ^ 2) for i in range(devices)])

    def cores(array):
        return lax.ppermute(array, "expert", [(i, i ^ 1) for i in range(devices)])

    def swap(blocks, pieces):
        own, near, far, diagonal = blocks
        size = -(-capacity // 16 // pieces) * 16
        passing = [cores(diagonal[i : i + size]) for i in range(0, capacity, size)]
        near = cores(near)
        return own, near, far, passing

    def send(own, near, far, passing, wait=True):
        after = run.pending + ([near] if wait else [])
        run.pending = [] if wait else [near]
        (both,) = run(
            join_kernel,
            [((2 * capacity, far.shape[1]), BF16)],
            "join",
            far,
            *passing,
            after=after,
        )
        return [own, near, across(both)]

    def spread(blocks, pieces=1):
        return send(*swap(blocks, pieces), wait=pieces == 1)

    pick, scaled, rows_x, rows_d, grads, hidden, terms = ({} for _ in range(7))

    def slots_x(s, x, pieces=1):
        pick[s], scaled[s], *blocks = run(
            functools.partial(slot_kernel, capacity),
            [((rows, tok_rows), BF16)] * 2 + [((capacity, features), BF16)] * PLANE,
            "slots_x",
            me,
            x,
            smem=1,
        )
        rows_x[s] = spread(blocks, pieces)

    def slots_d(s, d):
        blocks = run(
            functools.partial(gather_kernel, capacity),
            [((capacity, features), BF16)] * PLANE,
            "slots_d",
            scaled[s],
            d,
        )
        rows_d[s] = spread(blocks)

    def expert(s, after=()):
        grads[s], hidden[s], *terms[s] = run(
            expert_kernel,
            [((rows, 2 * units), BF16), ((rows, units), BF16)]
            + [((capacity, wide), BF16)] * PLANE,
            "expert",
            me,
            *rows_x[s],
            *rows_d[s],
            gate_mat,
            up_mat,
            down_mat,
            smem=1,
            limit=30,
            after=after,
        )

    def home(s, columns, *passed):
        return along(
            run(
                functools.partial(home_kernel, columns),
                [((tok_rows, columns.stop - columns.start), BF16)],
                "home",
                pick[s],
                *terms[s],
                *passed,
            )[0]
        )

    (packed,) = run(
        pack_kernel,
        [((tok_rows, wide), BF16)],
        "pack",
        ids,
        levels,
        tokens,
        hbm=3,
        scratch=[pltpu.VMEM(ids.shape, jnp.int32)] * 2 + [pltpu.SemaphoreType.DMA((3,))],
        limit=60,
    )
    x, d = along(packed), along(cotangent)
    slots_x(0, packed, 2)
    slots_d(0, cotangent)
    last = planes - 1
    for s in range(1, planes):
        (here,) = run.hold(x, after=rows_x[s - 1][2:])
        if s < last:
            x = along(here)
        slots_x(s, here, 2 if s == last else 1)
        if s == last:
            expert(s - 1)
        (here,) = run.hold(d, after=rows_d[s - 1][2:])
        if s < last:
            d = along(here)
        slots_d(s, here)
        if s == 1:
            expert(0)
        if s == 2:
            expert(1, after=rows_x[2][2:])
            terms[1] = spread(terms[1], 2)
    passed = home(1, slice(0, wide))
    terms[2] = send(*swap(run.hold(*terms[2], after=rows_x[last][2:]), 2), wait=False)
    swapped = swap(run.hold(*terms[0]), 2)
    run.pending = [swapped[1], *swapped[3]]
    expert(last, after=[passed])
    terms[last] = spread(terms[last], 2)
    terms[0] = send(*swapped)
    cuts = [0, 896, 1664, wide]
    columns = [slice(start, end) for start, end in zip(cuts, cuts[1:])]
    passed = [home(2, part, passed) for part in columns]
    passed = [home(last, part, whole) for whole, part in zip(passed, columns)]
    order = range(planes)
    gate_delta, up_delta, down_delta, _ = run(
        functools.partial(delta_kernel, planes),
        [((features, units), BF16)] * 2 + [((units, features), BF16), ((8, LANES), F32)],
        "deltas",
        *[block for s in order for block in rows_x[s]],
        *[block for s in order for block in rows_d[s]],
        *[grads[s] for s in order],
        *[hidden[s] for s in order],
        scratch=[pltpu.VMEM((planes * rows, features), BF16)] * 2,
        limit=40,
    )
    input_grad, router_grad = run(
        total_kernel,
        [((tok_rows, features), BF16), ((fanout, tok_rows), BF16)],
        "total",
        ids,
        levels,
        pick[0],
        *terms[0],
        *passed,
    )
    return input_grad, router_grad.T, gate_delta[None], up_delta[None], down_delta[None]


def solution(mesh):
    devices = mesh.shape["expert"]
    tokens, experts = P(("groups", "expert"), None), P("expert", None, None)
    deltas = P(("groups", "expert"), None, None)

    def on_device(*arrays):
        tok_rows, fanout = arrays[2].shape
        capacity = 3 * tok_rows * fanout // (2 * devices)
        plan = staged if PLANE * capacity > tok_rows and devices % PLANE == 0 else direct
        return plan(*arrays)

    return jax.shard_map(
        on_device,
        mesh=mesh,
        in_specs=(tokens, tokens, tokens, tokens, experts, experts, experts),
        out_specs=(tokens, tokens, deltas, deltas, deltas),
        check_vma=False,
    )
```

```python
import functools

import jax
import jax.numpy as jnp
from jax import lax
from jax.experimental import pallas as pl
from jax.experimental.pallas import tpu as pltpu
from jax.sharding import PartitionSpec as P

BF16 = jnp.bfloat16
F32 = jnp.float32
LANES = 128
PLANE = 4


def project(inputs, gate_mat, up_mat):
    gate_pre = jnp.dot(inputs, gate_mat, preferred_element_type=jnp.float32)
    up_pre = jnp.dot(inputs, up_mat, preferred_element_type=jnp.float32)
    return (gate_pre, up_pre)


def backward(inputs, prepared, cotangent, gating, gate_mat, up_mat, down_mat):
    gate_pre, up_pre = prepared
    sigmoid_gate = jax.nn.sigmoid(gate_pre)
    hidden = (gate_pre * sigmoid_gate * up_pre).astype(jnp.bfloat16)
    back_grad = lax.dot_general(
        cotangent, down_mat, (((1,), (1,)), ((), ())), preferred_element_type=jnp.float32
    )
    router_term = jnp.sum(hidden.astype(jnp.float32) * back_grad, axis=1).astype(jnp.bfloat16)
    hidden_grad = gating[:, None] * back_grad
    gate_grad = (
        hidden_grad * up_pre * sigmoid_gate * (1.0 + gate_pre * (1.0 - sigmoid_gate))
    ).astype(jnp.bfloat16)
    up_grad = (hidden_grad * gate_pre * sigmoid_gate).astype(jnp.bfloat16)
    input_term = lax.dot_general(
        gate_grad, gate_mat, (((1,), (1,)), ((), ())), preferred_element_type=jnp.float32
    )
    input_term = input_term + lax.dot_general(
        up_grad, up_mat, (((1,), (1,)), ((), ())), preferred_element_type=jnp.float32
    )
    input_term = input_term.astype(jnp.bfloat16)
    scaled = (gating[:, None] * cotangent.astype(jnp.float32)).astype(jnp.bfloat16)
    down_delta = lax.dot_general(
        hidden, scaled, (((0,), (0,)), ((), ())), preferred_element_type=jnp.float32
    )
    gate_delta = lax.dot_general(
        inputs, gate_grad, (((0,), (0,)), ((), ())), preferred_element_type=jnp.float32
    )
    up_delta = lax.dot_general(
        inputs, up_grad, (((0,), (0,)), ((), ())), preferred_element_type=jnp.float32
    )
    return (input_term, router_term, gate_delta, up_delta, down_delta)


def direct(tokens, cotangent, expert_ids, gate_levels, w_gate, w_up, w_down):
    devices = lax.axis_size("expert")
    tok_rows, fanout = expert_ids.shape
    features = tokens.shape[1]
    capacity = 3 * tok_rows * fanout // (2 * devices)
    slot_rows = devices * capacity
    gate_mat = w_gate[0]
    up_mat = w_up[0]
    down_mat = w_down[0]
    chosen = expert_ids.reshape(-1)
    indicator = (chosen[:, None] == jnp.arange(devices, dtype=jnp.int32)[None, :]).astype(jnp.int32)
    earlier = jnp.cumsum(indicator, axis=0) - indicator
    position = jnp.sum(earlier * indicator, axis=1)
    target = chosen * capacity + position
    gating_local = (gate_levels.reshape(-1).astype(jnp.float32) / 256.0).astype(jnp.bfloat16)
    outbox_x = (
        jnp.zeros((slot_rows, features), jnp.bfloat16)
        .at[target]
        .set(jnp.repeat(tokens, fanout, axis=0))
    )
    outbox_dy = (
        jnp.zeros((slot_rows, features), jnp.bfloat16)
        .at[target]
        .set(jnp.repeat(cotangent, fanout, axis=0))
    )
    outbox_g = jnp.zeros((slot_rows,), jnp.bfloat16).at[target].set(gating_local)
    outbox_x = outbox_x.reshape(devices, capacity, features)
    outbox_dy = outbox_dy.reshape(devices, capacity, features)
    outbox_g = outbox_g.reshape(devices, capacity)
    exchange = functools.partial(
        lax.all_to_all, axis_name="expert", split_axis=0, concat_axis=0, tiled=True
    )
    rows_x = exchange(outbox_x).reshape(slot_rows, features)
    rows_dy = exchange(outbox_dy).reshape(slot_rows, features)
    rows_g = exchange(outbox_g).reshape(-1).astype(jnp.float32)
    prepared = project(rows_x, gate_mat, up_mat)
    input_term, router_term, gate_delta, up_delta, down_delta = backward(
        rows_x, prepared, rows_dy, rows_g, gate_mat, up_mat, down_mat
    )
    back_term = exchange(input_term.reshape(devices, capacity, features))
    back_router = exchange(router_term.reshape(devices, capacity))
    gathered_term = back_term.reshape(slot_rows, features)[target].astype(jnp.float32)
    input_grad = jnp.sum(gathered_term.reshape(tok_rows, fanout, features), axis=1).astype(
        jnp.bfloat16
    )
    router_grad = back_router.reshape(-1)[target].reshape(tok_rows, fanout)
    return (
        input_grad,
        router_grad,
        gate_delta.astype(jnp.bfloat16)[None],
        up_delta.astype(jnp.bfloat16)[None],
        down_delta.astype(jnp.bfloat16)[None],
    )


def dot(a, b, contract=((1,), (0,))):
    return lax.dot_general(a, b, (contract, ((), ())), preferred_element_type=F32)


class Chain:
    def __init__(self):
        self.last = []
        self.pending = []

    def __call__(self, kernel, outs, name, *operands, after=(), scratch=(), smem=0, hbm=0, limit=16):
        vmem = pl.BlockSpec(memory_space=pltpu.VMEM)
        scalar = pl.BlockSpec(memory_space=pltpu.SMEM)
        anywhere = pl.BlockSpec(memory_space=pl.ANY)
        outside = pl.BlockSpec(memory_space=pltpu.HBM)
        unused = [*self.last, *after]
        fixed = len(operands)

        def body(*refs):
            kernel(*refs[:fixed], *refs[fixed + len(unused) :])

        made = pl.pallas_call(
            body,
            out_shape=[jax.ShapeDtypeStruct(shape, kind) for shape, kind in outs],
            in_specs=[scalar] * smem
            + [outside] * hbm
            + [vmem] * (fixed - smem - hbm)
            + [anywhere] * len(unused),
            out_specs=[vmem] * len(outs),
            scratch_shapes=list(scratch),
            name=name,
            compiler_params=pltpu.CompilerParams(vmem_limit_bytes=limit << 20),
            cost_estimate=pl.CostEstimate(flops=1000, bytes_accessed=1000, transcendentals=0),
        )(*operands, *unused)
        self.last = [min(made, key=lambda array: array.size)]
        return made

    def hold(self, *arrays, after=()):
        unused = [*self.last, *self.pending, *after]
        self.pending = []
        anywhere = pl.BlockSpec(memory_space=pl.ANY)
        held = pl.pallas_call(
            lambda *refs: None,
            out_shape=[jax.ShapeDtypeStruct(array.shape, array.dtype) for array in arrays],
            in_specs=[anywhere] * (len(arrays) + len(unused)),
            out_specs=[anywhere] * len(arrays),
            input_output_aliases={i: i for i in range(len(arrays))},
            name="hold",
            compiler_params=pltpu.CompilerParams(vmem_limit_bytes=1 << 20),
            cost_estimate=pl.CostEstimate(flops=1000, bytes_accessed=1000, transcendentals=0),
        )(*arrays, *unused)
        self.last = held[:1]
        return held


def pack_kernel(ids_ref, levels_ref, x_ref, out_ref, ids_here, levels_here, sems):
    fanout, rows = ids_ref.shape
    features = x_ref.shape[1]
    moves = [(ids_ref, ids_here), (levels_ref, levels_here), (x_ref, out_ref.at[:, :features])]
    copies = [
        pltpu.make_async_copy(source, target, sems.at[i])
        for i, (source, target) in enumerate(moves)
    ]
    for copy in copies:
        copy.start()
    for copy in copies[:2]:
        copy.wait()
    expert = lax.broadcasted_iota(jnp.int32, (LANES, rows), 0)
    gates = jnp.zeros((LANES, rows), F32)
    for k in range(fanout):
        value = levels_here[k : k + 1, :].astype(F32) * (1.0 / 256.0)
        gates = gates + jnp.where(ids_here[k : k + 1, :] == expert, value, 0.0)
    out_ref[:, features:] = gates.T.astype(BF16)
    copies[2].wait()


def joined(refs):
    return jnp.concatenate([ref[...] for ref in refs], axis=0)


def slot_kernel(capacity, me_ref, x_ref, pick_ref, scaled_ref, *block_refs):
    rows = x_ref.shape[0]
    features = x_ref.shape[1] - LANES
    expert = lax.broadcasted_iota(jnp.int32, (8, LANES), 1)
    wanted = jnp.bitwise_xor(lax.broadcasted_iota(jnp.int32, (8, LANES), 0), me_ref[0])
    chooser = jnp.where(expert == wanted, 1.0, 0.0).astype(BF16)
    gates = dot(chooser, x_ref[:, features:], ((1,), (1,)))
    routed = jnp.where(gates > 0.0, 1.0, 0.0)
    before = lax.broadcasted_iota(jnp.int32, (rows, rows), 0)
    after = lax.broadcasted_iota(jnp.int32, (rows, rows), 1)
    earlier = jnp.where(before < after, 1.0, 0.0).astype(BF16)
    place = dot(routed.astype(BF16), earlier)
    place = jnp.where(routed > 0.0, place, -1.0)
    slot = lax.broadcasted_iota(jnp.int32, (capacity, rows), 0).astype(F32)
    chosen = [place[i : i + 1, :] == slot for i in range(PLANE)]
    pick = jnp.concatenate([jnp.where(here, 1.0, 0.0) for here in chosen], axis=0).astype(BF16)
    pick_ref[...] = pick
    scaled_ref[...] = jnp.concatenate(
        [jnp.where(here, gates[i : i + 1, :], 0.0) for i, here in enumerate(chosen)], axis=0
    ).astype(BF16)
    picked = dot(pick, x_ref[:, :features]).astype(BF16)
    for i, block_ref in enumerate(block_refs):
        block_ref[...] = picked[capacity * i : capacity * (i + 1), :]


def gather_kernel(capacity, scaled_ref, d_ref, *block_refs):
    picked = dot(scaled_ref[...], d_ref[...]).astype(BF16)
    for i, block_ref in enumerate(block_refs):
        block_ref[...] = picked[capacity * i : capacity * (i + 1), :]


def join_kernel(*refs):
    refs[-1][...] = joined(refs[:-1])


def expert_kernel(me_ref, *refs):
    x_refs, d_refs, (gate_ref, up_ref, down_ref) = refs[:3], refs[3:6], refs[6:9]
    grads_ref, hidden_ref, *term_refs = refs[9:]
    features, units = gate_ref.shape
    x, d = joined(x_refs), joined(d_refs)
    rows = x.shape[0]
    gate_pre = dot(x, gate_ref[...])
    up_pre = dot(x, up_ref[...])
    hidden_grad = dot(d, down_ref[...], ((1,), (1,)))
    sigmoid_gate = jax.nn.sigmoid(gate_pre)
    silu = gate_pre * sigmoid_gate
    hidden = (silu * up_pre).astype(BF16)
    router = jnp.sum(hidden.astype(F32) * hidden_grad, axis=1, keepdims=True)
    gate_grad = hidden_grad * up_pre * sigmoid_gate * (1.0 + gate_pre * (1.0 - sigmoid_gate))
    gate_grad = gate_grad.astype(BF16)
    up_grad = (hidden_grad * silu).astype(BF16)
    grads_ref[:, :units] = gate_grad
    grads_ref[:, units:] = up_grad
    hidden_ref[...] = hidden
    term = dot(gate_grad, gate_ref[...], ((1,), (1,))) + dot(up_grad, up_ref[...], ((1,), (1,)))
    term = term.astype(BF16)
    mine = lax.broadcasted_iota(jnp.int32, (rows, LANES), 1) == me_ref[0]
    router = jnp.where(mine, router, 0.0).astype(BF16)
    count = rows // len(term_refs)
    for i, term_ref in enumerate(term_refs):
        part = slice(count * i, count * (i + 1))
        term_ref[:, :features] = term[part, :]
        term_ref[:, features:] = router[part, :]


def home_kernel(columns, pick_ref, *refs):
    terms = jnp.concatenate([ref[:, columns] for ref in refs[:3]], axis=0)
    total = dot(pick_ref[...], terms, ((0,), (0,)))
    for passed_ref in refs[3:-1]:
        passed = passed_ref[...]
        if passed.shape[1] > terms.shape[1]:
            passed = passed[:, columns]
        total = total + passed.astype(F32)
    refs[-1][...] = total.astype(BF16)


def total_kernel(ids_ref, levels_ref, pick_ref, *refs):
    term_refs, passed_refs, (grad_ref, router_ref) = refs[:3], refs[3:-2], refs[-2:]
    fanout, rows = ids_ref.shape
    features = grad_ref.shape[1]
    passed = jnp.concatenate([ref[...] for ref in passed_refs], axis=1)
    total = dot(pick_ref[...], joined(term_refs), ((0,), (0,))) + passed.astype(F32)
    grad_ref[...] = total[:, :features].astype(BF16)
    router = total[:, features:].T
    expert = lax.broadcasted_iota(jnp.int32, (LANES, rows), 0)
    for k in range(fanout):
        own = jnp.where(ids_ref[k : k + 1, :] == expert, router, 0.0)
        own = jnp.sum(own, axis=0, keepdims=True)
        own = own * (256.0 / levels_ref[k : k + 1, :].astype(F32))
        router_ref[k : k + 1, :] = own.astype(BF16)


def delta_kernel(chunks, *refs):
    x_refs, d_refs = refs[: 3 * chunks], refs[3 * chunks : 6 * chunks]
    grads_refs, hidden_refs = refs[6 * chunks : 7 * chunks], refs[7 * chunks : 8 * chunks]
    gate_ref, up_ref, down_ref, done_ref, x_all, d_all = refs[8 * chunks :]
    done_ref[...] = jnp.zeros_like(done_ref)
    features, units = gate_ref.shape
    start = 0
    for x_ref, d_ref in zip(x_refs, d_refs):
        rows = x_ref.shape[0]
        x_all[start : start + rows, :] = x_ref[...]
        d_all[start : start + rows, :] = d_ref[...]
        start += rows
    grads = jnp.concatenate([ref[...] for ref in grads_refs], axis=0)
    hidden = jnp.concatenate([ref[...] for ref in hidden_refs], axis=0)
    step = 512

    @pl.loop(0, features // step)
    def _(i):
        cols = pl.ds(pl.multiple_of(i * step, step), step)
        both = dot(x_all[:, cols], grads, ((0,), (0,))).astype(BF16)
        gate_ref[cols, :] = both[:, :units]
        up_ref[cols, :] = both[:, units:]
        down_ref[:, cols] = dot(hidden, d_all[:, cols], ((0,), (0,))).astype(BF16)


def staged(tokens, cotangent, expert_ids, gate_levels, w_gate, w_up, w_down):
    devices = lax.axis_size("expert")
    planes = devices // PLANE
    tok_rows, fanout = expert_ids.shape
    features = tokens.shape[1]
    units = w_gate.shape[2]
    capacity = 3 * tok_rows * fanout // (2 * devices)
    wide = features + LANES
    rows = PLANE * capacity
    me = lax.axis_index("expert").reshape(1)
    ids, levels = expert_ids.T, gate_levels.T
    gate_mat, up_mat, down_mat = w_gate[0], w_up[0], w_down[0]
    run = Chain()

    def along(array):
        return lax.ppermute(array, "expert", [(i, (i + PLANE) % devices) for i in range(devices)])

    def across(array):
        return lax.ppermute(array, "expert", [(i, i ^ 2) for i in range(devices)])

    def cores(array):
        return lax.ppermute(array, "expert", [(i, i ^ 1) for i in range(devices)])

    def swap(blocks, pieces):
        own, near, far, diagonal = blocks
        size = -(-capacity // 16 // pieces) * 16
        passing = [cores(diagonal[i : i + size]) for i in range(0, capacity, size)]
        near = cores(near)
        return own, near, far, passing

    def send(own, near, far, passing, wait=True):
        after = run.pending + ([near] if wait else [])
        run.pending = [] if wait else [near]
        (both,) = run(
            join_kernel,
            [((2 * capacity, far.shape[1]), BF16)],
            "join",
            far,
            *passing,
            after=after,
        )
        return [own, near, across(both)]

    def spread(blocks, pieces=1):
        return send(*swap(blocks, pieces), wait=pieces == 1)

    pick, scaled, rows_x, rows_d, grads, hidden, terms = ({} for _ in range(7))

    def slots_x(s, x, pieces=1):
        pick[s], scaled[s], *blocks = run(
            functools.partial(slot_kernel, capacity),
            [((rows, tok_rows), BF16)] * 2 + [((capacity, features), BF16)] * PLANE,
            "slots_x",
            me,
            x,
            smem=1,
        )
        rows_x[s] = spread(blocks, pieces)

    def slots_d(s, d, after=()):
        blocks = run(
            functools.partial(gather_kernel, capacity),
            [((capacity, features), BF16)] * PLANE,
            "slots_d",
            scaled[s],
            d,
            after=after,
        )
        rows_d[s] = spread(blocks)

    def expert(s, after=()):
        grads[s], hidden[s], *terms[s] = run(
            expert_kernel,
            [((rows, 2 * units), BF16), ((rows, units), BF16)]
            + [((capacity, wide), BF16)] * PLANE,
            "expert",
            me,
            *rows_x[s],
            *rows_d[s],
            gate_mat,
            up_mat,
            down_mat,
            smem=1,
            limit=30,
            after=after,
        )

    def home(s, columns, *passed):
        return along(
            run(
                functools.partial(home_kernel, columns),
                [((tok_rows, columns.stop - columns.start), BF16)],
                "home",
                pick[s],
                *terms[s],
                *passed,
            )[0]
        )

    (packed,) = run(
        pack_kernel,
        [((tok_rows, wide), BF16)],
        "pack",
        ids,
        levels,
        tokens,
        hbm=3,
        scratch=[pltpu.VMEM(ids.shape, jnp.int32)] * 2 + [pltpu.SemaphoreType.DMA((3,))],
        limit=60,
    )
    x, d = along(packed), along(cotangent)
    slots_x(0, packed, 2)
    slots_d(0, cotangent)
    last = planes - 1
    for s in range(1, planes):
        (here,) = run.hold(x, after=terms[1][1:] if s == last else rows_x[s - 1][2:])
        if s < last:
            x = along(here)
        slots_x(s, here, 2 if s == last else 1)
        if s > 1:
            expert(s - 1)
        if s == 2:
            terms[1] = spread(terms[1], 2)
            run.pending = []
        (here,) = run.hold(d, after=rows_d[s - 1][2:])
        if s == 1:
            d = along(here)
        if s == 2:
            run.pending += rows_x[s][2:]
        slots_d(s, here)
        if s == 1:
            expert(0)
        if s == 2:
            (here,) = run.hold(here)
            d = along(here)
    passed = home(1, slice(0, wide))
    terms[2] = send(*swap(run.hold(*terms[2], after=rows_x[last][2:]), 2), wait=False)
    swapped = swap(run.hold(*terms[0]), 2)
    run.pending = [swapped[1], *swapped[3]]
    expert(last)
    terms[last] = spread(terms[last], 2)
    terms[0] = send(*swapped)
    cuts = [0, 896, 1664, wide]
    columns = [slice(start, end) for start, end in zip(cuts, cuts[1:])]
    passed = [home(2, part, passed) for part in columns]
    passed = [home(last, part, whole) for whole, part in zip(passed, columns)]
    order = range(planes)
    gate_delta, up_delta, down_delta, _ = run(
        functools.partial(delta_kernel, planes),
        [((features, units), BF16)] * 2 + [((units, features), BF16), ((8, LANES), F32)],
        "deltas",
        *[block for s in order for block in rows_x[s]],
        *[block for s in order for block in rows_d[s]],
        *[grads[s] for s in order],
        *[hidden[s] for s in order],
        scratch=[pltpu.VMEM((planes * rows, features), BF16)] * 2,
        limit=40,
    )
    input_grad, router_grad = run(
        total_kernel,
        [((tok_rows, features), BF16), ((fanout, tok_rows), BF16)],
        "total",
        ids,
        levels,
        pick[0],
        *terms[0],
        *passed,
    )
    return input_grad, router_grad.T, gate_delta[None], up_delta[None], down_delta[None]


def solution(mesh):
    devices = mesh.shape["expert"]
    tokens, experts = P(("groups", "expert"), None), P("expert", None, None)
    deltas = P(("groups", "expert"), None, None)

    def on_device(*arrays):
        tok_rows, fanout = arrays[2].shape
        capacity = 3 * tok_rows * fanout // (2 * devices)
        plan = staged if PLANE * capacity > tok_rows and devices % PLANE == 0 else direct
        return plan(*arrays)

    return jax.shard_map(
        on_device,
        mesh=mesh,
        in_specs=(tokens, tokens, tokens, tokens, experts, experts, experts),
        out_specs=(tokens, tokens, deltas, deltas, deltas),
        check_vma=False,
    )
```

```python
import functools

import jax
import jax.numpy as jnp
from jax import lax
from jax.experimental import pallas as pl
from jax.experimental.pallas import tpu as pltpu
from jax.sharding import PartitionSpec as P

BF16 = jnp.bfloat16
F32 = jnp.float32
LANES = 128
PLANE = 4


def project(inputs, gate_mat, up_mat):
    gate_pre = jnp.dot(inputs, gate_mat, preferred_element_type=jnp.float32)
    up_pre = jnp.dot(inputs, up_mat, preferred_element_type=jnp.float32)
    return (gate_pre, up_pre)


def backward(inputs, prepared, cotangent, gating, gate_mat, up_mat, down_mat):
    gate_pre, up_pre = prepared
    sigmoid_gate = jax.nn.sigmoid(gate_pre)
    hidden = (gate_pre * sigmoid_gate * up_pre).astype(jnp.bfloat16)
    back_grad = lax.dot_general(
        cotangent, down_mat, (((1,), (1,)), ((), ())), preferred_element_type=jnp.float32
    )
    router_term = jnp.sum(hidden.astype(jnp.float32) * back_grad, axis=1).astype(jnp.bfloat16)
    hidden_grad = gating[:, None] * back_grad
    gate_grad = (
        hidden_grad * up_pre * sigmoid_gate * (1.0 + gate_pre * (1.0 - sigmoid_gate))
    ).astype(jnp.bfloat16)
    up_grad = (hidden_grad * gate_pre * sigmoid_gate).astype(jnp.bfloat16)
    input_term = lax.dot_general(
        gate_grad, gate_mat, (((1,), (1,)), ((), ())), preferred_element_type=jnp.float32
    )
    input_term = input_term + lax.dot_general(
        up_grad, up_mat, (((1,), (1,)), ((), ())), preferred_element_type=jnp.float32
    )
    input_term = input_term.astype(jnp.bfloat16)
    scaled = (gating[:, None] * cotangent.astype(jnp.float32)).astype(jnp.bfloat16)
    down_delta = lax.dot_general(
        hidden, scaled, (((0,), (0,)), ((), ())), preferred_element_type=jnp.float32
    )
    gate_delta = lax.dot_general(
        inputs, gate_grad, (((0,), (0,)), ((), ())), preferred_element_type=jnp.float32
    )
    up_delta = lax.dot_general(
        inputs, up_grad, (((0,), (0,)), ((), ())), preferred_element_type=jnp.float32
    )
    return (input_term, router_term, gate_delta, up_delta, down_delta)


def direct(tokens, cotangent, expert_ids, gate_levels, w_gate, w_up, w_down):
    devices = lax.axis_size("expert")
    tok_rows, fanout = expert_ids.shape
    features = tokens.shape[1]
    capacity = 3 * tok_rows * fanout // (2 * devices)
    slot_rows = devices * capacity
    gate_mat = w_gate[0]
    up_mat = w_up[0]
    down_mat = w_down[0]
    chosen = expert_ids.reshape(-1)
    indicator = (chosen[:, None] == jnp.arange(devices, dtype=jnp.int32)[None, :]).astype(jnp.int32)
    earlier = jnp.cumsum(indicator, axis=0) - indicator
    position = jnp.sum(earlier * indicator, axis=1)
    target = chosen * capacity + position
    gating_local = (gate_levels.reshape(-1).astype(jnp.float32) / 256.0).astype(jnp.bfloat16)
    outbox_x = (
        jnp.zeros((slot_rows, features), jnp.bfloat16)
        .at[target]
        .set(jnp.repeat(tokens, fanout, axis=0))
    )
    outbox_dy = (
        jnp.zeros((slot_rows, features), jnp.bfloat16)
        .at[target]
        .set(jnp.repeat(cotangent, fanout, axis=0))
    )
    outbox_g = jnp.zeros((slot_rows,), jnp.bfloat16).at[target].set(gating_local)
    outbox_x = outbox_x.reshape(devices, capacity, features)
    outbox_dy = outbox_dy.reshape(devices, capacity, features)
    outbox_g = outbox_g.reshape(devices, capacity)
    exchange = functools.partial(
        lax.all_to_all, axis_name="expert", split_axis=0, concat_axis=0, tiled=True
    )
    rows_x = exchange(outbox_x).reshape(slot_rows, features)
    rows_dy = exchange(outbox_dy).reshape(slot_rows, features)
    rows_g = exchange(outbox_g).reshape(-1).astype(jnp.float32)
    prepared = project(rows_x, gate_mat, up_mat)
    input_term, router_term, gate_delta, up_delta, down_delta = backward(
        rows_x, prepared, rows_dy, rows_g, gate_mat, up_mat, down_mat
    )
    back_term = exchange(input_term.reshape(devices, capacity, features))
    back_router = exchange(router_term.reshape(devices, capacity))
    gathered_term = back_term.reshape(slot_rows, features)[target].astype(jnp.float32)
    input_grad = jnp.sum(gathered_term.reshape(tok_rows, fanout, features), axis=1).astype(
        jnp.bfloat16
    )
    router_grad = back_router.reshape(-1)[target].reshape(tok_rows, fanout)
    return (
        input_grad,
        router_grad,
        gate_delta.astype(jnp.bfloat16)[None],
        up_delta.astype(jnp.bfloat16)[None],
        down_delta.astype(jnp.bfloat16)[None],
    )


def dot(a, b, contract=((1,), (0,))):
    return lax.dot_general(a, b, (contract, ((), ())), preferred_element_type=F32)


class Chain:
    def __init__(self):
        self.last = []
        self.pending = []

    def __call__(self, kernel, outs, name, *operands, after=(), scratch=(), smem=0, hbm=0, limit=16):
        vmem = pl.BlockSpec(memory_space=pltpu.VMEM)
        scalar = pl.BlockSpec(memory_space=pltpu.SMEM)
        anywhere = pl.BlockSpec(memory_space=pl.ANY)
        outside = pl.BlockSpec(memory_space=pltpu.HBM)
        unused = [*self.last, *after]
        fixed = len(operands)

        def body(*refs):
            kernel(*refs[:fixed], *refs[fixed + len(unused) :])

        made = pl.pallas_call(
            body,
            out_shape=[jax.ShapeDtypeStruct(shape, kind) for shape, kind in outs],
            in_specs=[scalar] * smem
            + [outside] * hbm
            + [vmem] * (fixed - smem - hbm)
            + [anywhere] * len(unused),
            out_specs=[vmem] * len(outs),
            scratch_shapes=list(scratch),
            name=name,
            compiler_params=pltpu.CompilerParams(vmem_limit_bytes=limit << 20),
            cost_estimate=pl.CostEstimate(flops=1000, bytes_accessed=1000, transcendentals=0),
        )(*operands, *unused)
        self.last = [min(made, key=lambda array: array.size)]
        return made

    def hold(self, *arrays, after=()):
        unused = [*self.last, *self.pending, *after]
        self.pending = []
        anywhere = pl.BlockSpec(memory_space=pl.ANY)
        held = pl.pallas_call(
            lambda *refs: None,
            out_shape=[jax.ShapeDtypeStruct(array.shape, array.dtype) for array in arrays],
            in_specs=[anywhere] * (len(arrays) + len(unused)),
            out_specs=[anywhere] * len(arrays),
            input_output_aliases={i: i for i in range(len(arrays))},
            name="hold",
            compiler_params=pltpu.CompilerParams(vmem_limit_bytes=1 << 20),
            cost_estimate=pl.CostEstimate(flops=1000, bytes_accessed=1000, transcendentals=0),
        )(*arrays, *unused)
        self.last = held[:1]
        return held


def pack_kernel(ids_ref, levels_ref, x_ref, out_ref, ids_here, levels_here, sems):
    fanout, rows = ids_ref.shape
    features = x_ref.shape[1]
    moves = [(ids_ref, ids_here), (levels_ref, levels_here), (x_ref, out_ref.at[:, :features])]
    copies = [
        pltpu.make_async_copy(source, target, sems.at[i])
        for i, (source, target) in enumerate(moves)
    ]
    for copy in copies:
        copy.start()
    for copy in copies[:2]:
        copy.wait()
    expert = lax.broadcasted_iota(jnp.int32, (LANES, rows), 0)
    gates = jnp.zeros((LANES, rows), F32)
    for k in range(fanout):
        value = levels_here[k : k + 1, :].astype(F32) * (1.0 / 256.0)
        gates = gates + jnp.where(ids_here[k : k + 1, :] == expert, value, 0.0)
    out_ref[:, features:] = gates.T.astype(BF16)
    copies[2].wait()


def joined(refs):
    return jnp.concatenate([ref[...] for ref in refs], axis=0)


def slot_kernel(capacity, me_ref, x_ref, pick_ref, scaled_ref, *block_refs):
    rows = x_ref.shape[0]
    features = x_ref.shape[1] - LANES
    expert = lax.broadcasted_iota(jnp.int32, (8, LANES), 1)
    wanted = jnp.bitwise_xor(lax.broadcasted_iota(jnp.int32, (8, LANES), 0), me_ref[0])
    chooser = jnp.where(expert == wanted, 1.0, 0.0).astype(BF16)
    gates = dot(chooser, x_ref[:, features:], ((1,), (1,)))
    routed = jnp.where(gates > 0.0, 1.0, 0.0)
    before = lax.broadcasted_iota(jnp.int32, (rows, rows), 0)
    after = lax.broadcasted_iota(jnp.int32, (rows, rows), 1)
    earlier = jnp.where(before < after, 1.0, 0.0).astype(BF16)
    place = dot(routed.astype(BF16), earlier)
    place = jnp.where(routed > 0.0, place, -1.0)
    slot = lax.broadcasted_iota(jnp.int32, (capacity, rows), 0).astype(F32)
    chosen = [place[i : i + 1, :] == slot for i in range(PLANE)]
    pick = jnp.concatenate([jnp.where(here, 1.0, 0.0) for here in chosen], axis=0).astype(BF16)
    pick_ref[...] = pick
    scaled_ref[...] = jnp.concatenate(
        [jnp.where(here, gates[i : i + 1, :], 0.0) for i, here in enumerate(chosen)], axis=0
    ).astype(BF16)
    picked = dot(pick, x_ref[:, :features]).astype(BF16)
    for i, block_ref in enumerate(block_refs):
        block_ref[...] = picked[capacity * i : capacity * (i + 1), :]


def gather_kernel(capacity, scaled_ref, d_ref, *block_refs):
    picked = dot(scaled_ref[...], d_ref[...]).astype(BF16)
    for i, block_ref in enumerate(block_refs):
        block_ref[...] = picked[capacity * i : capacity * (i + 1), :]


def join_kernel(*refs):
    refs[-1][...] = joined(refs[:-1])


def expert_kernel(me_ref, *refs):
    x_refs, d_refs, (gate_ref, up_ref, down_ref) = refs[:3], refs[3:6], refs[6:9]
    grads_ref, hidden_ref, *term_refs = refs[9:]
    features, units = gate_ref.shape
    x, d = joined(x_refs), joined(d_refs)
    rows = x.shape[0]
    gate_pre = dot(x, gate_ref[...])
    up_pre = dot(x, up_ref[...])
    hidden_grad = dot(d, down_ref[...], ((1,), (1,)))
    sigmoid_gate = jax.nn.sigmoid(gate_pre)
    silu = gate_pre * sigmoid_gate
    hidden = (silu * up_pre).astype(BF16)
    router = jnp.sum(hidden.astype(F32) * hidden_grad, axis=1, keepdims=True)
    gate_grad = hidden_grad * up_pre * sigmoid_gate * (1.0 + gate_pre * (1.0 - sigmoid_gate))
    gate_grad = gate_grad.astype(BF16)
    up_grad = (hidden_grad * silu).astype(BF16)
    grads_ref[:, :units] = gate_grad
    grads_ref[:, units:] = up_grad
    hidden_ref[...] = hidden
    term = dot(gate_grad, gate_ref[...], ((1,), (1,))) + dot(up_grad, up_ref[...], ((1,), (1,)))
    term = term.astype(BF16)
    mine = lax.broadcasted_iota(jnp.int32, (rows, LANES), 1) == me_ref[0]
    router = jnp.where(mine, router, 0.0).astype(BF16)
    count = rows // len(term_refs)
    for i, term_ref in enumerate(term_refs):
        part = slice(count * i, count * (i + 1))
        term_ref[:, :features] = term[part, :]
        term_ref[:, features:] = router[part, :]


def home_kernel(columns, pick_ref, *refs):
    terms = jnp.concatenate([ref[:, columns] for ref in refs[:3]], axis=0)
    total = dot(pick_ref[...], terms, ((0,), (0,)))
    for passed_ref in refs[3:-1]:
        passed = passed_ref[...]
        if passed.shape[1] > terms.shape[1]:
            passed = passed[:, columns]
        total = total + passed.astype(F32)
    refs[-1][...] = total.astype(BF16)


def total_kernel(ids_ref, levels_ref, pick_ref, *refs):
    term_refs, passed_refs, (grad_ref, router_ref) = refs[:3], refs[3:-2], refs[-2:]
    fanout, rows = ids_ref.shape
    features = grad_ref.shape[1]
    passed = jnp.concatenate([ref[...] for ref in passed_refs], axis=1)
    total = dot(pick_ref[...], joined(term_refs), ((0,), (0,))) + passed.astype(F32)
    grad_ref[...] = total[:, :features].astype(BF16)
    router = total[:, features:].T
    expert = lax.broadcasted_iota(jnp.int32, (LANES, rows), 0)
    for k in range(fanout):
        own = jnp.where(ids_ref[k : k + 1, :] == expert, router, 0.0)
        own = jnp.sum(own, axis=0, keepdims=True)
        own = own * (256.0 / levels_ref[k : k + 1, :].astype(F32))
        router_ref[k : k + 1, :] = own.astype(BF16)


def delta_kernel(chunks, *refs):
    x_refs, d_refs = refs[: 3 * chunks], refs[3 * chunks : 6 * chunks]
    grads_refs, hidden_refs = refs[6 * chunks : 7 * chunks], refs[7 * chunks : 8 * chunks]
    gate_ref, up_ref, down_ref, done_ref, x_all, d_all = refs[8 * chunks :]
    done_ref[...] = jnp.zeros_like(done_ref)
    features, units = gate_ref.shape
    start = 0
    for x_ref, d_ref in zip(x_refs, d_refs):
        rows = x_ref.shape[0]
        x_all[start : start + rows, :] = x_ref[...]
        d_all[start : start + rows, :] = d_ref[...]
        start += rows
    grads = jnp.concatenate([ref[...] for ref in grads_refs], axis=0)
    hidden = jnp.concatenate([ref[...] for ref in hidden_refs], axis=0)
    step = 512

    @pl.loop(0, features // step)
    def _(i):
        cols = pl.ds(pl.multiple_of(i * step, step), step)
        both = dot(x_all[:, cols], grads, ((0,), (0,))).astype(BF16)
        gate_ref[cols, :] = both[:, :units]
        up_ref[cols, :] = both[:, units:]
        down_ref[:, cols] = dot(hidden, d_all[:, cols], ((0,), (0,))).astype(BF16)


def staged(tokens, cotangent, expert_ids, gate_levels, w_gate, w_up, w_down):
    devices = lax.axis_size("expert")
    planes = devices // PLANE
    tok_rows, fanout = expert_ids.shape
    features = tokens.shape[1]
    units = w_gate.shape[2]
    capacity = 3 * tok_rows * fanout // (2 * devices)
    wide = features + LANES
    rows = PLANE * capacity
    me = lax.axis_index("expert").reshape(1)
    ids, levels = expert_ids.T, gate_levels.T
    gate_mat, up_mat, down_mat = w_gate[0], w_up[0], w_down[0]
    run = Chain()

    ring = [*range(0, planes, 2), *range(1, planes, 2)[::-1]]
    follows = dict(zip(ring, ring[1:] + ring[:1]))

    def along(array):
        pairs = [(i, follows[i // PLANE] * PLANE + i % PLANE) for i in range(devices)]
        return lax.ppermute(array, "expert", pairs)

    def across(array):
        return lax.ppermute(array, "expert", [(i, i ^ 2) for i in range(devices)])

    def cores(array):
        return lax.ppermute(array, "expert", [(i, i ^ 1) for i in range(devices)])

    def swap(blocks, pieces):
        own, near, far, diagonal = blocks
        size = -(-capacity // 16 // pieces) * 16
        passing = [cores(diagonal[i : i + size]) for i in range(0, capacity, size)]
        near = cores(near)
        return own, near, far, passing

    def send(own, near, far, passing, wait=True):
        after = run.pending + ([near] if wait else [])
        run.pending = [] if wait else [near]
        (both,) = run(
            join_kernel,
            [((2 * capacity, far.shape[1]), BF16)],
            "join",
            far,
            *passing,
            after=after,
        )
        return [own, near, across(both)]

    def spread(blocks, pieces=1):
        return send(*swap(blocks, pieces), wait=pieces == 1)

    pick, scaled, rows_x, rows_d, grads, hidden, terms = ({} for _ in range(7))

    def slots_x(s, x, pieces=1):
        pick[s], scaled[s], *blocks = run(
            functools.partial(slot_kernel, capacity),
            [((rows, tok_rows), BF16)] * 2 + [((capacity, features), BF16)] * PLANE,
            "slots_x",
            me,
            x,
            smem=1,
        )
        rows_x[s] = spread(blocks, pieces)

    def slots_d(s, d, after=()):
        blocks = run(
            functools.partial(gather_kernel, capacity),
            [((capacity, features), BF16)] * PLANE,
            "slots_d",
            scaled[s],
            d,
            after=after,
        )
        rows_d[s] = spread(blocks)

    def expert(s, after=()):
        grads[s], hidden[s], *terms[s] = run(
            expert_kernel,
            [((rows, 2 * units), BF16), ((rows, units), BF16)]
            + [((capacity, wide), BF16)] * PLANE,
            "expert",
            me,
            *rows_x[s],
            *rows_d[s],
            gate_mat,
            up_mat,
            down_mat,
            smem=1,
            limit=30,
            after=after,
        )

    def home(s, columns, *passed):
        return along(
            run(
                functools.partial(home_kernel, columns),
                [((tok_rows, columns.stop - columns.start), BF16)],
                "home",
                pick[s],
                *terms[s],
                *passed,
            )[0]
        )

    (packed,) = run(
        pack_kernel,
        [((tok_rows, wide), BF16)],
        "pack",
        ids,
        levels,
        tokens,
        hbm=3,
        scratch=[pltpu.VMEM(ids.shape, jnp.int32)] * 2 + [pltpu.SemaphoreType.DMA((3,))],
        limit=60,
    )
    x, d = along(packed), along(cotangent)
    slots_x(0, packed, 2)
    slots_d(0, cotangent)
    last = planes - 1
    for s in range(1, planes):
        (here,) = run.hold(x, after=terms[1][1:] if s == last else rows_x[s - 1][2:])
        if s < last:
            x = along(here)
        slots_x(s, here, 2 if s == last else 1)
        if s > 1:
            expert(s - 1)
        if s == 2:
            terms[1] = spread(terms[1], 2)
            run.pending = []
        (here,) = run.hold(d, after=rows_d[s - 1][2:])
        if s == 1:
            d = along(here)
        if s == 2:
            run.pending += rows_x[s][2:]
        slots_d(s, here)
        if s == 1:
            expert(0)
        if s == 2:
            (here,) = run.hold(here)
            d = along(here)
    passed = home(1, slice(0, wide))
    terms[2] = send(*swap(run.hold(*terms[2], after=rows_x[last][2:]), 2), wait=False)
    swapped = swap(run.hold(*terms[0]), 2)
    run.pending = [swapped[1], *swapped[3]]
    expert(last)
    terms[last] = spread(terms[last], 2)
    terms[0] = send(*swapped)
    cuts = [0, 896, 1664, wide]
    columns = [slice(start, end) for start, end in zip(cuts, cuts[1:])]
    passed = [home(2, part, passed) for part in columns]
    passed = [home(last, part, whole) for whole, part in zip(passed, columns)]
    order = range(planes)
    gate_delta, up_delta, down_delta, _ = run(
        functools.partial(delta_kernel, planes),
        [((features, units), BF16)] * 2 + [((units, features), BF16), ((8, LANES), F32)],
        "deltas",
        *[block for s in order for block in rows_x[s]],
        *[block for s in order for block in rows_d[s]],
        *[grads[s] for s in order],
        *[hidden[s] for s in order],
        scratch=[pltpu.VMEM((planes * rows, features), BF16)] * 2,
        limit=40,
    )
    input_grad, router_grad = run(
        total_kernel,
        [((tok_rows, features), BF16), ((fanout, tok_rows), BF16)],
        "total",
        ids,
        levels,
        pick[0],
        *terms[0],
        *passed,
    )
    return input_grad, router_grad.T, gate_delta[None], up_delta[None], down_delta[None]


def solution(mesh):
    devices = mesh.shape["expert"]
    tokens, experts = P(("groups", "expert"), None), P("expert", None, None)
    deltas = P(("groups", "expert"), None, None)

    def on_device(*arrays):
        tok_rows, fanout = arrays[2].shape
        capacity = 3 * tok_rows * fanout // (2 * devices)
        plan = staged if PLANE * capacity > tok_rows and devices % PLANE == 0 else direct
        return plan(*arrays)

    return jax.shard_map(
        on_device,
        mesh=mesh,
        in_specs=(tokens, tokens, tokens, tokens, experts, experts, experts),
        out_specs=(tokens, tokens, deltas, deltas, deltas),
        check_vma=False,
    )
```

```python
import functools

import jax
import jax.numpy as jnp
from jax import lax
from jax.experimental import pallas as pl
from jax.experimental.pallas import tpu as pltpu
from jax.sharding import PartitionSpec as P

BF16 = jnp.bfloat16
F32 = jnp.float32
LANES = 128
PLANE = 4


def project(inputs, gate_mat, up_mat):
    gate_pre = jnp.dot(inputs, gate_mat, preferred_element_type=jnp.float32)
    up_pre = jnp.dot(inputs, up_mat, preferred_element_type=jnp.float32)
    return (gate_pre, up_pre)


def backward(inputs, prepared, cotangent, gating, gate_mat, up_mat, down_mat):
    gate_pre, up_pre = prepared
    sigmoid_gate = jax.nn.sigmoid(gate_pre)
    hidden = (gate_pre * sigmoid_gate * up_pre).astype(jnp.bfloat16)
    back_grad = lax.dot_general(
        cotangent, down_mat, (((1,), (1,)), ((), ())), preferred_element_type=jnp.float32
    )
    router_term = jnp.sum(hidden.astype(jnp.float32) * back_grad, axis=1).astype(jnp.bfloat16)
    hidden_grad = gating[:, None] * back_grad
    gate_grad = (
        hidden_grad * up_pre * sigmoid_gate * (1.0 + gate_pre * (1.0 - sigmoid_gate))
    ).astype(jnp.bfloat16)
    up_grad = (hidden_grad * gate_pre * sigmoid_gate).astype(jnp.bfloat16)
    input_term = lax.dot_general(
        gate_grad, gate_mat, (((1,), (1,)), ((), ())), preferred_element_type=jnp.float32
    )
    input_term = input_term + lax.dot_general(
        up_grad, up_mat, (((1,), (1,)), ((), ())), preferred_element_type=jnp.float32
    )
    input_term = input_term.astype(jnp.bfloat16)
    scaled = (gating[:, None] * cotangent.astype(jnp.float32)).astype(jnp.bfloat16)
    down_delta = lax.dot_general(
        hidden, scaled, (((0,), (0,)), ((), ())), preferred_element_type=jnp.float32
    )
    gate_delta = lax.dot_general(
        inputs, gate_grad, (((0,), (0,)), ((), ())), preferred_element_type=jnp.float32
    )
    up_delta = lax.dot_general(
        inputs, up_grad, (((0,), (0,)), ((), ())), preferred_element_type=jnp.float32
    )
    return (input_term, router_term, gate_delta, up_delta, down_delta)


def direct(tokens, cotangent, expert_ids, gate_levels, w_gate, w_up, w_down):
    devices = lax.axis_size("expert")
    tok_rows, fanout = expert_ids.shape
    features = tokens.shape[1]
    capacity = 3 * tok_rows * fanout // (2 * devices)
    slot_rows = devices * capacity
    gate_mat = w_gate[0]
    up_mat = w_up[0]
    down_mat = w_down[0]
    chosen = expert_ids.reshape(-1)
    indicator = (chosen[:, None] == jnp.arange(devices, dtype=jnp.int32)[None, :]).astype(jnp.int32)
    earlier = jnp.cumsum(indicator, axis=0) - indicator
    position = jnp.sum(earlier * indicator, axis=1)
    target = chosen * capacity + position
    gating_local = (gate_levels.reshape(-1).astype(jnp.float32) / 256.0).astype(jnp.bfloat16)
    outbox_x = (
        jnp.zeros((slot_rows, features), jnp.bfloat16)
        .at[target]
        .set(jnp.repeat(tokens, fanout, axis=0))
    )
    outbox_dy = (
        jnp.zeros((slot_rows, features), jnp.bfloat16)
        .at[target]
        .set(jnp.repeat(cotangent, fanout, axis=0))
    )
    outbox_g = jnp.zeros((slot_rows,), jnp.bfloat16).at[target].set(gating_local)
    outbox_x = outbox_x.reshape(devices, capacity, features)
    outbox_dy = outbox_dy.reshape(devices, capacity, features)
    outbox_g = outbox_g.reshape(devices, capacity)
    exchange = functools.partial(
        lax.all_to_all, axis_name="expert", split_axis=0, concat_axis=0, tiled=True
    )
    rows_x = exchange(outbox_x).reshape(slot_rows, features)
    rows_dy = exchange(outbox_dy).reshape(slot_rows, features)
    rows_g = exchange(outbox_g).reshape(-1).astype(jnp.float32)
    prepared = project(rows_x, gate_mat, up_mat)
    input_term, router_term, gate_delta, up_delta, down_delta = backward(
        rows_x, prepared, rows_dy, rows_g, gate_mat, up_mat, down_mat
    )
    back_term = exchange(input_term.reshape(devices, capacity, features))
    back_router = exchange(router_term.reshape(devices, capacity))
    gathered_term = back_term.reshape(slot_rows, features)[target].astype(jnp.float32)
    input_grad = jnp.sum(gathered_term.reshape(tok_rows, fanout, features), axis=1).astype(
        jnp.bfloat16
    )
    router_grad = back_router.reshape(-1)[target].reshape(tok_rows, fanout)
    return (
        input_grad,
        router_grad,
        gate_delta.astype(jnp.bfloat16)[None],
        up_delta.astype(jnp.bfloat16)[None],
        down_delta.astype(jnp.bfloat16)[None],
    )


def dot(a, b, contract=((1,), (0,))):
    return lax.dot_general(a, b, (contract, ((), ())), preferred_element_type=F32)


class Chain:
    def __init__(self):
        self.last = []
        self.pending = []

    def __call__(self, kernel, outs, name, *operands, after=(), scratch=(), smem=0, hbm=0, limit=16):
        vmem = pl.BlockSpec(memory_space=pltpu.VMEM)
        scalar = pl.BlockSpec(memory_space=pltpu.SMEM)
        anywhere = pl.BlockSpec(memory_space=pl.ANY)
        outside = pl.BlockSpec(memory_space=pltpu.HBM)
        unused = [*self.last, *after]
        fixed = len(operands)

        def body(*refs):
            kernel(*refs[:fixed], *refs[fixed + len(unused) :])

        made = pl.pallas_call(
            body,
            out_shape=[jax.ShapeDtypeStruct(shape, kind) for shape, kind in outs],
            in_specs=[scalar] * smem
            + [outside] * hbm
            + [vmem] * (fixed - smem - hbm)
            + [anywhere] * len(unused),
            out_specs=[vmem] * len(outs),
            scratch_shapes=list(scratch),
            name=name,
            compiler_params=pltpu.CompilerParams(vmem_limit_bytes=limit << 20),
            cost_estimate=pl.CostEstimate(flops=1000, bytes_accessed=1000, transcendentals=0),
        )(*operands, *unused)
        self.last = [min(made, key=lambda array: array.size)]
        return made

    def hold(self, *arrays, after=()):
        unused = [*self.last, *self.pending, *after]
        self.pending = []
        anywhere = pl.BlockSpec(memory_space=pl.ANY)
        held = pl.pallas_call(
            lambda *refs: None,
            out_shape=[jax.ShapeDtypeStruct(array.shape, array.dtype) for array in arrays],
            in_specs=[anywhere] * (len(arrays) + len(unused)),
            out_specs=[anywhere] * len(arrays),
            input_output_aliases={i: i for i in range(len(arrays))},
            name="hold",
            compiler_params=pltpu.CompilerParams(vmem_limit_bytes=1 << 20),
            cost_estimate=pl.CostEstimate(flops=1000, bytes_accessed=1000, transcendentals=0),
        )(*arrays, *unused)
        self.last = held[:1]
        return held


def joined(refs):
    return jnp.concatenate([ref[...] for ref in refs], axis=0)


def unstacked(ref, rows, start, stop):
    blocks = range(start // LANES, stop // LANES)
    return jnp.concatenate([ref[rows * i : rows * (i + 1), :] for i in blocks], axis=1)


def pack_kernel(ids_ref, levels_ref, x_ref, out_ref, ids_here, levels_here, sems):
    fanout, rows = ids_ref.shape
    features = x_ref.shape[1]
    experts = out_ref.shape[0] - rows * features // LANES
    moves = [(ids_ref, ids_here), (levels_ref, levels_here)]
    for i in range(features // LANES):
        source = x_ref.at[:, LANES * i : LANES * (i + 1)]
        moves.append((source, out_ref.at[rows * i : rows * (i + 1), :]))
    copies = [
        pltpu.make_async_copy(source, target, sems.at[i])
        for i, (source, target) in enumerate(moves)
    ]
    for copy in copies:
        copy.start()
    for copy in copies[:2]:
        copy.wait()
    expert = lax.broadcasted_iota(jnp.int32, (experts, rows), 0)
    gates = jnp.zeros((experts, rows), F32)
    for k in range(fanout):
        value = levels_here[k : k + 1, :].astype(F32) * (1.0 / 256.0)
        gates = gates + jnp.where(ids_here[k : k + 1, :] == expert, value, 0.0)
    out_ref[out_ref.shape[0] - experts :, :] = gates.astype(BF16)
    for copy in copies[2:]:
        copy.wait()


def slot_kernel(capacity, me_ref, x_ref, pick_ref, scaled_ref, *block_refs):
    features = block_refs[0].shape[1]
    rows = pick_ref.shape[1]
    table = x_ref[rows * features // LANES :, :]
    experts = table.shape[0]
    expert = lax.broadcasted_iota(jnp.int32, (8, experts), 1)
    wanted = jnp.bitwise_xor(lax.broadcasted_iota(jnp.int32, (8, experts), 0), me_ref[0])
    chooser = jnp.where(expert == wanted, 1.0, 0.0).astype(BF16)
    gates = dot(chooser, table)
    routed = jnp.where(gates > 0.0, 1.0, 0.0)
    before = lax.broadcasted_iota(jnp.int32, (rows, rows), 0)
    after = lax.broadcasted_iota(jnp.int32, (rows, rows), 1)
    earlier = jnp.where(before < after, 1.0, 0.0).astype(BF16)
    place = dot(routed.astype(BF16), earlier)
    place = jnp.where(routed > 0.0, place, -1.0)
    slot = lax.broadcasted_iota(jnp.int32, (capacity, rows), 0).astype(F32)
    chosen = [place[i : i + 1, :] == slot for i in range(PLANE)]
    pick = jnp.concatenate([jnp.where(here, 1.0, 0.0) for here in chosen], axis=0).astype(BF16)
    pick_ref[...] = pick
    scaled_ref[...] = jnp.concatenate(
        [jnp.where(here, gates[i : i + 1, :], 0.0) for i, here in enumerate(chosen)], axis=0
    ).astype(BF16)
    picked = dot(pick, unstacked(x_ref, rows, 0, features)).astype(BF16)
    for i, block_ref in enumerate(block_refs):
        block_ref[...] = picked[capacity * i : capacity * (i + 1), :]


def gather_kernel(capacity, scaled_ref, d_ref, *block_refs):
    picked = dot(scaled_ref[...], d_ref[...]).astype(BF16)
    for i, block_ref in enumerate(block_refs):
        block_ref[...] = picked[capacity * i : capacity * (i + 1), :]


def join_kernel(*refs):
    refs[-1][...] = joined(refs[:-1])


def stack_kernel(features, *refs):
    *block_refs, out_ref = refs
    rows = sum(ref.shape[0] for ref in block_refs)
    for i in range(features // LANES):
        blocks = [ref[:, LANES * i : LANES * (i + 1)] for ref in block_refs]
        out_ref[rows * i : rows * (i + 1), :] = jnp.concatenate(blocks, axis=0)
    lanes = jnp.concatenate([ref[:, features:] for ref in block_refs], axis=0).astype(F32)
    blank = jnp.zeros((LANES - rows, LANES), F32)
    experts = out_ref.shape[0] - rows * features // LANES
    router = jnp.concatenate([lanes, blank], axis=0).T[:experts, :]
    out_ref[rows * features // LANES :, :] = router.astype(BF16)


def expert_kernel(me_ref, *refs):
    x_refs, d_refs, (gate_ref, up_ref, down_ref) = refs[:3], refs[3:6], refs[6:9]
    grads_ref, hidden_ref, *term_refs = refs[9:]
    features, units = gate_ref.shape
    x, d = joined(x_refs), joined(d_refs)
    rows = x.shape[0]
    gate_pre = dot(x, gate_ref[...])
    up_pre = dot(x, up_ref[...])
    hidden_grad = dot(d, down_ref[...], ((1,), (1,)))
    sigmoid_gate = jax.nn.sigmoid(gate_pre)
    silu = gate_pre * sigmoid_gate
    hidden = (silu * up_pre).astype(BF16)
    router = jnp.sum(hidden.astype(F32) * hidden_grad, axis=1, keepdims=True)
    gate_grad = hidden_grad * up_pre * sigmoid_gate * (1.0 + gate_pre * (1.0 - sigmoid_gate))
    gate_grad = gate_grad.astype(BF16)
    up_grad = (hidden_grad * silu).astype(BF16)
    grads_ref[:, :units] = gate_grad
    grads_ref[:, units:] = up_grad
    hidden_ref[...] = hidden
    term = dot(gate_grad, gate_ref[...], ((1,), (1,))) + dot(up_grad, up_ref[...], ((1,), (1,)))
    term = term.astype(BF16)
    mine = lax.broadcasted_iota(jnp.int32, (rows, LANES), 1) == me_ref[0]
    router = jnp.where(mine, router, 0.0).astype(BF16)
    count = rows // len(term_refs)
    for i, term_ref in enumerate(term_refs):
        part = slice(count * i, count * (i + 1))
        term_ref[:, :features] = term[part, :]
        term_ref[:, features:] = router[part, :]


def plane_sum(pick_ref, term_refs, features, columns, experts):
    own_ref, near_ref, far_ref = term_refs
    half = pick_ref.shape[0] // 2
    terms = jnp.concatenate(
        [
            own_ref[:, columns],
            near_ref[:, columns],
            unstacked(far_ref, half, columns.start, columns.stop),
        ],
        axis=0,
    )
    total = dot(pick_ref[...], terms, ((0,), (0,)))
    if not experts:
        return total, None
    lanes = jnp.concatenate([own_ref[:, features:], near_ref[:, features:]], axis=0)
    router = dot(lanes, pick_ref[:half, :], ((0,), (0,)))[:experts, :]
    router = router + dot(far_ref[half * features // LANES :, :half], pick_ref[half:, :])
    return total, router


def home_kernel(features, columns, pick_ref, *refs):
    *refs, out_ref = refs
    rows = pick_ref.shape[1]
    experts = out_ref.shape[0] - rows
    total, router = plane_sum(pick_ref, refs[:3], features, columns, experts)
    for passed_ref in refs[3:]:
        passed = passed_ref[:rows, :]
        if passed.shape[1] > total.shape[1]:
            passed = passed[:, columns]
        total = total + passed.astype(F32)
        if experts:
            router = router + passed_ref[rows:, :LANES].astype(F32)
    out_ref[:rows, :] = total.astype(BF16)
    if experts:
        rest = jnp.zeros((experts, out_ref.shape[1] - rows), F32)
        out_ref[rows:, :] = jnp.concatenate([router, rest], axis=1).astype(BF16)


def total_kernel(ids_ref, levels_ref, pick_ref, *refs):
    term_refs, passed_refs, (grad_ref, router_ref) = refs[:3], refs[3:-2], refs[-2:]
    fanout, rows = ids_ref.shape
    features = grad_ref.shape[1]
    experts = passed_refs[-1].shape[0] - rows
    passed = jnp.concatenate([ref[:rows, :] for ref in passed_refs], axis=1)
    total, router = plane_sum(pick_ref, term_refs, features, slice(0, features), experts)
    grad_ref[...] = (total + passed.astype(F32)).astype(BF16)
    router = router + passed_refs[-1][rows:, :LANES].astype(F32)
    expert = lax.broadcasted_iota(jnp.int32, (experts, rows), 0)
    for k in range(fanout):
        own = jnp.where(ids_ref[k : k + 1, :] == expert, router, 0.0)
        own = jnp.sum(own, axis=0, keepdims=True)
        own = own * (256.0 / levels_ref[k : k + 1, :].astype(F32))
        router_ref[k : k + 1, :] = own.astype(BF16)


def stacked(refs, whole_ref):
    start = 0
    for ref in refs:
        whole_ref[start : start + ref.shape[0], :] = ref[...]
        start += ref.shape[0]


def down_kernel(chunks, *refs):
    *d_refs, down_ref, done_ref, d_all = refs
    hidden_refs, d_refs = d_refs[:chunks], d_refs[chunks:]
    done_ref[...] = jnp.zeros_like(done_ref)
    stacked(d_refs, d_all)
    hidden = joined(hidden_refs)
    step = 512

    @pl.loop(0, down_ref.shape[1] // step)
    def _(i):
        cols = pl.ds(pl.multiple_of(i * step, step), step)
        down_ref[:, cols] = dot(hidden, d_all[:, cols], ((0,), (0,))).astype(BF16)


def gate_up_kernel(chunks, *refs):
    *x_refs, gate_ref, up_ref, done_ref, x_all = refs
    grads_refs, x_refs = x_refs[:chunks], x_refs[chunks:]
    done_ref[...] = jnp.zeros_like(done_ref)
    stacked(x_refs, x_all)
    grads = joined(grads_refs)
    features, units = gate_ref.shape
    step = 512

    @pl.loop(0, features // step)
    def _(i):
        cols = pl.ds(pl.multiple_of(i * step, step), step)
        both = dot(x_all[:, cols], grads, ((0,), (0,))).astype(BF16)
        gate_ref[cols, :] = both[:, :units]
        up_ref[cols, :] = both[:, units:]


def staged(tokens, cotangent, expert_ids, gate_levels, w_gate, w_up, w_down):
    devices = lax.axis_size("expert")
    planes = devices // PLANE
    tok_rows, fanout = expert_ids.shape
    features = tokens.shape[1]
    units = w_gate.shape[2]
    capacity = 3 * tok_rows * fanout // (2 * devices)
    wide = features + LANES
    rows = PLANE * capacity
    me = lax.axis_index("expert").reshape(1)
    ids, levels = expert_ids.T, gate_levels.T
    gate_mat, up_mat, down_mat = w_gate[0], w_up[0], w_down[0]
    run = Chain()

    ring = [*range(0, planes, 2), *range(1, planes, 2)[::-1]]
    follows = dict(zip(ring, ring[1:] + ring[:1]))

    def along(array):
        pairs = [(i, follows[i // PLANE] * PLANE + i % PLANE) for i in range(devices)]
        return lax.ppermute(array, "expert", pairs)

    def across(array):
        return lax.ppermute(array, "expert", [(i, i ^ 2) for i in range(devices)])

    def cores(array):
        return lax.ppermute(array, "expert", [(i, i ^ 1) for i in range(devices)])

    def swap(blocks, pieces):
        own, near, far, diagonal = blocks
        size = -(-capacity // 16 // pieces) * 16
        passing = [cores(diagonal[i : i + size]) for i in range(0, capacity, size)]
        near = cores(near)
        return own, near, far, passing

    def send(own, near, far, passing, wait=True):
        after = run.pending + ([near] if wait else [])
        run.pending = [] if wait else [near]
        if far.shape[1] > features:
            kernel = functools.partial(stack_kernel, features)
            shape = (2 * capacity * features // LANES + devices, LANES)
        else:
            kernel, shape = join_kernel, (2 * capacity, features)
        (both,) = run(
            kernel,
            [(shape, BF16)],
            "join",
            far,
            *passing,
            after=after,
        )
        return [own, near, across(both)]

    def spread(blocks, pieces=1):
        return send(*swap(blocks, pieces), wait=pieces == 1)

    pick, scaled, rows_x, rows_d, grads, hidden, terms = ({} for _ in range(7))

    def slots_x(s, x, pieces=1):
        pick[s], scaled[s], *blocks = run(
            functools.partial(slot_kernel, capacity),
            [((rows, tok_rows), BF16)] * 2 + [((capacity, features), BF16)] * PLANE,
            "slots_x",
            me,
            x,
            smem=1,
        )
        rows_x[s] = spread(blocks, pieces)

    def slots_d(s, d, after=()):
        blocks = run(
            functools.partial(gather_kernel, capacity),
            [((capacity, features), BF16)] * PLANE,
            "slots_d",
            scaled[s],
            d,
            after=after,
        )
        rows_d[s] = spread(blocks)

    def expert(s, after=()):
        grads[s], hidden[s], *terms[s] = run(
            expert_kernel,
            [((rows, 2 * units), BF16), ((rows, units), BF16)]
            + [((capacity, wide), BF16)] * PLANE,
            "expert",
            me,
            *rows_x[s],
            *rows_d[s],
            gate_mat,
            up_mat,
            down_mat,
            smem=1,
            limit=30,
            after=after,
        )

    def home(s, columns, *passed):
        return along(
            run(
                functools.partial(home_kernel, features, columns),
                [
                    (
                        (
                            tok_rows + (devices if columns.stop == features else 0),
                            columns.stop - columns.start,
                        ),
                        BF16,
                    )
                ],
                "home",
                pick[s],
                *terms[s],
                *passed,
            )[0]
        )

    (packed,) = run(
        pack_kernel,
        [((tok_rows * features // LANES + devices, tok_rows), BF16)],
        "pack",
        ids,
        levels,
        tokens,
        hbm=3,
        scratch=[pltpu.VMEM(ids.shape, jnp.int32)] * 2
        + [pltpu.SemaphoreType.DMA((2 + features // LANES,))],
        limit=60,
    )
    x, d = along(packed), along(cotangent)
    slots_x(0, packed, 2)
    slots_d(0, cotangent)
    last = planes - 1
    for s in range(1, planes):
        (here,) = run.hold(x, after=terms[1][1:] if s == last else rows_x[s - 1][2:])
        if s < last:
            x = along(here)
        slots_x(s, here, 2 if s == last else 1)
        if s == 2:
            expert(1)
            terms[1] = spread(terms[1], 2)
            run.pending = []
        if s == last:
            passed = home(1, slice(0, features))
        (here,) = run.hold(d, after=rows_d[s - 1][2:])
        if s == 1:
            d = along(here)
        if s == 2:
            run.pending += rows_x[s][2:]
        slots_d(s, here)
        if s == 1:
            expert(0)
        if s == 2:
            (here,) = run.hold(here)
            d = along(here)
    expert(2)
    terms[2] = send(*swap(run.hold(*terms[2], after=rows_x[last][2:]), 2), wait=False)
    swapped = swap(run.hold(*terms[0], after=[passed]), 2)
    run.pending = [swapped[1], *swapped[3]]
    expert(last)
    terms[last] = spread(terms[last], 2)
    terms[0] = send(*swapped)
    order = range(planes)
    down_delta, _ = run(
        functools.partial(down_kernel, planes),
        [((units, features), BF16), ((8, LANES), F32)],
        "down_delta",
        *[hidden[s] for s in order],
        *[block for s in order for block in rows_d[s]],
        scratch=[pltpu.VMEM((planes * rows, features), BF16)],
    )
    cuts = [0, 896, 1536, features]
    columns = [slice(start, end) for start, end in zip(cuts, cuts[1:])]
    passed = [home(2, part, passed) for part in columns]
    passed = [home(last, part, whole) for whole, part in zip(passed, columns)]
    gate_delta, up_delta, _ = run(
        functools.partial(gate_up_kernel, planes),
        [((features, units), BF16)] * 2 + [((8, LANES), F32)],
        "gate_up_delta",
        *[grads[s] for s in order],
        *[block for s in order for block in rows_x[s]],
        scratch=[pltpu.VMEM((planes * rows, features), BF16)],
    )
    input_grad, router_grad = run(
        total_kernel,
        [((tok_rows, features), BF16), ((fanout, tok_rows), BF16)],
        "total",
        ids,
        levels,
        pick[0],
        *terms[0],
        *passed,
    )
    return input_grad, router_grad.T, gate_delta[None], up_delta[None], down_delta[None]


def solution(mesh):
    devices = mesh.shape["expert"]
    tokens, experts = P(("groups", "expert"), None), P("expert", None, None)
    deltas = P(("groups", "expert"), None, None)

    def on_device(*arrays):
        tok_rows, fanout = arrays[2].shape
        capacity = 3 * tok_rows * fanout // (2 * devices)
        plan = staged if PLANE * capacity > tok_rows and devices % PLANE == 0 else direct
        return plan(*arrays)

    return jax.shard_map(
        on_device,
        mesh=mesh,
        in_specs=(tokens, tokens, tokens, tokens, experts, experts, experts),
        out_specs=(tokens, tokens, deltas, deltas, deltas),
        check_vma=False,
    )
```

```python
import functools

import jax
import jax.numpy as jnp
from jax import lax
from jax.experimental import pallas as pl
from jax.experimental.pallas import tpu as pltpu
from jax.sharding import PartitionSpec as P

BF16 = jnp.bfloat16
F32 = jnp.float32
LANES = 128
PLANE = 4


def project(inputs, gate_mat, up_mat):
    gate_pre = jnp.dot(inputs, gate_mat, preferred_element_type=jnp.float32)
    up_pre = jnp.dot(inputs, up_mat, preferred_element_type=jnp.float32)
    return (gate_pre, up_pre)


def backward(inputs, prepared, cotangent, gating, gate_mat, up_mat, down_mat):
    gate_pre, up_pre = prepared
    sigmoid_gate = jax.nn.sigmoid(gate_pre)
    hidden = (gate_pre * sigmoid_gate * up_pre).astype(jnp.bfloat16)
    back_grad = lax.dot_general(
        cotangent, down_mat, (((1,), (1,)), ((), ())), preferred_element_type=jnp.float32
    )
    router_term = jnp.sum(hidden.astype(jnp.float32) * back_grad, axis=1).astype(jnp.bfloat16)
    hidden_grad = gating[:, None] * back_grad
    gate_grad = (
        hidden_grad * up_pre * sigmoid_gate * (1.0 + gate_pre * (1.0 - sigmoid_gate))
    ).astype(jnp.bfloat16)
    up_grad = (hidden_grad * gate_pre * sigmoid_gate).astype(jnp.bfloat16)
    input_term = lax.dot_general(
        gate_grad, gate_mat, (((1,), (1,)), ((), ())), preferred_element_type=jnp.float32
    )
    input_term = input_term + lax.dot_general(
        up_grad, up_mat, (((1,), (1,)), ((), ())), preferred_element_type=jnp.float32
    )
    input_term = input_term.astype(jnp.bfloat16)
    scaled = (gating[:, None] * cotangent.astype(jnp.float32)).astype(jnp.bfloat16)
    down_delta = lax.dot_general(
        hidden, scaled, (((0,), (0,)), ((), ())), preferred_element_type=jnp.float32
    )
    gate_delta = lax.dot_general(
        inputs, gate_grad, (((0,), (0,)), ((), ())), preferred_element_type=jnp.float32
    )
    up_delta = lax.dot_general(
        inputs, up_grad, (((0,), (0,)), ((), ())), preferred_element_type=jnp.float32
    )
    return (input_term, router_term, gate_delta, up_delta, down_delta)


def direct(tokens, cotangent, expert_ids, gate_levels, w_gate, w_up, w_down):
    devices = lax.axis_size("expert")
    tok_rows, fanout = expert_ids.shape
    features = tokens.shape[1]
    capacity = 3 * tok_rows * fanout // (2 * devices)
    slot_rows = devices * capacity
    gate_mat = w_gate[0]
    up_mat = w_up[0]
    down_mat = w_down[0]
    chosen = expert_ids.reshape(-1)
    indicator = (chosen[:, None] == jnp.arange(devices, dtype=jnp.int32)[None, :]).astype(jnp.int32)
    earlier = jnp.cumsum(indicator, axis=0) - indicator
    position = jnp.sum(earlier * indicator, axis=1)
    target = chosen * capacity + position
    gating_local = (gate_levels.reshape(-1).astype(jnp.float32) / 256.0).astype(jnp.bfloat16)
    outbox_x = (
        jnp.zeros((slot_rows, features), jnp.bfloat16)
        .at[target]
        .set(jnp.repeat(tokens, fanout, axis=0))
    )
    outbox_dy = (
        jnp.zeros((slot_rows, features), jnp.bfloat16)
        .at[target]
        .set(jnp.repeat(cotangent, fanout, axis=0))
    )
    outbox_g = jnp.zeros((slot_rows,), jnp.bfloat16).at[target].set(gating_local)
    outbox_x = outbox_x.reshape(devices, capacity, features)
    outbox_dy = outbox_dy.reshape(devices, capacity, features)
    outbox_g = outbox_g.reshape(devices, capacity)
    exchange = functools.partial(
        lax.all_to_all, axis_name="expert", split_axis=0, concat_axis=0, tiled=True
    )
    rows_x = exchange(outbox_x).reshape(slot_rows, features)
    rows_dy = exchange(outbox_dy).reshape(slot_rows, features)
    rows_g = exchange(outbox_g).reshape(-1).astype(jnp.float32)
    prepared = project(rows_x, gate_mat, up_mat)
    input_term, router_term, gate_delta, up_delta, down_delta = backward(
        rows_x, prepared, rows_dy, rows_g, gate_mat, up_mat, down_mat
    )
    back_term = exchange(input_term.reshape(devices, capacity, features))
    back_router = exchange(router_term.reshape(devices, capacity))
    gathered_term = back_term.reshape(slot_rows, features)[target].astype(jnp.float32)
    input_grad = jnp.sum(gathered_term.reshape(tok_rows, fanout, features), axis=1).astype(
        jnp.bfloat16
    )
    router_grad = back_router.reshape(-1)[target].reshape(tok_rows, fanout)
    return (
        input_grad,
        router_grad,
        gate_delta.astype(jnp.bfloat16)[None],
        up_delta.astype(jnp.bfloat16)[None],
        down_delta.astype(jnp.bfloat16)[None],
    )


def dot(a, b, contract=((1,), (0,))):
    return lax.dot_general(a, b, (contract, ((), ())), preferred_element_type=F32)


class Chain:
    def __init__(self):
        self.last = []
        self.pending = []

    def __call__(self, kernel, outs, name, *operands, after=(), scratch=(), smem=0, hbm=0, limit=16):
        vmem = pl.BlockSpec(memory_space=pltpu.VMEM)
        scalar = pl.BlockSpec(memory_space=pltpu.SMEM)
        anywhere = pl.BlockSpec(memory_space=pl.ANY)
        outside = pl.BlockSpec(memory_space=pltpu.HBM)
        unused = [*self.last, *after]
        fixed = len(operands)

        def body(*refs):
            kernel(*refs[:fixed], *refs[fixed + len(unused) :])

        made = pl.pallas_call(
            body,
            out_shape=[jax.ShapeDtypeStruct(shape, kind) for shape, kind in outs],
            in_specs=[scalar] * smem
            + [outside] * hbm
            + [vmem] * (fixed - smem - hbm)
            + [anywhere] * len(unused),
            out_specs=[vmem] * len(outs),
            scratch_shapes=list(scratch),
            name=name,
            compiler_params=pltpu.CompilerParams(vmem_limit_bytes=limit << 20),
            cost_estimate=pl.CostEstimate(flops=1000, bytes_accessed=1000, transcendentals=0),
        )(*operands, *unused)
        self.last = [min(made, key=lambda array: array.size)]
        return made

    def hold(self, *arrays, after=()):
        unused = [*self.last, *self.pending, *after]
        self.pending = []
        anywhere = pl.BlockSpec(memory_space=pl.ANY)
        held = pl.pallas_call(
            lambda *refs: None,
            out_shape=[jax.ShapeDtypeStruct(array.shape, array.dtype) for array in arrays],
            in_specs=[anywhere] * (len(arrays) + len(unused)),
            out_specs=[anywhere] * len(arrays),
            input_output_aliases={i: i for i in range(len(arrays))},
            name="hold",
            compiler_params=pltpu.CompilerParams(vmem_limit_bytes=1 << 20),
            cost_estimate=pl.CostEstimate(flops=1000, bytes_accessed=1000, transcendentals=0),
        )(*arrays, *unused)
        self.last = held[:1]
        return held


def joined(refs):
    return jnp.concatenate([ref[...] for ref in refs], axis=0)


def unstacked(ref, rows, start, stop):
    blocks = range(start // LANES, stop // LANES)
    return jnp.concatenate([ref[rows * i : rows * (i + 1), :] for i in blocks], axis=1)


def pack_kernel(ids_ref, levels_ref, x_ref, out_ref, ids_here, levels_here, sems):
    fanout, rows = ids_ref.shape
    features = x_ref.shape[1]
    experts = out_ref.shape[0] - rows * features // LANES
    moves = [(ids_ref, ids_here), (levels_ref, levels_here)]
    for i in range(features // LANES):
        source = x_ref.at[:, LANES * i : LANES * (i + 1)]
        moves.append((source, out_ref.at[rows * i : rows * (i + 1), :]))
    copies = [
        pltpu.make_async_copy(source, target, sems.at[i])
        for i, (source, target) in enumerate(moves)
    ]
    for copy in copies:
        copy.start()
    for copy in copies[:2]:
        copy.wait()
    expert = lax.broadcasted_iota(jnp.int32, (experts, rows), 0)
    gates = jnp.zeros((experts, rows), F32)
    for k in range(fanout):
        value = levels_here[k : k + 1, :].astype(F32) * (1.0 / 256.0)
        gates = gates + jnp.where(ids_here[k : k + 1, :] == expert, value, 0.0)
    out_ref[out_ref.shape[0] - experts :, :] = gates.astype(BF16)
    for copy in copies[2:]:
        copy.wait()


def slot_kernel(capacity, me_ref, x_ref, pick_ref, scaled_ref, *block_refs):
    features = block_refs[0].shape[1]
    rows = pick_ref.shape[1]
    table = x_ref[rows * features // LANES :, :]
    experts = table.shape[0]
    expert = lax.broadcasted_iota(jnp.int32, (8, experts), 1)
    wanted = jnp.bitwise_xor(lax.broadcasted_iota(jnp.int32, (8, experts), 0), me_ref[0])
    chooser = jnp.where(expert == wanted, 1.0, 0.0).astype(BF16)
    gates = dot(chooser, table)
    routed = jnp.where(gates > 0.0, 1.0, 0.0)
    before = lax.broadcasted_iota(jnp.int32, (rows, rows), 0)
    after = lax.broadcasted_iota(jnp.int32, (rows, rows), 1)
    earlier = jnp.where(before < after, 1.0, 0.0).astype(BF16)
    place = dot(routed.astype(BF16), earlier)
    place = jnp.where(routed > 0.0, place, -1.0)
    slot = lax.broadcasted_iota(jnp.int32, (capacity, rows), 0).astype(F32)
    chosen = [place[i : i + 1, :] == slot for i in range(PLANE)]
    pick = jnp.concatenate([jnp.where(here, 1.0, 0.0) for here in chosen], axis=0).astype(BF16)
    pick_ref[...] = pick
    scaled_ref[...] = jnp.concatenate(
        [jnp.where(here, gates[i : i + 1, :], 0.0) for i, here in enumerate(chosen)], axis=0
    ).astype(BF16)
    picked = dot(pick, unstacked(x_ref, rows, 0, features)).astype(BF16)
    for i, block_ref in enumerate(block_refs):
        block_ref[...] = picked[capacity * i : capacity * (i + 1), :]


def gather_kernel(capacity, scaled_ref, d_ref, *block_refs):
    picked = dot(scaled_ref[...], d_ref[...]).astype(BF16)
    for i, block_ref in enumerate(block_refs):
        block_ref[...] = picked[capacity * i : capacity * (i + 1), :]


def join_kernel(*refs):
    refs[-1][...] = joined(refs[:-1])


def stack_kernel(features, *refs):
    *block_refs, out_ref = refs
    rows = sum(ref.shape[0] for ref in block_refs)
    for i in range(features // LANES):
        blocks = [ref[:, LANES * i : LANES * (i + 1)] for ref in block_refs]
        out_ref[rows * i : rows * (i + 1), :] = jnp.concatenate(blocks, axis=0)
    lanes = jnp.concatenate([ref[:, features:] for ref in block_refs], axis=0).astype(F32)
    blank = jnp.zeros((LANES - rows, LANES), F32)
    experts = out_ref.shape[0] - rows * features // LANES
    router = jnp.concatenate([lanes, blank], axis=0).T[:experts, :]
    out_ref[rows * features // LANES :, :] = router.astype(BF16)


def expert_kernel(me_ref, *refs):
    x_refs, d_refs, (gate_ref, up_ref, down_ref) = refs[:3], refs[3:6], refs[6:9]
    grads_ref, hidden_ref, *term_refs = refs[9:]
    features, units = gate_ref.shape
    x, d = joined(x_refs), joined(d_refs)
    rows = x.shape[0]
    gate_pre = dot(x, gate_ref[...])
    up_pre = dot(x, up_ref[...])
    hidden_grad = dot(d, down_ref[...], ((1,), (1,)))
    sigmoid_gate = jax.nn.sigmoid(gate_pre)
    silu = gate_pre * sigmoid_gate
    hidden = (silu * up_pre).astype(BF16)
    router = jnp.sum(hidden.astype(F32) * hidden_grad, axis=1, keepdims=True)
    gate_grad = hidden_grad * up_pre * sigmoid_gate * (1.0 + gate_pre * (1.0 - sigmoid_gate))
    gate_grad = gate_grad.astype(BF16)
    up_grad = (hidden_grad * silu).astype(BF16)
    grads_ref[:, :units] = gate_grad
    grads_ref[:, units:] = up_grad
    hidden_ref[...] = hidden
    term = dot(gate_grad, gate_ref[...], ((1,), (1,))) + dot(up_grad, up_ref[...], ((1,), (1,)))
    term = term.astype(BF16)
    mine = lax.broadcasted_iota(jnp.int32, (rows, LANES), 1) == me_ref[0]
    router = jnp.where(mine, router, 0.0).astype(BF16)
    count = rows // len(term_refs)
    for i, term_ref in enumerate(term_refs):
        part = slice(count * i, count * (i + 1))
        term_ref[:, :features] = term[part, :]
        term_ref[:, features:] = router[part, :]


def plane_sum(pick_ref, term_refs, features, columns, experts):
    own_ref, near_ref, far_ref = term_refs
    half = pick_ref.shape[0] // 2
    terms = jnp.concatenate(
        [
            own_ref[:, columns],
            near_ref[:, columns],
            unstacked(far_ref, half, columns.start, columns.stop),
        ],
        axis=0,
    )
    total = dot(pick_ref[...], terms, ((0,), (0,)))
    if not experts:
        return total, None
    lanes = jnp.concatenate([own_ref[:, features:], near_ref[:, features:]], axis=0)
    router = dot(lanes, pick_ref[:half, :], ((0,), (0,)))[:experts, :]
    router = router + dot(far_ref[half * features // LANES :, :half], pick_ref[half:, :])
    return total, router


def home_kernel(features, columns, pick_ref, *refs):
    *refs, out_ref = refs
    rows = pick_ref.shape[1]
    experts = out_ref.shape[0] - rows
    total, router = plane_sum(pick_ref, refs[:3], features, columns, experts)
    for passed_ref in refs[3:]:
        passed = passed_ref[:rows, :]
        if passed.shape[1] > total.shape[1]:
            passed = passed[:, columns]
        total = total + passed.astype(F32)
        if experts:
            router = router + passed_ref[rows:, :LANES].astype(F32)
    out_ref[:rows, :] = total.astype(BF16)
    if experts:
        rest = jnp.zeros((experts, out_ref.shape[1] - rows), F32)
        out_ref[rows:, :] = jnp.concatenate([router, rest], axis=1).astype(BF16)


def total_kernel(ids_ref, levels_ref, pick_ref, *refs):
    term_refs, passed_refs, (grad_ref, router_ref) = refs[:3], refs[3:-2], refs[-2:]
    fanout, rows = ids_ref.shape
    features = grad_ref.shape[1]
    experts = passed_refs[-1].shape[0] - rows
    passed = jnp.concatenate([ref[:rows, :] for ref in passed_refs], axis=1)
    total, router = plane_sum(pick_ref, term_refs, features, slice(0, features), experts)
    grad_ref[...] = (total + passed.astype(F32)).astype(BF16)
    router = router + passed_refs[-1][rows:, :LANES].astype(F32)
    expert = lax.broadcasted_iota(jnp.int32, (experts, rows), 0)
    for k in range(fanout):
        own = jnp.where(ids_ref[k : k + 1, :] == expert, router, 0.0)
        own = jnp.sum(own, axis=0, keepdims=True)
        own = own * (256.0 / levels_ref[k : k + 1, :].astype(F32))
        router_ref[k : k + 1, :] = own.astype(BF16)


def stacked(refs, whole_ref):
    start = 0
    for ref in refs:
        whole_ref[start : start + ref.shape[0], :] = ref[...]
        start += ref.shape[0]


def down_kernel(chunks, *refs):
    *d_refs, down_ref, done_ref, d_all = refs
    hidden_refs, d_refs = d_refs[:chunks], d_refs[chunks:]
    done_ref[...] = jnp.zeros_like(done_ref)
    stacked(d_refs, d_all)
    hidden = joined(hidden_refs)
    step = 512

    @pl.loop(0, down_ref.shape[1] // step)
    def _(i):
        cols = pl.ds(pl.multiple_of(i * step, step), step)
        down_ref[:, cols] = dot(hidden, d_all[:, cols], ((0,), (0,))).astype(BF16)


def gate_up_kernel(chunks, *refs):
    *x_refs, gate_ref, up_ref, done_ref, x_all = refs
    grads_refs, x_refs = x_refs[:chunks], x_refs[chunks:]
    done_ref[...] = jnp.zeros_like(done_ref)
    stacked(x_refs, x_all)
    grads = joined(grads_refs)
    features, units = gate_ref.shape
    step = 512

    @pl.loop(0, features // step)
    def _(i):
        cols = pl.ds(pl.multiple_of(i * step, step), step)
        both = dot(x_all[:, cols], grads, ((0,), (0,))).astype(BF16)
        gate_ref[cols, :] = both[:, :units]
        up_ref[cols, :] = both[:, units:]


def staged(tokens, cotangent, expert_ids, gate_levels, w_gate, w_up, w_down):
    devices = lax.axis_size("expert")
    planes = devices // PLANE
    tok_rows, fanout = expert_ids.shape
    features = tokens.shape[1]
    units = w_gate.shape[2]
    capacity = 3 * tok_rows * fanout // (2 * devices)
    wide = features + LANES
    rows = PLANE * capacity
    me = lax.axis_index("expert").reshape(1)
    ids, levels = expert_ids.T, gate_levels.T
    gate_mat, up_mat, down_mat = w_gate[0], w_up[0], w_down[0]
    run = Chain()

    ring = [*range(0, planes, 2), *range(1, planes, 2)[::-1]]
    follows = dict(zip(ring, ring[1:] + ring[:1]))

    def along(array):
        pairs = [(i, follows[i // PLANE] * PLANE + i % PLANE) for i in range(devices)]
        return lax.ppermute(array, "expert", pairs)

    def across(array):
        return lax.ppermute(array, "expert", [(i, i ^ 2) for i in range(devices)])

    def cores(array):
        return lax.ppermute(array, "expert", [(i, i ^ 1) for i in range(devices)])

    def swap(blocks, pieces):
        own, near, far, diagonal = blocks
        size = -(-capacity // 16 // pieces) * 16
        passing = [cores(diagonal[i : i + size]) for i in range(0, capacity, size)]
        near = cores(near)
        return own, near, far, passing

    def send(own, near, far, passing, wait=True):
        after = run.pending + ([near] if wait else [])
        run.pending = [] if wait else [near]
        if far.shape[1] > features:
            kernel = functools.partial(stack_kernel, features)
            shape = (2 * capacity * features // LANES + devices, LANES)
        else:
            kernel, shape = join_kernel, (2 * capacity, features)
        (both,) = run(
            kernel,
            [(shape, BF16)],
            "join",
            far,
            *passing,
            after=after,
        )
        return [own, near, across(both)]

    def spread(blocks, pieces=1):
        return send(*swap(blocks, pieces), wait=pieces == 1)

    pick, scaled, rows_x, rows_d, grads, hidden, terms = ({} for _ in range(7))

    def slots_x(s, x, pieces=1):
        pick[s], scaled[s], *blocks = run(
            functools.partial(slot_kernel, capacity),
            [((rows, tok_rows), BF16)] * 2 + [((capacity, features), BF16)] * PLANE,
            "slots_x",
            me,
            x,
            smem=1,
        )
        rows_x[s] = spread(blocks, pieces)

    def slots_d(s, d, after=()):
        blocks = run(
            functools.partial(gather_kernel, capacity),
            [((capacity, features), BF16)] * PLANE,
            "slots_d",
            scaled[s],
            d,
            after=after,
        )
        rows_d[s] = spread(blocks)

    def expert(s, after=()):
        grads[s], hidden[s], *terms[s] = run(
            expert_kernel,
            [((rows, 2 * units), BF16), ((rows, units), BF16)]
            + [((capacity, wide), BF16)] * PLANE,
            "expert",
            me,
            *rows_x[s],
            *rows_d[s],
            gate_mat,
            up_mat,
            down_mat,
            smem=1,
            limit=30,
            after=after,
        )

    def home(s, columns, *passed):
        return along(
            run(
                functools.partial(home_kernel, features, columns),
                [
                    (
                        (
                            tok_rows + (devices if columns.stop == features else 0),
                            columns.stop - columns.start,
                        ),
                        BF16,
                    )
                ],
                "home",
                pick[s],
                *terms[s],
                *passed,
            )[0]
        )

    (packed,) = run(
        pack_kernel,
        [((tok_rows * features // LANES + devices, tok_rows), BF16)],
        "pack",
        ids,
        levels,
        tokens,
        hbm=3,
        scratch=[pltpu.VMEM(ids.shape, jnp.int32)] * 2
        + [pltpu.SemaphoreType.DMA((2 + features // LANES,))],
        limit=60,
    )
    x, d = along(packed), along(cotangent)
    slots_x(0, packed, 2)
    slots_d(0, cotangent)
    last = planes - 1
    for s in range(1, planes):
        (here,) = run.hold(x, after=terms[1][1:] if s == last else rows_x[s - 1][2:])
        if s < last:
            x = along(here)
        slots_x(s, here, 2 if s == last else 1)
        if s == 2:
            expert(1)
            terms[1] = spread(terms[1], 2)
            run.pending = []
        if s == last:
            passed = home(1, slice(0, features))
        (here,) = run.hold(d, after=rows_d[s - 1][2:])
        if s == 1:
            d = along(here)
        if s == 2:
            run.pending += rows_x[s][2:]
        slots_d(s, here)
        if s == 1:
            expert(0)
        if s == 2:
            (here,) = run.hold(here)
            d = along(here)
    expert(2)
    terms[2] = send(*swap(run.hold(*terms[2], after=rows_x[last][2:]), 2), wait=False)
    swapped = swap(run.hold(*terms[0], after=[passed]), 2)
    run.pending = [swapped[1], *swapped[3]]
    expert(last)
    terms[last] = spread(terms[last], 2)
    terms[0] = send(*swapped)
    order = range(planes)
    cuts = [0, 896, 1536, features]
    columns = [slice(start, end) for start, end in zip(cuts, cuts[1:])]
    passed = [home(2, part, passed) for part in columns]
    down_delta, _ = run(
        functools.partial(down_kernel, planes),
        [((units, features), BF16), ((8, LANES), F32)],
        "down_delta",
        *[hidden[s] for s in order],
        *[block for s in order for block in rows_d[s]],
        scratch=[pltpu.VMEM((planes * rows, features), BF16)],
    )
    passed = [home(last, part, whole) for whole, part in zip(passed, columns)]
    gate_delta, up_delta, _ = run(
        functools.partial(gate_up_kernel, planes),
        [((features, units), BF16)] * 2 + [((8, LANES), F32)],
        "gate_up_delta",
        *[grads[s] for s in order],
        *[block for s in order for block in rows_x[s]],
        scratch=[pltpu.VMEM((planes * rows, features), BF16)],
    )
    input_grad, router_grad = run(
        total_kernel,
        [((tok_rows, features), BF16), ((fanout, tok_rows), BF16)],
        "total",
        ids,
        levels,
        pick[0],
        *terms[0],
        *passed,
    )
    return input_grad, router_grad.T, gate_delta[None], up_delta[None], down_delta[None]


def solution(mesh):
    devices = mesh.shape["expert"]
    tokens, experts = P(("groups", "expert"), None), P("expert", None, None)
    deltas = P(("groups", "expert"), None, None)

    def on_device(*arrays):
        tok_rows, fanout = arrays[2].shape
        capacity = 3 * tok_rows * fanout // (2 * devices)
        plan = staged if PLANE * capacity > tok_rows and devices % PLANE == 0 else direct
        return plan(*arrays)

    return jax.shard_map(
        on_device,
        mesh=mesh,
        in_specs=(tokens, tokens, tokens, tokens, experts, experts, experts),
        out_specs=(tokens, tokens, deltas, deltas, deltas),
        check_vma=False,
    )
```

```python
import functools

import jax
import jax.numpy as jnp
from jax import lax
from jax.experimental import pallas as pl
from jax.experimental.pallas import tpu as pltpu
from jax.sharding import PartitionSpec as P

BF16 = jnp.bfloat16
F32 = jnp.float32
LANES = 128
PLANE = 4


def project(inputs, gate_mat, up_mat):
    gate_pre = jnp.dot(inputs, gate_mat, preferred_element_type=jnp.float32)
    up_pre = jnp.dot(inputs, up_mat, preferred_element_type=jnp.float32)
    return (gate_pre, up_pre)


def backward(inputs, prepared, cotangent, gating, gate_mat, up_mat, down_mat):
    gate_pre, up_pre = prepared
    sigmoid_gate = jax.nn.sigmoid(gate_pre)
    hidden = (gate_pre * sigmoid_gate * up_pre).astype(jnp.bfloat16)
    back_grad = lax.dot_general(
        cotangent, down_mat, (((1,), (1,)), ((), ())), preferred_element_type=jnp.float32
    )
    router_term = jnp.sum(hidden.astype(jnp.float32) * back_grad, axis=1).astype(jnp.bfloat16)
    hidden_grad = gating[:, None] * back_grad
    gate_grad = (
        hidden_grad * up_pre * sigmoid_gate * (1.0 + gate_pre * (1.0 - sigmoid_gate))
    ).astype(jnp.bfloat16)
    up_grad = (hidden_grad * gate_pre * sigmoid_gate).astype(jnp.bfloat16)
    input_term = lax.dot_general(
        gate_grad, gate_mat, (((1,), (1,)), ((), ())), preferred_element_type=jnp.float32
    )
    input_term = input_term + lax.dot_general(
        up_grad, up_mat, (((1,), (1,)), ((), ())), preferred_element_type=jnp.float32
    )
    input_term = input_term.astype(jnp.bfloat16)
    scaled = (gating[:, None] * cotangent.astype(jnp.float32)).astype(jnp.bfloat16)
    down_delta = lax.dot_general(
        hidden, scaled, (((0,), (0,)), ((), ())), preferred_element_type=jnp.float32
    )
    gate_delta = lax.dot_general(
        inputs, gate_grad, (((0,), (0,)), ((), ())), preferred_element_type=jnp.float32
    )
    up_delta = lax.dot_general(
        inputs, up_grad, (((0,), (0,)), ((), ())), preferred_element_type=jnp.float32
    )
    return (input_term, router_term, gate_delta, up_delta, down_delta)


def direct(tokens, cotangent, expert_ids, gate_levels, w_gate, w_up, w_down):
    devices = lax.axis_size("expert")
    tok_rows, fanout = expert_ids.shape
    features = tokens.shape[1]
    capacity = 3 * tok_rows * fanout // (2 * devices)
    slot_rows = devices * capacity
    gate_mat = w_gate[0]
    up_mat = w_up[0]
    down_mat = w_down[0]
    chosen = expert_ids.reshape(-1)
    indicator = (chosen[:, None] == jnp.arange(devices, dtype=jnp.int32)[None, :]).astype(jnp.int32)
    earlier = jnp.cumsum(indicator, axis=0) - indicator
    position = jnp.sum(earlier * indicator, axis=1)
    target = chosen * capacity + position
    gating_local = (gate_levels.reshape(-1).astype(jnp.float32) / 256.0).astype(jnp.bfloat16)
    outbox_x = (
        jnp.zeros((slot_rows, features), jnp.bfloat16)
        .at[target]
        .set(jnp.repeat(tokens, fanout, axis=0))
    )
    outbox_dy = (
        jnp.zeros((slot_rows, features), jnp.bfloat16)
        .at[target]
        .set(jnp.repeat(cotangent, fanout, axis=0))
    )
    outbox_g = jnp.zeros((slot_rows,), jnp.bfloat16).at[target].set(gating_local)
    outbox_x = outbox_x.reshape(devices, capacity, features)
    outbox_dy = outbox_dy.reshape(devices, capacity, features)
    outbox_g = outbox_g.reshape(devices, capacity)
    exchange = functools.partial(
        lax.all_to_all, axis_name="expert", split_axis=0, concat_axis=0, tiled=True
    )
    rows_x = exchange(outbox_x).reshape(slot_rows, features)
    rows_dy = exchange(outbox_dy).reshape(slot_rows, features)
    rows_g = exchange(outbox_g).reshape(-1).astype(jnp.float32)
    prepared = project(rows_x, gate_mat, up_mat)
    input_term, router_term, gate_delta, up_delta, down_delta = backward(
        rows_x, prepared, rows_dy, rows_g, gate_mat, up_mat, down_mat
    )
    back_term = exchange(input_term.reshape(devices, capacity, features))
    back_router = exchange(router_term.reshape(devices, capacity))
    gathered_term = back_term.reshape(slot_rows, features)[target].astype(jnp.float32)
    input_grad = jnp.sum(gathered_term.reshape(tok_rows, fanout, features), axis=1).astype(
        jnp.bfloat16
    )
    router_grad = back_router.reshape(-1)[target].reshape(tok_rows, fanout)
    return (
        input_grad,
        router_grad,
        gate_delta.astype(jnp.bfloat16)[None],
        up_delta.astype(jnp.bfloat16)[None],
        down_delta.astype(jnp.bfloat16)[None],
    )


def dot(a, b, contract=((1,), (0,))):
    return lax.dot_general(a, b, (contract, ((), ())), preferred_element_type=F32)


class Chain:
    def __init__(self):
        self.last = []
        self.pending = []

    def __call__(self, kernel, outs, name, *operands, after=(), scratch=(), smem=0, hbm=0, hbm_out=(), limit=16):
        vmem = pl.BlockSpec(memory_space=pltpu.VMEM)
        scalar = pl.BlockSpec(memory_space=pltpu.SMEM)
        anywhere = pl.BlockSpec(memory_space=pl.ANY)
        outside = pl.BlockSpec(memory_space=pltpu.HBM)
        unused = [*self.last, *after]
        fixed = len(operands)

        def body(*refs):
            kernel(*refs[:fixed], *refs[fixed + len(unused) :])

        made = pl.pallas_call(
            body,
            out_shape=[jax.ShapeDtypeStruct(shape, kind) for shape, kind in outs],
            in_specs=[scalar] * smem
            + [outside] * hbm
            + [vmem] * (fixed - smem - hbm)
            + [anywhere] * len(unused),
            out_specs=[outside if i in hbm_out else vmem for i in range(len(outs))],
            scratch_shapes=list(scratch),
            name=name,
            compiler_params=pltpu.CompilerParams(vmem_limit_bytes=limit << 20),
            cost_estimate=pl.CostEstimate(flops=1000, bytes_accessed=1000, transcendentals=0),
        )(*operands, *unused)
        self.last = [min(made, key=lambda array: array.size)]
        return made

    def hold(self, *arrays, after=()):
        unused = [*self.last, *self.pending, *after]
        self.pending = []
        anywhere = pl.BlockSpec(memory_space=pl.ANY)
        held = pl.pallas_call(
            lambda *refs: None,
            out_shape=[jax.ShapeDtypeStruct(array.shape, array.dtype) for array in arrays],
            in_specs=[anywhere] * (len(arrays) + len(unused)),
            out_specs=[anywhere] * len(arrays),
            input_output_aliases={i: i for i in range(len(arrays))},
            name="hold",
            compiler_params=pltpu.CompilerParams(vmem_limit_bytes=1 << 20),
            cost_estimate=pl.CostEstimate(flops=1000, bytes_accessed=1000, transcendentals=0),
        )(*arrays, *unused)
        self.last = held[:1]
        return held


def joined(refs):
    return jnp.concatenate([ref[...] for ref in refs], axis=0)


def unstacked(ref, rows, start, stop):
    blocks = range(start // LANES, stop // LANES)
    return jnp.concatenate([ref[rows * i : rows * (i + 1), :] for i in blocks], axis=1)


def pack_kernel(ids_ref, levels_ref, x_ref, out_ref, ids_here, levels_here, sems):
    fanout, rows = ids_ref.shape
    features = x_ref.shape[1]
    experts = out_ref.shape[0] - rows * features // LANES
    moves = [(ids_ref, ids_here), (levels_ref, levels_here)]
    for i in range(features // LANES):
        source = x_ref.at[:, LANES * i : LANES * (i + 1)]
        moves.append((source, out_ref.at[rows * i : rows * (i + 1), :]))
    copies = [
        pltpu.make_async_copy(source, target, sems.at[i])
        for i, (source, target) in enumerate(moves)
    ]
    for copy in copies:
        copy.start()
    for copy in copies[:2]:
        copy.wait()
    expert = lax.broadcasted_iota(jnp.int32, (experts, rows), 0)
    gates = jnp.zeros((experts, rows), F32)
    for k in range(fanout):
        value = levels_here[k : k + 1, :].astype(F32) * (1.0 / 256.0)
        gates = gates + jnp.where(ids_here[k : k + 1, :] == expert, value, 0.0)
    out_ref[out_ref.shape[0] - experts :, :] = gates.astype(BF16)
    for copy in copies[2:]:
        copy.wait()


def slot_kernel(capacity, me_ref, x_ref, pick_ref, scaled_ref, *block_refs):
    features = block_refs[0].shape[1]
    rows = pick_ref.shape[1]
    table = x_ref[rows * features // LANES :, :]
    experts = table.shape[0]
    expert = lax.broadcasted_iota(jnp.int32, (8, experts), 1)
    wanted = jnp.bitwise_xor(lax.broadcasted_iota(jnp.int32, (8, experts), 0), me_ref[0])
    chooser = jnp.where(expert == wanted, 1.0, 0.0).astype(BF16)
    gates = dot(chooser, table)
    routed = jnp.where(gates > 0.0, 1.0, 0.0)
    before = lax.broadcasted_iota(jnp.int32, (rows, rows), 0)
    after = lax.broadcasted_iota(jnp.int32, (rows, rows), 1)
    earlier = jnp.where(before < after, 1.0, 0.0).astype(BF16)
    place = dot(routed.astype(BF16), earlier)
    place = jnp.where(routed > 0.0, place, -1.0)
    slot = lax.broadcasted_iota(jnp.int32, (capacity, rows), 0).astype(F32)
    chosen = [place[i : i + 1, :] == slot for i in range(PLANE)]
    pick = jnp.concatenate([jnp.where(here, 1.0, 0.0) for here in chosen], axis=0).astype(BF16)
    pick_ref[...] = pick
    scaled_ref[...] = jnp.concatenate(
        [jnp.where(here, gates[i : i + 1, :], 0.0) for i, here in enumerate(chosen)], axis=0
    ).astype(BF16)
    picked = dot(pick, unstacked(x_ref, rows, 0, features)).astype(BF16)
    for i, block_ref in enumerate(block_refs):
        block_ref[...] = picked[capacity * i : capacity * (i + 1), :]


def gather_kernel(capacity, scaled_ref, d_ref, *block_refs):
    picked = dot(scaled_ref[...], d_ref[...]).astype(BF16)
    for i, block_ref in enumerate(block_refs):
        block_ref[...] = picked[capacity * i : capacity * (i + 1), :]


def join_kernel(*refs):
    refs[-1][...] = joined(refs[:-1])


def stack_kernel(features, *refs):
    *block_refs, out_ref = refs
    rows = sum(ref.shape[0] for ref in block_refs)
    for i in range(features // LANES):
        blocks = [ref[:, LANES * i : LANES * (i + 1)] for ref in block_refs]
        out_ref[rows * i : rows * (i + 1), :] = jnp.concatenate(blocks, axis=0)
    lanes = jnp.concatenate([ref[:, features:] for ref in block_refs], axis=0).astype(F32)
    blank = jnp.zeros((LANES - rows, LANES), F32)
    experts = out_ref.shape[0] - rows * features // LANES
    router = jnp.concatenate([lanes, blank], axis=0).T[:experts, :]
    out_ref[rows * features // LANES :, :] = router.astype(BF16)


def expert_kernel(me_ref, *refs):
    x_refs, d_refs, (gate_ref, up_ref, down_ref) = refs[:3], refs[3:6], refs[6:9]
    grads_ref, hidden_ref, *term_refs = refs[9:]
    features, units = gate_ref.shape
    x, d = joined(x_refs), joined(d_refs)
    rows = x.shape[0]
    gate_pre = dot(x, gate_ref[...])
    up_pre = dot(x, up_ref[...])
    hidden_grad = dot(d, down_ref[...], ((1,), (1,)))
    sigmoid_gate = jax.nn.sigmoid(gate_pre)
    silu = gate_pre * sigmoid_gate
    hidden = (silu * up_pre).astype(BF16)
    router = jnp.sum(hidden.astype(F32) * hidden_grad, axis=1, keepdims=True)
    gate_grad = hidden_grad * up_pre * sigmoid_gate * (1.0 + gate_pre * (1.0 - sigmoid_gate))
    gate_grad = gate_grad.astype(BF16)
    up_grad = (hidden_grad * silu).astype(BF16)
    grads_ref[:, :units] = gate_grad
    grads_ref[:, units:] = up_grad
    hidden_ref[...] = hidden
    term = dot(gate_grad, gate_ref[...], ((1,), (1,))) + dot(up_grad, up_ref[...], ((1,), (1,)))
    term = term.astype(BF16)
    mine = lax.broadcasted_iota(jnp.int32, (rows, LANES), 1) == me_ref[0]
    router = jnp.where(mine, router, 0.0).astype(BF16)
    count = rows // len(term_refs)
    for i, term_ref in enumerate(term_refs):
        part = slice(count * i, count * (i + 1))
        term_ref[:, :features] = term[part, :]
        term_ref[:, features:] = router[part, :]


def plane_sum(pick_ref, term_refs, features, columns, experts):
    own_ref, near_ref, far_ref = term_refs
    half = pick_ref.shape[0] // 2
    terms = jnp.concatenate(
        [
            own_ref[:, columns],
            near_ref[:, columns],
            unstacked(far_ref, half, columns.start, columns.stop),
        ],
        axis=0,
    )
    total = dot(pick_ref[...], terms, ((0,), (0,)))
    if not experts:
        return total, None
    lanes = jnp.concatenate([own_ref[:, features:], near_ref[:, features:]], axis=0)
    router = dot(lanes, pick_ref[:half, :], ((0,), (0,)))[:experts, :]
    router = router + dot(far_ref[half * features // LANES :, :half], pick_ref[half:, :])
    return total, router


def home_kernel(features, columns, pick_ref, *refs):
    *refs, out_ref = refs
    rows = pick_ref.shape[1]
    experts = out_ref.shape[0] - rows
    total, router = plane_sum(pick_ref, refs[:3], features, columns, experts)
    for passed_ref in refs[3:]:
        passed = passed_ref[:rows, :]
        if passed.shape[1] > total.shape[1]:
            passed = passed[:, columns]
        total = total + passed.astype(F32)
        if experts:
            router = router + passed_ref[rows:, :LANES].astype(F32)
    out_ref[:rows, :] = total.astype(BF16)
    if experts:
        rest = jnp.zeros((experts, out_ref.shape[1] - rows), F32)
        out_ref[rows:, :] = jnp.concatenate([router, rest], axis=1).astype(BF16)


def own_kernel(pick_ref, *refs):
    *term_refs, sum_ref, rows_ref = refs
    features = sum_ref.shape[1]
    total, router = plane_sum(pick_ref, term_refs, features, slice(0, features), rows_ref.shape[0])
    sum_ref[...] = total.astype(BF16)
    rows_ref[...] = router


def total_kernel(ids_ref, levels_ref, sum_ref, rows_ref, *refs):
    passed_refs, (grad_ref, router_ref) = refs[:-2], refs[-2:]
    fanout, rows = ids_ref.shape
    experts = rows_ref.shape[0]
    passed = jnp.concatenate([ref[:rows, :] for ref in passed_refs], axis=1)
    grad_ref[...] = (sum_ref[...].astype(F32) + passed.astype(F32)).astype(BF16)
    router = rows_ref[...] + passed_refs[-1][rows:, :LANES].astype(F32)
    expert = lax.broadcasted_iota(jnp.int32, (experts, rows), 0)
    for k in range(fanout):
        own = jnp.where(ids_ref[k : k + 1, :] == expert, router, 0.0)
        own = jnp.sum(own, axis=0, keepdims=True)
        own = own * (256.0 / levels_ref[k : k + 1, :].astype(F32))
        router_ref[k : k + 1, :] = own.astype(BF16)


def stacked(refs, whole_ref):
    start = 0
    for ref in refs:
        whole_ref[start : start + ref.shape[0], :] = ref[...]
        start += ref.shape[0]


def down_kernel(chunks, *refs):
    *d_refs, down_ref, done_ref, d_all, parts, sems = refs
    hidden_refs, d_refs = d_refs[:chunks], d_refs[chunks:]
    done_ref[...] = jnp.zeros_like(done_ref)
    stacked(d_refs, d_all)
    hidden = joined(hidden_refs)
    count, _, step = parts.shape
    copies = []
    for i in range(count):
        cols = slice(step * i, step * (i + 1))
        parts[i] = dot(hidden, d_all[:, cols], ((0,), (0,))).astype(BF16)
        copies.append(pltpu.make_async_copy(parts.at[i], down_ref.at[:, cols], sems.at[i]))
        copies[-1].start()
    for copy in copies:
        copy.wait()


def gate_up_kernel(chunks, *refs):
    *x_refs, gate_ref, up_ref, done_ref, x_all, parts, sems = refs
    grads_refs, x_refs = x_refs[:chunks], x_refs[chunks:]
    done_ref[...] = jnp.zeros_like(done_ref)
    stacked(x_refs, x_all)
    grads = joined(grads_refs)
    count, _, step, units = parts.shape
    copies = []
    for i in range(count):
        cols = slice(step * i, step * (i + 1))
        both = dot(x_all[:, cols], grads, ((0,), (0,))).astype(BF16)
        for j, out_ref in enumerate((gate_ref, up_ref)):
            parts[i, j] = both[:, units * j : units * (j + 1)]
            copy = pltpu.make_async_copy(parts.at[i, j], out_ref.at[cols, :], sems.at[i, j])
            copy.start()
            copies.append(copy)
    for copy in copies:
        copy.wait()


def staged(tokens, cotangent, expert_ids, gate_levels, w_gate, w_up, w_down):
    devices = lax.axis_size("expert")
    planes = devices // PLANE
    tok_rows, fanout = expert_ids.shape
    features = tokens.shape[1]
    units = w_gate.shape[2]
    capacity = 3 * tok_rows * fanout // (2 * devices)
    wide = features + LANES
    rows = PLANE * capacity
    me = lax.axis_index("expert").reshape(1)
    ids, levels = expert_ids.T, gate_levels.T
    gate_mat, up_mat, down_mat = w_gate[0], w_up[0], w_down[0]
    run = Chain()

    ring = [*range(0, planes, 2), *range(1, planes, 2)[::-1]]
    follows = dict(zip(ring, ring[1:] + ring[:1]))

    def along(array):
        pairs = [(i, follows[i // PLANE] * PLANE + i % PLANE) for i in range(devices)]
        return lax.ppermute(array, "expert", pairs)

    def across(array):
        return lax.ppermute(array, "expert", [(i, i ^ 2) for i in range(devices)])

    def cores(array):
        return lax.ppermute(array, "expert", [(i, i ^ 1) for i in range(devices)])

    def swap(blocks, pieces):
        own, near, far, diagonal = blocks
        size = -(-capacity // 16 // pieces) * 16
        passing = [cores(diagonal[i : i + size]) for i in range(0, capacity, size)]
        near = cores(near)
        return own, near, far, passing

    def send(own, near, far, passing, wait=True):
        after = run.pending + ([near] if wait else [])
        run.pending = [] if wait else [near]
        if far.shape[1] > features:
            kernel = functools.partial(stack_kernel, features)
            shape = (2 * capacity * features // LANES + devices, LANES)
        else:
            kernel, shape = join_kernel, (2 * capacity, features)
        (both,) = run(
            kernel,
            [(shape, BF16)],
            "join",
            far,
            *passing,
            after=after,
        )
        return [own, near, across(both)]

    def spread(blocks, pieces=1):
        return send(*swap(blocks, pieces), wait=pieces == 1)

    pick, scaled, rows_x, rows_d, grads, hidden, terms = ({} for _ in range(7))

    def slots_x(s, x, pieces=1):
        pick[s], scaled[s], *blocks = run(
            functools.partial(slot_kernel, capacity),
            [((rows, tok_rows), BF16)] * 2 + [((capacity, features), BF16)] * PLANE,
            "slots_x",
            me,
            x,
            smem=1,
        )
        rows_x[s] = spread(blocks, pieces)

    def slots_d(s, d, after=()):
        blocks = run(
            functools.partial(gather_kernel, capacity),
            [((capacity, features), BF16)] * PLANE,
            "slots_d",
            scaled[s],
            d,
            after=after,
        )
        rows_d[s] = spread(blocks)

    def expert(s, after=()):
        grads[s], hidden[s], *terms[s] = run(
            expert_kernel,
            [((rows, 2 * units), BF16), ((rows, units), BF16)]
            + [((capacity, wide), BF16)] * PLANE,
            "expert",
            me,
            *rows_x[s],
            *rows_d[s],
            gate_mat,
            up_mat,
            down_mat,
            smem=1,
            limit=30,
            after=after,
        )

    def home(s, columns, *passed):
        return along(
            run(
                functools.partial(home_kernel, features, columns),
                [
                    (
                        (
                            tok_rows + (devices if columns.stop == features else 0),
                            columns.stop - columns.start,
                        ),
                        BF16,
                    )
                ],
                "home",
                pick[s],
                *terms[s],
                *passed,
            )[0]
        )

    (packed,) = run(
        pack_kernel,
        [((tok_rows * features // LANES + devices, tok_rows), BF16)],
        "pack",
        ids,
        levels,
        tokens,
        hbm=3,
        scratch=[pltpu.VMEM(ids.shape, jnp.int32)] * 2
        + [pltpu.SemaphoreType.DMA((2 + features // LANES,))],
        limit=60,
    )
    x, d = along(packed), along(cotangent)
    slots_x(0, packed, 2)
    slots_d(0, cotangent)
    last = planes - 1
    for s in range(1, planes):
        (here,) = run.hold(x, after=terms[1][1:] if s == last else rows_x[s - 1][2:])
        if s < last:
            x = along(here)
        slots_x(s, here, 2 if s == last else 1)
        if s == 2:
            expert(1)
            terms[1] = spread(terms[1], 2)
            run.pending = []
        if s == last:
            passed = home(1, slice(0, features))
        (here,) = run.hold(d, after=rows_d[s - 1][2:])
        if s == 1:
            d = along(here)
        if s == 2:
            run.pending += rows_x[s][2:]
        slots_d(s, here)
        if s == 1:
            expert(0)
        if s == 2:
            (here,) = run.hold(here)
            d = along(here)
    expert(2)
    terms[2] = send(*swap(run.hold(*terms[2], after=rows_x[last][2:]), 2), wait=False)
    swapped = swap(run.hold(*terms[0], after=[passed]), 2)
    run.pending = [swapped[1], *swapped[3]]
    expert(last)
    terms[last] = spread(terms[last], 2)
    terms[0] = send(*swapped)
    order = range(planes)
    cuts = [0, 896, 1536, features]
    columns = [slice(start, end) for start, end in zip(cuts, cuts[1:])]
    passed = [home(2, part, passed) for part in columns]
    down_delta, _ = run(
        functools.partial(down_kernel, planes),
        [((units, features), BF16), ((8, LANES), F32)],
        "down_delta",
        *[hidden[s] for s in order],
        *[block for s in order for block in rows_d[s]],
        hbm_out=(0,),
        scratch=[
            pltpu.VMEM((planes * rows, features), BF16),
            pltpu.VMEM((4, units, features // 4), BF16),
            pltpu.SemaphoreType.DMA((4,)),
        ],
    )
    passed = [home(last, part, whole) for whole, part in zip(passed, columns)]
    gate_delta, up_delta, _ = run(
        functools.partial(gate_up_kernel, planes),
        [((features, units), BF16)] * 2 + [((8, LANES), F32)],
        "gate_up_delta",
        *[grads[s] for s in order],
        *[block for s in order for block in rows_x[s]],
        hbm_out=(0, 1),
        scratch=[
            pltpu.VMEM((planes * rows, features), BF16),
            pltpu.VMEM((4, 2, features // 4, units), BF16),
            pltpu.SemaphoreType.DMA((4, 2)),
        ],
    )
    own_sum, own_router = run(
        own_kernel,
        [((tok_rows, features), BF16), ((devices, tok_rows), F32)],
        "own",
        pick[0],
        *terms[0],
    )
    input_grad, router_grad = run(
        total_kernel,
        [((tok_rows, features), BF16), ((fanout, tok_rows), BF16)],
        "total",
        ids,
        levels,
        own_sum,
        own_router,
        *passed,
    )
    return input_grad, router_grad.T, gate_delta[None], up_delta[None], down_delta[None]


def solution(mesh):
    devices = mesh.shape["expert"]
    tokens, experts = P(("groups", "expert"), None), P("expert", None, None)
    deltas = P(("groups", "expert"), None, None)

    def on_device(*arrays):
        tok_rows, fanout = arrays[2].shape
        capacity = 3 * tok_rows * fanout // (2 * devices)
        plan = staged if PLANE * capacity > tok_rows and devices == 4 * PLANE else direct
        return plan(*arrays)

    return jax.shard_map(
        on_device,
        mesh=mesh,
        in_specs=(tokens, tokens, tokens, tokens, experts, experts, experts),
        out_specs=(tokens, tokens, deltas, deltas, deltas),
        check_vma=False,
    )
```

```python
import functools

import jax
import jax.numpy as jnp
from jax import lax
from jax.experimental import pallas as pl
from jax.experimental.pallas import tpu as pltpu
from jax.sharding import PartitionSpec as P

BF16 = jnp.bfloat16
F32 = jnp.float32
LANES = 128
PLANE = 4


def project(inputs, gate_mat, up_mat):
    gate_pre = jnp.dot(inputs, gate_mat, preferred_element_type=jnp.float32)
    up_pre = jnp.dot(inputs, up_mat, preferred_element_type=jnp.float32)
    return (gate_pre, up_pre)


def backward(inputs, prepared, cotangent, gating, gate_mat, up_mat, down_mat):
    gate_pre, up_pre = prepared
    sigmoid_gate = jax.nn.sigmoid(gate_pre)
    hidden = (gate_pre * sigmoid_gate * up_pre).astype(jnp.bfloat16)
    back_grad = lax.dot_general(
        cotangent, down_mat, (((1,), (1,)), ((), ())), preferred_element_type=jnp.float32
    )
    router_term = jnp.sum(hidden.astype(jnp.float32) * back_grad, axis=1).astype(jnp.bfloat16)
    hidden_grad = gating[:, None] * back_grad
    gate_grad = (
        hidden_grad * up_pre * sigmoid_gate * (1.0 + gate_pre * (1.0 - sigmoid_gate))
    ).astype(jnp.bfloat16)
    up_grad = (hidden_grad * gate_pre * sigmoid_gate).astype(jnp.bfloat16)
    input_term = lax.dot_general(
        gate_grad, gate_mat, (((1,), (1,)), ((), ())), preferred_element_type=jnp.float32
    )
    input_term = input_term + lax.dot_general(
        up_grad, up_mat, (((1,), (1,)), ((), ())), preferred_element_type=jnp.float32
    )
    input_term = input_term.astype(jnp.bfloat16)
    scaled = (gating[:, None] * cotangent.astype(jnp.float32)).astype(jnp.bfloat16)
    down_delta = lax.dot_general(
        hidden, scaled, (((0,), (0,)), ((), ())), preferred_element_type=jnp.float32
    )
    gate_delta = lax.dot_general(
        inputs, gate_grad, (((0,), (0,)), ((), ())), preferred_element_type=jnp.float32
    )
    up_delta = lax.dot_general(
        inputs, up_grad, (((0,), (0,)), ((), ())), preferred_element_type=jnp.float32
    )
    return (input_term, router_term, gate_delta, up_delta, down_delta)


def direct(tokens, cotangent, expert_ids, gate_levels, w_gate, w_up, w_down):
    devices = lax.axis_size("expert")
    tok_rows, fanout = expert_ids.shape
    features = tokens.shape[1]
    capacity = 3 * tok_rows * fanout // (2 * devices)
    slot_rows = devices * capacity
    gate_mat = w_gate[0]
    up_mat = w_up[0]
    down_mat = w_down[0]
    chosen = expert_ids.reshape(-1)
    indicator = (chosen[:, None] == jnp.arange(devices, dtype=jnp.int32)[None, :]).astype(jnp.int32)
    earlier = jnp.cumsum(indicator, axis=0) - indicator
    position = jnp.sum(earlier * indicator, axis=1)
    target = chosen * capacity + position
    gating_local = (gate_levels.reshape(-1).astype(jnp.float32) / 256.0).astype(jnp.bfloat16)
    outbox_x = (
        jnp.zeros((slot_rows, features), jnp.bfloat16)
        .at[target]
        .set(jnp.repeat(tokens, fanout, axis=0))
    )
    outbox_dy = (
        jnp.zeros((slot_rows, features), jnp.bfloat16)
        .at[target]
        .set(jnp.repeat(cotangent, fanout, axis=0))
    )
    outbox_g = jnp.zeros((slot_rows,), jnp.bfloat16).at[target].set(gating_local)
    outbox_x = outbox_x.reshape(devices, capacity, features)
    outbox_dy = outbox_dy.reshape(devices, capacity, features)
    outbox_g = outbox_g.reshape(devices, capacity)
    exchange = functools.partial(
        lax.all_to_all, axis_name="expert", split_axis=0, concat_axis=0, tiled=True
    )
    rows_x = exchange(outbox_x).reshape(slot_rows, features)
    rows_dy = exchange(outbox_dy).reshape(slot_rows, features)
    rows_g = exchange(outbox_g).reshape(-1).astype(jnp.float32)
    prepared = project(rows_x, gate_mat, up_mat)
    input_term, router_term, gate_delta, up_delta, down_delta = backward(
        rows_x, prepared, rows_dy, rows_g, gate_mat, up_mat, down_mat
    )
    back_term = exchange(input_term.reshape(devices, capacity, features))
    back_router = exchange(router_term.reshape(devices, capacity))
    gathered_term = back_term.reshape(slot_rows, features)[target].astype(jnp.float32)
    input_grad = jnp.sum(gathered_term.reshape(tok_rows, fanout, features), axis=1).astype(
        jnp.bfloat16
    )
    router_grad = back_router.reshape(-1)[target].reshape(tok_rows, fanout)
    return (
        input_grad,
        router_grad,
        gate_delta.astype(jnp.bfloat16)[None],
        up_delta.astype(jnp.bfloat16)[None],
        down_delta.astype(jnp.bfloat16)[None],
    )


def dot(a, b, contract=((1,), (0,))):
    return lax.dot_general(a, b, (contract, ((), ())), preferred_element_type=F32)


class Chain:
    def __init__(self):
        self.last = []
        self.pending = []

    def __call__(self, kernel, outs, name, *operands, after=(), scratch=(), smem=0, hbm=0, hbm_out=(), limit=16):
        vmem = pl.BlockSpec(memory_space=pltpu.VMEM)
        scalar = pl.BlockSpec(memory_space=pltpu.SMEM)
        anywhere = pl.BlockSpec(memory_space=pl.ANY)
        outside = pl.BlockSpec(memory_space=pltpu.HBM)
        unused = [*self.last, *after]
        fixed = len(operands)

        def body(*refs):
            kernel(*refs[:fixed], *refs[fixed + len(unused) :])

        made = pl.pallas_call(
            body,
            out_shape=[jax.ShapeDtypeStruct(shape, kind) for shape, kind in outs],
            in_specs=[scalar] * smem
            + [outside] * hbm
            + [vmem] * (fixed - smem - hbm)
            + [anywhere] * len(unused),
            out_specs=[outside if i in hbm_out else vmem for i in range(len(outs))],
            scratch_shapes=list(scratch),
            name=name,
            compiler_params=pltpu.CompilerParams(vmem_limit_bytes=limit << 20),
            cost_estimate=pl.CostEstimate(flops=1000, bytes_accessed=1000, transcendentals=0),
        )(*operands, *unused)
        self.last = [min(made, key=lambda array: array.size)]
        return made

    def hold(self, *arrays, after=()):
        unused = [*self.last, *self.pending, *after]
        self.pending = []
        anywhere = pl.BlockSpec(memory_space=pl.ANY)
        held = pl.pallas_call(
            lambda *refs: None,
            out_shape=[jax.ShapeDtypeStruct(array.shape, array.dtype) for array in arrays],
            in_specs=[anywhere] * (len(arrays) + len(unused)),
            out_specs=[anywhere] * len(arrays),
            input_output_aliases={i: i for i in range(len(arrays))},
            name="hold",
            compiler_params=pltpu.CompilerParams(vmem_limit_bytes=1 << 20),
            cost_estimate=pl.CostEstimate(flops=1000, bytes_accessed=1000, transcendentals=0),
        )(*arrays, *unused)
        self.last = held[:1]
        return held


def joined(refs):
    return jnp.concatenate([ref[...] for ref in refs], axis=0)


def unstacked(ref, rows, start, stop):
    blocks = range(start // LANES, stop // LANES)
    return jnp.concatenate([ref[rows * i : rows * (i + 1), :] for i in blocks], axis=1)


def pack_kernel(ids_ref, levels_ref, x_ref, out_ref, ids_here, levels_here, sems):
    fanout, rows = ids_ref.shape
    features = x_ref.shape[1]
    experts = out_ref.shape[0] - rows * features // LANES
    moves = [(ids_ref, ids_here), (levels_ref, levels_here)]
    for i in range(features // LANES):
        source = x_ref.at[:, LANES * i : LANES * (i + 1)]
        moves.append((source, out_ref.at[rows * i : rows * (i + 1), :]))
    copies = [
        pltpu.make_async_copy(source, target, sems.at[i])
        for i, (source, target) in enumerate(moves)
    ]
    for copy in copies:
        copy.start()
    for copy in copies[:2]:
        copy.wait()
    expert = lax.broadcasted_iota(jnp.int32, (experts, rows), 0)
    gates = jnp.zeros((experts, rows), F32)
    for k in range(fanout):
        value = levels_here[k : k + 1, :].astype(F32) * (1.0 / 256.0)
        gates = gates + jnp.where(ids_here[k : k + 1, :] == expert, value, 0.0)
    out_ref[out_ref.shape[0] - experts :, :] = gates.astype(BF16)
    for copy in copies[2:]:
        copy.wait()


def slot_kernel(capacity, me_ref, x_ref, pick_ref, scaled_ref, *block_refs):
    features = block_refs[0].shape[1]
    rows = pick_ref.shape[1]
    table = x_ref[rows * features // LANES :, :]
    experts = table.shape[0]
    expert = lax.broadcasted_iota(jnp.int32, (8, experts), 1)
    wanted = jnp.bitwise_xor(lax.broadcasted_iota(jnp.int32, (8, experts), 0), me_ref[0])
    chooser = jnp.where(expert == wanted, 1.0, 0.0).astype(BF16)
    gates = dot(chooser, table)
    routed = jnp.where(gates > 0.0, 1.0, 0.0)
    before = lax.broadcasted_iota(jnp.int32, (rows, rows), 0)
    after = lax.broadcasted_iota(jnp.int32, (rows, rows), 1)
    earlier = jnp.where(before < after, 1.0, 0.0).astype(BF16)
    place = dot(routed.astype(BF16), earlier)
    place = jnp.where(routed > 0.0, place, -1.0)
    slot = lax.broadcasted_iota(jnp.int32, (capacity, rows), 0).astype(F32)
    chosen = [place[i : i + 1, :] == slot for i in range(PLANE)]
    pick = jnp.concatenate([jnp.where(here, 1.0, 0.0) for here in chosen], axis=0).astype(BF16)
    pick_ref[...] = pick
    scaled_ref[...] = jnp.concatenate(
        [jnp.where(here, gates[i : i + 1, :], 0.0) for i, here in enumerate(chosen)], axis=0
    ).astype(BF16)
    picked = dot(pick, unstacked(x_ref, rows, 0, features)).astype(BF16)
    for i, block_ref in enumerate(block_refs):
        block_ref[...] = picked[capacity * i : capacity * (i + 1), :]


def gather_kernel(capacity, scaled_ref, d_ref, *block_refs):
    picked = dot(scaled_ref[...], d_ref[...]).astype(BF16)
    for i, block_ref in enumerate(block_refs):
        block_ref[...] = picked[capacity * i : capacity * (i + 1), :]


def join_kernel(*refs):
    refs[-1][...] = joined(refs[:-1])


def stack_kernel(features, *refs):
    *block_refs, out_ref = refs
    rows = sum(ref.shape[0] for ref in block_refs)
    for i in range(features // LANES):
        blocks = [ref[:, LANES * i : LANES * (i + 1)] for ref in block_refs]
        out_ref[rows * i : rows * (i + 1), :] = jnp.concatenate(blocks, axis=0)
    lanes = jnp.concatenate([ref[:, features:] for ref in block_refs], axis=0).astype(F32)
    blank = jnp.zeros((LANES - rows, LANES), F32)
    experts = out_ref.shape[0] - rows * features // LANES
    router = jnp.concatenate([lanes, blank], axis=0).T[:experts, :]
    out_ref[rows * features // LANES :, :] = router.astype(BF16)


def expert_kernel(me_ref, *refs):
    x_refs, d_refs, (gate_ref, up_ref, down_ref) = refs[:3], refs[3:6], refs[6:9]
    grads_ref, hidden_ref, *term_refs = refs[9:]
    features, units = gate_ref.shape
    x, d = joined(x_refs), joined(d_refs)
    rows = x.shape[0]
    gate_pre = dot(x, gate_ref[...])
    up_pre = dot(x, up_ref[...])
    hidden_grad = dot(d, down_ref[...], ((1,), (1,)))
    sigmoid_gate = jax.nn.sigmoid(gate_pre)
    silu = gate_pre * sigmoid_gate
    hidden = (silu * up_pre).astype(BF16)
    router = jnp.sum(hidden.astype(F32) * hidden_grad, axis=1, keepdims=True)
    gate_grad = hidden_grad * up_pre * sigmoid_gate * (1.0 + gate_pre * (1.0 - sigmoid_gate))
    gate_grad = gate_grad.astype(BF16)
    up_grad = (hidden_grad * silu).astype(BF16)
    grads_ref[:, :units] = gate_grad
    grads_ref[:, units:] = up_grad
    hidden_ref[...] = hidden
    term = dot(gate_grad, gate_ref[...], ((1,), (1,))) + dot(up_grad, up_ref[...], ((1,), (1,)))
    term = term.astype(BF16)
    mine = lax.broadcasted_iota(jnp.int32, (rows, LANES), 1) == me_ref[0]
    router = jnp.where(mine, router, 0.0).astype(BF16)
    count = rows // len(term_refs)
    for i, term_ref in enumerate(term_refs):
        part = slice(count * i, count * (i + 1))
        term_ref[:, :features] = term[part, :]
        term_ref[:, features:] = router[part, :]


def plane_sum(pick_ref, term_refs, features, columns, experts):
    own_ref, near_ref, far_ref = term_refs
    half = pick_ref.shape[0] // 2
    terms = jnp.concatenate(
        [
            own_ref[:, columns],
            near_ref[:, columns],
            unstacked(far_ref, half, columns.start, columns.stop),
        ],
        axis=0,
    )
    total = dot(pick_ref[...], terms, ((0,), (0,)))
    if not experts:
        return total, None
    lanes = jnp.concatenate([own_ref[:, features:], near_ref[:, features:]], axis=0)
    router = dot(lanes, pick_ref[:half, :], ((0,), (0,)))[:experts, :]
    router = router + dot(far_ref[half * features // LANES :, :half], pick_ref[half:, :])
    return total, router


def home_kernel(features, columns, pick_ref, *refs):
    *refs, out_ref = refs
    rows = pick_ref.shape[1]
    experts = out_ref.shape[0] - rows
    total, router = plane_sum(pick_ref, refs[:3], features, columns, experts)
    for passed_ref in refs[3:]:
        passed = passed_ref[:rows, :]
        if passed.shape[1] > total.shape[1]:
            passed = passed[:, columns]
        total = total + passed.astype(F32)
        if experts:
            router = router + passed_ref[rows:, :LANES].astype(F32)
    out_ref[:rows, :] = total.astype(BF16)
    if experts:
        rest = jnp.zeros((experts, out_ref.shape[1] - rows), F32)
        out_ref[rows:, :] = jnp.concatenate([router, rest], axis=1).astype(BF16)


def own_kernel(pick_ref, *refs):
    *term_refs, sum_ref, rows_ref = refs
    features = sum_ref.shape[1]
    total, router = plane_sum(pick_ref, term_refs, features, slice(0, features), rows_ref.shape[0])
    sum_ref[...] = total.astype(BF16)
    rows_ref[...] = router


def total_kernel(ids_ref, levels_ref, sum_ref, rows_ref, *refs):
    passed_refs, (grad_ref, router_ref) = refs[:-2], refs[-2:]
    fanout, rows = ids_ref.shape
    experts = rows_ref.shape[0]
    passed = jnp.concatenate([ref[:rows, :] for ref in passed_refs], axis=1)
    grad_ref[...] = (sum_ref[...].astype(F32) + passed.astype(F32)).astype(BF16)
    router = rows_ref[...] + passed_refs[-1][rows:, :LANES].astype(F32)
    expert = lax.broadcasted_iota(jnp.int32, (experts, rows), 0)
    for k in range(fanout):
        own = jnp.where(ids_ref[k : k + 1, :] == expert, router, 0.0)
        own = jnp.sum(own, axis=0, keepdims=True)
        own = own * (256.0 / levels_ref[k : k + 1, :].astype(F32))
        router_ref[k : k + 1, :] = own.astype(BF16)


def stacked(refs, whole_ref):
    start = 0
    for ref in refs:
        whole_ref[start : start + ref.shape[0], :] = ref[...]
        start += ref.shape[0]


def down_kernel(chunks, *refs):
    *d_refs, down_ref, done_ref, d_all, parts, sems = refs
    hidden_refs, d_refs = d_refs[:chunks], d_refs[chunks:]
    done_ref[...] = jnp.zeros_like(done_ref)
    stacked(d_refs, d_all)
    hidden = joined(hidden_refs)
    count, _, step = parts.shape
    copies = []
    for i in range(count):
        cols = slice(step * i, step * (i + 1))
        parts[i] = dot(hidden, d_all[:, cols], ((0,), (0,))).astype(BF16)
        copies.append(pltpu.make_async_copy(parts.at[i], down_ref.at[:, cols], sems.at[i]))
        copies[-1].start()
    for copy in copies:
        copy.wait()


def gate_up_kernel(chunks, *refs):
    *x_refs, gate_ref, up_ref, done_ref, x_all, parts, sems = refs
    grads_refs, x_refs = x_refs[:chunks], x_refs[chunks:]
    done_ref[...] = jnp.zeros_like(done_ref)
    stacked(x_refs, x_all)
    grads = joined(grads_refs)
    count, _, step, units = parts.shape
    copies = []
    for i in range(count):
        cols = slice(step * i, step * (i + 1))
        both = dot(x_all[:, cols], grads, ((0,), (0,))).astype(BF16)
        for j, out_ref in enumerate((gate_ref, up_ref)):
            parts[i, j] = both[:, units * j : units * (j + 1)]
            copy = pltpu.make_async_copy(parts.at[i, j], out_ref.at[cols, :], sems.at[i, j])
            copy.start()
            copies.append(copy)
    for copy in copies:
        copy.wait()


def staged(tokens, cotangent, expert_ids, gate_levels, w_gate, w_up, w_down):
    devices = lax.axis_size("expert")
    planes = devices // PLANE
    tok_rows, fanout = expert_ids.shape
    features = tokens.shape[1]
    units = w_gate.shape[2]
    capacity = 3 * tok_rows * fanout // (2 * devices)
    wide = features + LANES
    rows = PLANE * capacity
    me = lax.axis_index("expert").reshape(1)
    ids, levels = expert_ids.T, gate_levels.T
    gate_mat, up_mat, down_mat = w_gate[0], w_up[0], w_down[0]
    run = Chain()

    ring = [*range(0, planes, 2), *range(1, planes, 2)[::-1]]
    follows = dict(zip(ring, ring[1:] + ring[:1]))

    def along(array):
        pairs = [(i, follows[i // PLANE] * PLANE + i % PLANE) for i in range(devices)]
        return lax.ppermute(array, "expert", pairs)

    def across(array):
        return lax.ppermute(array, "expert", [(i, i ^ 2) for i in range(devices)])

    def cores(array):
        return lax.ppermute(array, "expert", [(i, i ^ 1) for i in range(devices)])

    def swap(blocks, pieces):
        own, near, far, diagonal = blocks
        size = -(-capacity // 16 // pieces) * 16
        passing = [cores(diagonal[i : i + size]) for i in range(0, capacity, size)]
        near = cores(near)
        return own, near, far, passing

    def send(own, near, far, passing, wait=True):
        after = run.pending + ([near] if wait else [])
        run.pending = [] if wait else [near]
        if far.shape[1] > features:
            kernel = functools.partial(stack_kernel, features)
            shape = (2 * capacity * features // LANES + devices, LANES)
        else:
            kernel, shape = join_kernel, (2 * capacity, features)
        (both,) = run(
            kernel,
            [(shape, BF16)],
            "join",
            far,
            *passing,
            after=after,
        )
        return [own, near, across(both)]

    def spread(blocks, pieces=1):
        return send(*swap(blocks, pieces), wait=pieces == 1)

    pick, scaled, rows_x, rows_d, grads, hidden, terms = ({} for _ in range(7))

    def slots_x(s, x, pieces=1):
        pick[s], scaled[s], *blocks = run(
            functools.partial(slot_kernel, capacity),
            [((rows, tok_rows), BF16)] * 2 + [((capacity, features), BF16)] * PLANE,
            "slots_x",
            me,
            x,
            smem=1,
        )
        rows_x[s] = spread(blocks, pieces)

    def slots_d(s, d, pieces=1):
        blocks = run(
            functools.partial(gather_kernel, capacity),
            [((capacity, features), BF16)] * PLANE,
            "slots_d",
            scaled[s],
            d,
        )
        rows_d[s] = spread(blocks, pieces)

    def expert(s, after=()):
        grads[s], hidden[s], *terms[s] = run(
            expert_kernel,
            [((rows, 2 * units), BF16), ((rows, units), BF16)]
            + [((capacity, wide), BF16)] * PLANE,
            "expert",
            me,
            *rows_x[s],
            *rows_d[s],
            gate_mat,
            up_mat,
            down_mat,
            smem=1,
            limit=30,
            after=after,
        )

    def home(s, columns, *passed):
        return along(
            run(
                functools.partial(home_kernel, features, columns),
                [
                    (
                        (
                            tok_rows + (devices if columns.stop == features else 0),
                            columns.stop - columns.start,
                        ),
                        BF16,
                    )
                ],
                "home",
                pick[s],
                *terms[s],
                *passed,
            )[0]
        )

    (packed,) = run(
        pack_kernel,
        [((tok_rows * features // LANES + devices, tok_rows), BF16)],
        "pack",
        ids,
        levels,
        tokens,
        hbm=3,
        scratch=[pltpu.VMEM(ids.shape, jnp.int32)] * 2
        + [pltpu.SemaphoreType.DMA((2 + features // LANES,))],
        limit=60,
    )
    x, d = along(packed), along(cotangent)
    slots_x(0, packed, 2)
    slots_d(0, cotangent)
    last = planes - 1
    for s in range(1, planes):
        (here,) = run.hold(x, after=terms[1][2:] if s == last else rows_x[s - 1][2:])
        if s < last:
            x = along(here)
        slots_x(s, here, 2 if s == last else 1)
        if s == 2:
            expert(1)
            terms[1] = spread(terms[1], 2)
            run.pending = []
        if s == last:
            passed = home(1, slice(0, features))
        (here,) = run.hold(d, after=rows_d[s - 1][2:])
        if s == 1:
            d = along(here)
        if s == 2:
            run.pending += rows_x[s][2:]
        slots_d(s, here, 2 if s == 2 else 1)
        if s == 1:
            expert(0)
        if s == 2:
            run.pending = []
            (here,) = run.hold(here)
            d = along(here)
    expert(2)
    terms[2] = send(*swap(run.hold(*terms[2], after=rows_x[last][2:]), 2), wait=False)
    swapped = swap(run.hold(*terms[0], after=[passed]), 2)
    run.pending = [swapped[1], *swapped[3]]
    expert(last)
    terms[last] = spread(terms[last], 2)
    terms[0] = send(*swapped)
    order = range(planes)
    cuts = [0, 896, 1536, features]
    columns = [slice(start, end) for start, end in zip(cuts, cuts[1:])]
    passed = [home(2, part, passed) for part in columns]
    down_delta, _ = run(
        functools.partial(down_kernel, planes),
        [((units, features), BF16), ((8, LANES), F32)],
        "down_delta",
        *[hidden[s] for s in order],
        *[block for s in order for block in rows_d[s]],
        hbm_out=(0,),
        scratch=[
            pltpu.VMEM((planes * rows, features), BF16),
            pltpu.VMEM((4, units, features // 4), BF16),
            pltpu.SemaphoreType.DMA((4,)),
        ],
    )
    passed = [home(last, part, whole) for whole, part in zip(passed, columns)]
    gate_delta, up_delta, _ = run(
        functools.partial(gate_up_kernel, planes),
        [((features, units), BF16)] * 2 + [((8, LANES), F32)],
        "gate_up_delta",
        *[grads[s] for s in order],
        *[block for s in order for block in rows_x[s]],
        hbm_out=(0, 1),
        scratch=[
            pltpu.VMEM((planes * rows, features), BF16),
            pltpu.VMEM((4, 2, features // 4, units), BF16),
            pltpu.SemaphoreType.DMA((4, 2)),
        ],
    )
    own_sum, own_router = run(
        own_kernel,
        [((tok_rows, features), BF16), ((devices, tok_rows), F32)],
        "own",
        pick[0],
        *terms[0],
    )
    input_grad, router_grad = run(
        total_kernel,
        [((tok_rows, features), BF16), ((fanout, tok_rows), BF16)],
        "total",
        ids,
        levels,
        own_sum,
        own_router,
        *passed,
    )
    return input_grad, router_grad.T, gate_delta[None], up_delta[None], down_delta[None]


def solution(mesh):
    devices = mesh.shape["expert"]
    tokens, experts = P(("groups", "expert"), None), P("expert", None, None)
    deltas = P(("groups", "expert"), None, None)

    def on_device(*arrays):
        tok_rows, fanout = arrays[2].shape
        capacity = 3 * tok_rows * fanout // (2 * devices)
        plan = staged if PLANE * capacity > tok_rows and devices == 4 * PLANE else direct
        return plan(*arrays)

    return jax.shard_map(
        on_device,
        mesh=mesh,
        in_specs=(tokens, tokens, tokens, tokens, experts, experts, experts),
        out_specs=(tokens, tokens, deltas, deltas, deltas),
        check_vma=False,
    )
```
